128 devices in a mesh: mx: 8 (over x, core), my: 16 (over y, z).
Axes of the slice: x: 4, y: 4, z: 4, core: 2. Of those that a mesh axis runs over, the one named last changes fastest.
Arguments:
- lanczos_block: float32 [16, 64, 2048], P(None, 'mx', 'my'), may hold values from -6 to 6
- previous_block: float32 [16, 64, 2048], P(None, 'mx', 'my'), may hold values from -6 to 6
- previous_beta: float32 [16, 16], replicated, may hold values from -2 to 2
- prior_reaction: float32 [64, 2048], P('mx', 'my'), may hold values from 0.02 to 0.5
- vert_coupling: float32 [15, 64, 2048], P(None, 'mx', 'my'), may hold values from 2 to 20
- horiz_coupling: float32 [16, 64, 2048], P(None, 'mx', 'my'), may hold values from 0.05 to 0.25
- friction: float32 [64, 2048], P('mx', 'my'), may hold values from 0.5 to 2
- base_velocity: float32 [2, 64, 2048], P(None, 'mx', 'my'), may hold values from -4 to 4
- layers: int32 [64, 2048], P('mx', 'my'), may hold values from 1 to 16
- obs_dest: int32 [32768, 1], P(('mx', 'my')), may hold values from 0 to 127; in each aligned block of 256 rows (0 to 255, 256 to 511, ...) at most 4 rows name the same one
- obs_cell: int32 [32768], P(('mx', 'my')), may hold values from 0 to 1023
- obs_weight: float32 [32768, 2], P(('mx', 'my')), may hold values from 40 to 400
Outputs:
- next_block: float32 [16, 64, 2048], P(None, 'mx', 'my')
- block_alpha: float32 [16, 16], replicated
- block_beta: float32 [16, 16], replicated
The draws below stay inside these ranges and needn't reach their ends.
Inputs may be any that keep to these rules, and one draw needn't show every extreme that they name: `obs_dest`: within the rows of one device, no device index appears more than 4 times, and some index appears exactly 4 times.
All inputs are finite; a program needn't handle non-finite values.
Results may differ from the reference program's by a relative error of at most 0.0002.
Values sent between devices are 32-bit elements; how exact they have to be, the bound alone decides.
No kernel may reach another device: no remote copies, remote signals or barrier semaphores. Data moves between devices by JAX's collectives and lax.ppermute only.
A program may use at most 64 MiB of HBM per device.

```python
import math
import jax
import jax.numpy as jnp
import numpy as np
from jax import lax

B = 16
NZ = 16
SWEEPS = 3
PRIOR_ITERS = 3
CX = 8
CY = 128
OBS_DEV = 256
NX = 64
NY = 2048
OBS_TOTAL = 32768
CAP = 4
N_MX = 8
N_MY = 16


def touch_ends(array, key, least, largest):
    longest = array.shape.index(max(array.shape))
    spots = []
    for shift in (0, 1):
        where = [jax.random.randint(jax.random.fold_in(key, axis), (), 0, length) for axis, length in enumerate(array.shape)]
        where[longest] = (where[longest] + shift) % array.shape[longest]
        spots.append(tuple(where))
    return array.at[spots[0]].set(least).at[spots[1]].set(largest)


def block_scale(key, dims, pieces, smallest, largest):
    gain, own = 1.0, jax.random.fold_in(key, 6)
    for dim, blocks in pieces:
        heights = jnp.exp(jax.random.uniform(jax.random.fold_in(own, dim), (blocks,), jnp.float32, smallest / len(pieces), largest / len(pieces)))
        gain = gain * jnp.repeat(heights, dims[dim] // blocks).reshape([-1 if axis == dim else 1 for axis in range(len(dims))])
    return gain


def shared_out(rng, own, number, rows, amount, top, most, lean):
    ranking = jax.random.permutation(rng, amount)
    packed, usual = load_shares(amount, rows * top, most, lean, True), load_shares(amount, rows * top, most, lean, False)
    places = jnp.arange(amount)

    def named(tallies, rotation):
        used = int((tallies > 0).sum())
        fixed = max(1, used // 4)
        shifted = fixed + (places - fixed + rotation * (used - fixed)) % max(1, amount - fixed)
        return jnp.zeros((amount,), jnp.int32).at[ranking[jnp.where(places < fixed, places, shifted)]].set(jnp.asarray(tallies, jnp.int32))

    tallies = jnp.where(number % 4 == 0, named(packed, number // 4), named(usual, number - number // 4 - 1))
    mixed = jax.random.permutation(jax.random.fold_in(own, 3), amount)
    giver, sink = mixed[0:amount // 2 * 2:2], mixed[1:amount // 2 * 2:2]
    room = jnp.minimum(tallies[giver] - 1, most - tallies[sink]) // 2
    room = jnp.where((giver == ranking[0]) | (sink == ranking[0]) | (tallies[sink] == 0), 0, jnp.maximum(room, 0))
    shifted = jax.random.randint(jax.random.fold_in(own, 4), (amount // 2,), 0, 1 << 20) % (room + 1)
    tallies = tallies.at[giver].add(-shifted).at[sink].add(shifted)
    members = jnp.searchsorted(jnp.cumsum(tallies), jnp.arange(rows * top), side="right").astype(jnp.int32)
    grid = members.reshape(top, rows).T
    grid = grid[jax.random.permutation(jax.random.fold_in(own, 1), rows)]
    rotation = jax.random.randint(jax.random.fold_in(own, 2), (rows, 1), 0, top)
    return jnp.take_along_axis(grid, (jnp.arange(top)[None, :] + rotation) % top, axis=1)


def load_shares(count, total, limit, skew, full):
    portions = [(1 << 20) // math.isqrt(standing ** skew) + 1 for standing in range(1, count + 1)]
    largest = limit if full else min(limit, max(-(-total // count), total * portions[0] // sum(portions)))
    least = 1 if total - largest >= count - 1 else 0
    given, rest = [largest] + [least] * (count - 1), total - largest - least * (count - 1)
    while rest > 0:
        free = [i for i in range(1, count) if given[i] < largest] or [i for i in range(1, count) if given[i] < limit]
        mass, remaining = sum([portions[i] for i in free]), rest
        for i in free:
            extra = min(limit - given[i], max(1, remaining * portions[i] // mass), rest)
            given[i] = given[i] + extra
            rest = rest - extra
    return np.array(given)


def scatter_about(stream_key, shape, spread, limit, split=(), kind=jnp.bfloat16):
    drawn = jax.random.normal(stream_key, shape, jnp.float32) * spread
    if len(split) > 0:
        drawn = block_scale(stream_key, shape, split, -0.22, 0.18) * drawn
    return jnp.clip(drawn, min=-limit, max=limit).astype(kind)


def setup_inputs(seed: int = 0) -> dict:
    keys = jax.random.split(jax.random.key(seed), 13)
    lanczos_block = scatter_about(keys[0], (B, NX, NY), 1.0, 6.0, ((1, 8), (2, 16)), jnp.float32)
    previous_block = scatter_about(keys[1], (B, NX, NY), 1.0, 6.0, ((1, 8), (2, 16)), jnp.float32)
    previous_beta = scatter_about(keys[2], (B, B), 0.3, 2.0, (), jnp.float32)
    prior_reaction = jnp.clip(jnp.exp(math.log(0.5) - 3.218876 * jax.random.uniform(keys[3], (NX, NY), jnp.float32) ** block_scale(keys[3], (NX, NY), ((0, 8), (1, 16)), -0.2, 0.2)), 0.02, 0.5)
    vert_coupling = jnp.clip(jnp.exp(math.log(20.0) - 2.3025851 * jax.random.uniform(keys[4], (NZ - 1, NX, NY), jnp.float32) ** block_scale(keys[4], (NZ - 1, NX, NY), ((1, 8), (2, 16)), -0.2, 0.2)), 2.0, 20.0)
    horiz_coupling = jnp.clip(jnp.exp(math.log(0.25) - 1.609438 * jax.random.uniform(keys[5], (NZ, NX, NY), jnp.float32) ** block_scale(keys[5], (NZ, NX, NY), ((1, 8), (2, 16)), -0.2, 0.2)), 0.05, 0.25)
    friction = jnp.clip(jnp.exp(math.log(2.0) - 1.3862944 * jax.random.uniform(keys[6], (NX, NY), jnp.float32) ** block_scale(keys[6], (NX, NY), ((0, 8), (1, 16)), -0.2, 0.2)), 0.5, 2.0)
    base_velocity = scatter_about(keys[7], (2, NX, NY), 1.0, 4.0, ((1, 8), (2, 16)), jnp.float32)
    layers = touch_ends(jax.random.randint(keys[8], (NX, NY), 1, NZ + 1), jax.random.fold_in(keys[8], 1), 1, NZ).astype(jnp.int32)
    obs_dest_keys = jax.random.split(jax.random.fold_in(keys[9], 1), OBS_TOTAL // OBS_DEV)
    obs_dest_turns = jax.random.permutation(jax.random.fold_in(keys[9], 3), OBS_TOTAL // OBS_DEV)
    obs_dest = jax.vmap(lambda own, number: shared_out(jax.random.fold_in(keys[9], 2), own, number, OBS_DEV, N_MX * N_MY, 1, CAP, 2))(obs_dest_keys, obs_dest_turns).reshape((OBS_TOTAL, 1))
    obs_cell = touch_ends(jax.random.randint(keys[10], (OBS_TOTAL,), 0, CX * CY), jax.random.fold_in(keys[10], 1), 0, (CX * CY) - 1).astype(jnp.int32)
    obs_weight = jnp.clip(jnp.exp(math.log(400.0) - 2.3025851 * jax.random.uniform(keys[11], (OBS_TOTAL, 2), jnp.float32) ** block_scale(keys[11], (OBS_TOTAL, 2), ((0, 128),), -0.2, 0.2)), 40.0, 400.0)
    return {"lanczos_block": lanczos_block, "previous_block": previous_block, "previous_beta": previous_beta, "prior_reaction": prior_reaction, "vert_coupling": vert_coupling, "horiz_coupling": horiz_coupling, "friction": friction, "base_velocity": base_velocity, "layers": layers, "obs_dest": obs_dest, "obs_cell": obs_cell, "obs_weight": obs_weight}


base_damping = 0.02
highest = lax.Precision.HIGHEST

def neighbour_sum(padded):
    return padded[..., 2:, 1:-1] + padded[..., :-2, 1:-1] + padded[..., 1:-1, 2:] + padded[..., 1:-1, :-2]

def local_neighbours(grid_field):
    widths = [(0, 0)] * (grid_field.ndim - 2) + [(1, 1), (1, 1)]
    return neighbour_sum(jnp.pad(grid_field, widths))

def top_layer(active):
    return active - jnp.concatenate([active[1:], jnp.zeros_like(active[:1])], axis=0)

def column_factors(vert_coupling, horiz_coupling, friction, active):
    coupling_up = vert_coupling * active[1:]
    lateral = horiz_coupling * active
    zero_row = jnp.zeros_like(coupling_up[:1])
    from_below = jnp.concatenate([zero_row, coupling_up], axis=0)
    from_above = jnp.concatenate([coupling_up, zero_row], axis=0)
    bed_drag = jnp.concatenate([friction[None], jnp.zeros_like(lateral[1:])], axis=0)
    diagonal = (base_damping + lateral + from_below + from_above + bed_drag) * active + (1.0 - active)
    pivot_list = [diagonal[0]]
    for layer_idx in range(1, diagonal.shape[0]):
        pivot_list.append(diagonal[layer_idx] - coupling_up[layer_idx - 1] * coupling_up[layer_idx - 1] / pivot_list[layer_idx - 1])
    pivots = jnp.stack(pivot_list, axis=0)
    ratios = coupling_up / pivots[:-1]
    return (coupling_up, lateral, ratios, pivots)

def column_solve(source, coupling_up, ratios, pivots):
    layer_count = pivots.shape[0]
    carried = [source[..., 0, :, :]]
    for layer_idx in range(1, layer_count):
        carried.append(source[..., layer_idx, :, :] + ratios[layer_idx - 1] * carried[layer_idx - 1])
    solved = [carried[layer_count - 1] / pivots[layer_count - 1]]
    for layer_idx in range(layer_count - 2, -1, -1):
        solved.append((carried[layer_idx] + coupling_up[layer_idx] * solved[-1]) / pivots[layer_idx])
    return jnp.stack(solved[::-1], axis=-3)

def column_map(source, factors, neighbours):
    coupling_up, lateral, ratios, pivots = factors
    iterate = column_solve(source, coupling_up, ratios, pivots)
    for sweep_idx in range(SWEEPS):
        iterate = column_solve(source + lateral * neighbours(lateral * iterate), coupling_up, ratios, pivots)
    return iterate

def prior_solve(right_side, reaction):
    solution = jnp.zeros_like(right_side)
    residual = right_side
    search = right_side
    norm_now = jnp.sum(residual * residual, axis=(1, 2))
    for iter_idx in range(PRIOR_ITERS):
        applied_dir = (reaction + 4.0) * search - local_neighbours(search)
        step_size = norm_now / jnp.sum(search * applied_dir, axis=(1, 2))
        solution = solution + step_size[:, None, None] * search
        residual = residual - step_size[:, None, None] * applied_dir
        if iter_idx + 1 < PRIOR_ITERS:
            norm_next = jnp.sum(residual * residual, axis=(1, 2))
            search = residual + (norm_next / norm_now)[:, None, None] * search
            norm_now = norm_next
    return solution

def reference(lanczos_block, previous_block, previous_beta, prior_reaction, vert_coupling, horiz_coupling, friction, base_velocity, layers, obs_dest, obs_cell, obs_weight):
    layer_ids = jnp.arange(NZ, dtype=jnp.int32)[:, None, None]
    active = (layer_ids < layers[None]).astype(jnp.float32)
    surface_mask = top_layer(active)
    factors = column_factors(vert_coupling, horiz_coupling, friction, active)
    smoothed = prior_solve(lanczos_block, prior_reaction)
    tile_row = obs_dest[:, 0] // N_MY
    tile_col = obs_dest[:, 0] % N_MY
    grid_row = tile_row * CX + obs_cell // CY
    grid_col = tile_col * CY + obs_cell % CY
    flat_index = (grid_row * NY + grid_col).astype(jnp.int32)
    column_weight = jnp.zeros((2, NX * NY), jnp.float32).at[:, flat_index].add(jnp.transpose(obs_weight)).reshape(2, NX, NY)
    bed_factor = friction * base_velocity
    bed_onehot = (layer_ids == 0).astype(jnp.float32)

    def hessian_column(smoothed_one):
        bed_source = (bed_factor * smoothed_one)[:, None] * bed_onehot
        velocity = column_map(bed_source, factors, local_neighbours)
        surface = jnp.sum(velocity * surface_mask, axis=1)
        misfit = column_weight * surface
        adjoint = column_map(misfit[:, None] * surface_mask, factors, local_neighbours)
        return jnp.sum(bed_factor * adjoint[:, 0], axis=0)
    pulled = lax.map(hessian_column, smoothed)
    applied = prior_solve(pulled, prior_reaction)
    cell_count = NX * NY
    applied_rows = applied.reshape(B, cell_count)
    basis_rows = lanczos_block.reshape(B, cell_count)
    prior_rows = previous_block.reshape(B, cell_count)
    residual_rows = applied_rows - jnp.dot(previous_beta, prior_rows, precision=highest)
    block_alpha = jnp.dot(basis_rows, jnp.transpose(residual_rows), precision=highest) / cell_count
    projected = residual_rows - jnp.dot(jnp.transpose(block_alpha), basis_rows, precision=highest)
    gram_matrix = jnp.dot(projected, jnp.transpose(projected), precision=highest) / cell_count
    factor = jnp.linalg.cholesky(gram_matrix)
    next_rows = jax.scipy.linalg.solve_triangular(factor, projected, lower=True)
    return (next_rows.reshape(B, NX, NY), block_alpha, jnp.transpose(factor))
```

```python
import functools

import jax
import jax.numpy as jnp
from jax import lax
from jax.experimental import pallas as pl
from jax.experimental.pallas import tpu as pltpu
from jax.sharding import PartitionSpec as P

base_damping = 0.02
highest = lax.Precision.HIGHEST
SHIFT = 4.25
SCALE = 4.25
LANES = 128
HALO = 8
AXES = ("mx", "my")
VMEM_LIMIT = 56 * 1024 * 1024

F_RATIO = 0
F_PIVOT = 15
F_INV_LAT = 31
F_TOP = 32
F_LAYER = 33
F_BED = 34
F_REACT = 36
FIELDS = 37


def params():
    return pltpu.CompilerParams(vmem_limit_bytes=VMEM_LIMIT)


def lane_ids(shape):
    return lax.broadcasted_iota(jnp.int32, shape, len(shape) - 1)


def row_ids(shape):
    return lax.broadcasted_iota(jnp.int32, shape, len(shape) - 2)


def pack_kernel(
    block, previous, reaction, vert, horiz, friction, velocity, layers, out, prev_out, low, high, rows
):
    vectors, tile_x, tile_y = block.shape
    layer_count = horiz.shape[0]
    depth = layers[...]
    active = [(depth > k).astype(jnp.float32) for k in range(layer_count)]
    zero = jnp.zeros((tile_x, tile_y), jnp.float32)
    up = [vert[k] * active[k + 1] for k in range(layer_count - 1)] + [zero]
    lateral = [horiz[k] * active[k] for k in range(layer_count)]
    pivots = []
    for k in range(layer_count):
        drag = friction[...] if k == 0 else up[k - 1]
        diagonal = (base_damping + lateral[k] + drag + up[k]) * active[k] + (1.0 - active[k])
        if k > 0:
            diagonal = diagonal - up[k - 1] * up[k - 1] / pivots[k - 1]
        pivots.append(diagonal)
    top = zero
    for b in range(vectors):
        rows[pl.ds(b, tile_x, stride=vectors), :] = block[b]

    def put(field, value):
        rows[pl.ds(vectors * tile_x + field * tile_x, tile_x), :] = value

    for k in range(layer_count):
        put(F_PIVOT + k, lateral[k] * lateral[k] / pivots[k])
        is_top = depth == k + 1
        top = jnp.where(is_top, lateral[k] / pivots[k], top)
        if k + 1 < layer_count:
            below = jnp.where(depth > k + 1, lateral[k + 1], 1.0)
            put(F_RATIO + k, up[k] * lateral[k] / (pivots[k] * below))
    put(F_INV_LAT, 1.0 / lateral[0])
    put(F_TOP, top)
    put(F_LAYER, depth.astype(jnp.float32))
    put(F_BED, friction[...] * velocity[0])
    put(F_BED + 1, friction[...] * velocity[1])
    put(F_REACT, reaction[...])
    used = vectors * tile_x + FIELDS * tile_x
    rows[used:, :] = jnp.zeros((rows.shape[0] - used, tile_y), jnp.float32)
    for t in range(rows.shape[0] // LANES):
        out[t] = rows[t * LANES : (t + 1) * LANES, :].T
    low[...] = out[:, 0:HALO, :]
    high[...] = out[:, tile_y - HALO : tile_y, :]
    for b in range(vectors):
        rows[pl.ds(b, tile_x, stride=vectors), :] = previous[b]
    prev_out[...] = rows[0:LANES, :].T


def table_kernel(dest, cell, weight, out):
    count = dest.shape[0]
    devices = out.shape[0]
    onehot = dest[...] == lane_ids((count, devices))
    lower = row_ids((count, count)) >= lane_ids((count, count))
    running = jnp.dot(
        lower.astype(jnp.bfloat16), onehot.astype(jnp.bfloat16), preferred_element_type=jnp.float32
    )
    chosen = onehot.astype(jnp.float32)
    rank = jnp.sum(running * chosen, axis=1, keepdims=True).astype(jnp.int32) - 1
    lane = lane_ids((count, LANES))
    kind = lane // 4
    value = jnp.where(
        kind == 0,
        weight[:, 0:1],
        jnp.where(kind == 1, weight[:, 1:2], jnp.where(kind == 2, cell[...].astype(jnp.float32), 0.0)),
    )
    value = jnp.where(lane % 4 == rank, value, 0.0)
    out[...] = jnp.dot(chosen.T, value, precision=highest, preferred_element_type=jnp.float32)


def neighbour_sum(field, stride):
    rows, lanes = field.shape
    return (
        pltpu.roll(field, 1, 0)
        + pltpu.roll(field, rows - 1, 0)
        + pltpu.roll(field, stride, 1)
        + pltpu.roll(field, lanes - stride, 1)
    )


def shifted_prior(field, reaction, stride):
    image = (reaction - (SHIFT - 4.0)) * field - neighbour_sum(field, stride)
    return jnp.where(reaction > 0.0, image * (1.0 / SCALE), 0.0)


def expand(tiles, field, vectors, tile_x):
    place = field * tile_x
    tile, lane = place // LANES, place % LANES
    out = []
    for part in tiles:
        source = part[tile + 1]
        index = lane + lane_ids(source.shape) // vectors
        out.append(jnp.take_along_axis(source, index, axis=1))
    return jnp.concatenate(out, axis=1)


def fold(row, stride):
    shift = LANES // 2
    while shift >= stride:
        row = row + pltpu.roll(row, shift, 1)
        shift //= 2
    return row


def moment_kernel(vectors, flags, own, left, right, table, out, basis):
    tile_x = LANES // vectors
    rows = own.shape[1]
    weights = (flags[0], None, flags[1])

    def part_tile(t):
        result = []
        for ref, flag in zip((left, own, right), weights):
            value = ref[t]
            result.append(value if flag is None else value * flag)
        return result

    place = F_REACT * tile_x
    tile, lane = place // LANES, place % LANES
    index = lane + lane_ids((rows, LANES)) // vectors
    reaction = jnp.concatenate(
        [jnp.take_along_axis(part, index, axis=1) for part in part_tile(tile + 1)], axis=1
    )
    v0 = jnp.concatenate(part_tile(0), axis=1)
    v1 = shifted_prior(v0, reaction, vectors)
    v2 = shifted_prior(v1, reaction, vectors)
    v3 = shifted_prior(v2, reaction, vectors)
    for i, value in enumerate((v0, v1, v2)):
        for t in range(3):
            basis[i, t] = value[:, t * LANES : (t + 1) * LANES]
    own_of = [v[HALO : rows - HALO, LANES : 2 * LANES] for v in (v0, v1, v2, v3)]
    pairs = ((0, 0), (0, 1), (1, 1), (1, 2), (2, 2), (2, 3))
    group = lane_ids((1, LANES)) // vectors
    message = jnp.zeros((1, LANES), jnp.float32)
    for j, (a, b) in enumerate(pairs):
        total = fold(jnp.sum(own_of[a] * own_of[b], axis=0, keepdims=True), vectors)
        message = jnp.where(group == j + 1, total, message)
    out[...] = table[...] + message


def galerkin(moments):
    m = moments
    a = [SHIFT * m[i] + SCALE * m[i + 1] for i in range(5)]

    def over(top, pivot):
        return jnp.where(pivot > 0.0, top / jnp.where(pivot > 0.0, pivot, 1.0), 0.0)

    l10, l20 = over(a[1], a[0]), over(a[2], a[0])
    d1 = a[2] - l10 * a[1]
    e12 = a[3] - l20 * a[1]
    l21 = over(e12, d1)
    d2 = a[4] - l20 * a[2] - l21 * e12
    z1 = m[1] - l10 * m[0]
    z2 = m[2] - l20 * m[0] - l21 * z1
    y2 = over(z2, d2)
    y1 = over(z1, d1) - l21 * y2
    y0 = over(m[0], a[0]) - l10 * y1 - l20 * y2
    return y0, y1, y2


def split_rows(source, target, flag=None):
    count = target.shape[-3]
    for i in range(count):
        value = source[pl.ds(i, 8, stride=count), :]
        target[i] = value if flag is None else value * flag


def join_rows(source, target):
    count = source.shape[0]
    for t in range(target.shape[0]):
        for i in range(count):
            target[t, pl.ds(i, 8, stride=count), :] = source[i, :, t * LANES : (t + 1) * LANES]


def joined(flat):
    return jnp.concatenate([flat[t] for t in range(3)], axis=1)


def split_parts(own, left, right, flags, parts):
    for p, (ref, flag) in enumerate(((left, flags[0]), (own, None), (right, flags[1]))):
        for t in range(own.shape[0]):
            split_rows(ref.at[t], parts.at[p, t], flag)


def prepare_row(i, parts, ratio, pivot, bed_col, top_col, vectors, tile_x, layer_count):
    tiles = [[parts[p, t, i] for t in range(parts.shape[1])] for p in range(3)]
    get = functools.partial(expand, tiles, vectors=vectors, tile_x=tile_x)
    inv_lat, top, depth = get(F_INV_LAT), get(F_TOP), get(F_LAYER)
    ratios, pivots = [], []
    for k in range(layer_count):
        pivots.append(get(F_PIVOT + k))
        pivot[k, i] = pivots[k]
        if k + 1 < layer_count:
            ratios.append(get(F_RATIO + k))
            ratio[k, i] = ratios[k]
    forward = [inv_lat]
    for k in range(1, layer_count):
        forward.append(ratios[k - 1] * forward[k - 1])
    bed, surf = None, None
    for k in range(layer_count - 1, -1, -1):
        is_top = depth == float(k + 1)
        if bed is None:
            bed = pivots[k] * forward[k]
            surf = jnp.where(is_top, top, 0.0)
        else:
            bed = pivots[k] * forward[k] + ratios[k] * bed
            surf = jnp.where(is_top, top, ratios[k] * surf)
        bed_col[k, i] = bed
        top_col[k, i] = surf
    return get, inv_lat


def lateral_sum(field, c, k, i, stride):
    centre = field[c, k, i + 1]
    lanes = centre.shape[1]
    return (
        field[c, k, i]
        + field[c, k, i + 2]
        + pltpu.roll(centre, stride, 1)
        + pltpu.roll(centre, lanes - stride, 1)
    )


def wrap_rows(field):
    count = field.shape[2] - 2

    def body(k, carry):
        for c in range(2):
            field[c, k, 0] = pltpu.roll(field[c, k, count], 1, 0)
            field[c, k, count + 1] = pltpu.roll(field[c, k, 1], 7, 0)
        return carry

    lax.fori_loop(0, field.shape[1], body, 0)


def sweep(source, target, ratio, pivot, stride, bed_source=None, top_col=None, top_source=None):
    layer_count = pivot.shape[0]

    def body(i, carry):
        for c in range(2):
            carried = []
            for k in range(layer_count):
                value = lateral_sum(source, c, k, i, stride)
                if k > 0:
                    value = value + ratio[k - 1, i] * carried[k - 1]
                elif bed_source is not None:
                    value = value + bed_source[c, i]
                carried.append(value)
            solved = None
            extra = top_source[c, i] if top_source is not None else None
            for k in range(layer_count - 1, -1, -1):
                value = pivot[k, i] * carried[k]
                if solved is not None:
                    value = value + ratio[k, i] * solved
                solved = value
                if extra is not None:
                    value = value + top_col[k, i] * extra
                target[c, k, i + 1] = value
        return carry

    lax.fori_loop(0, pivot.shape[1], body, 0)
    wrap_rows(target)


def velocity_kernel(
    vectors, flags, message, own, left, right, basis,
    misfit, low, high,
    ratio, pivot, bed_col, top_col, one, two, source, parts, flat, smooth, surface, flat_out,
):
    tile_x = LANES // vectors
    layer_count = pivot.shape[0]
    total_rows = own.shape[1]
    count = total_rows // 8
    tile_y = total_rows - 2 * HALO
    group = lane_ids((8, LANES)) // vectors
    summed = jnp.broadcast_to(jnp.sum(message[...], axis=0, keepdims=True), (8, LANES))
    moments = [fold(jnp.where(group == j + 1, summed, 0.0), vectors) for j in range(6)]
    y = [v[0:1] for v in galerkin(moments)]
    for t in range(3):
        flat[t] = y[0] * basis[0, t] + y[1] * basis[1, t] + y[2] * basis[2, t]
    for t in range(3):
        split_rows(flat.at[t], smooth.at[t])
    split_parts(own, left, right, flags, parts)

    def prepare(i, carry):
        get, inv_lat = prepare_row(
            i, parts, ratio, pivot, bed_col, top_col, vectors, tile_x, layer_count
        )
        for c in range(2):
            bed = get(F_BED + c) * jnp.concatenate([smooth[t, i] for t in range(3)], axis=1)
            source[c, i] = bed * inv_lat
            for k in range(layer_count):
                one[c, k, i + 1] = bed_col[k, i] * bed
        return carry

    lax.fori_loop(0, count, prepare, 0)
    wrap_rows(one)
    sweep(one, two, ratio, pivot, vectors, bed_source=source)
    sweep(two, one, ratio, pivot, vectors, bed_source=source)
    middle = slice(LANES, 2 * LANES)

    def finish(i, carry):
        for c in range(2):
            total = top_col[0, i, :, middle] * source[c, i, :, middle]
            for k in range(layer_count):
                total = total + top_col[k, i, :, middle] * lateral_sum(one, c, k, i, vectors)[:, middle]
            surface[c, i] = total
        return carry

    lax.fori_loop(0, count, finish, 0)

    lane = lane_ids((LANES, LANES))
    for c in range(2):
        total = jnp.zeros((LANES, LANES), jnp.float32)
        for r in range(4):
            cell = message[:, 8 + r : 9 + r].astype(jnp.int32)
            weight = message[:, 4 * c + r : 4 * c + r + 1]
            at_row = (cell % tile_y == lane).astype(jnp.float32)
            at_lane = jnp.where(cell // tile_y == lane // vectors, weight, 0.0)
            total = total + jnp.dot(
                at_row.T, at_lane, precision=highest, preferred_element_type=jnp.float32
            )
        join_rows(surface.at[c], flat_out)
        misfit[c] = total * flat_out[0, HALO : HALO + tile_y, :]
    low[...] = misfit[:, 0:HALO, :]
    high[...] = misfit[:, tile_y - HALO :, :]


def adjoint_kernel(
    vectors, flags, own, left, right, misfit, misfit_left, misfit_right, previous,
    out, stacked,
    ratio, pivot, bed_col, top_col, one, two, source, parts, flat, pulled, bed, reaction_all, lateral, sides,
):
    tile_x = LANES // vectors
    layer_count = pivot.shape[0]
    total_rows = own.shape[1]
    count = total_rows // 8
    split_parts(own, left, right, flags, parts)
    for c in range(2):
        split_rows(misfit_left.at[c], sides.at[c, 0], flags[0])
        split_rows(misfit.at[c], sides.at[c, 1])
        split_rows(misfit_right.at[c], sides.at[c, 2], flags[1])

    def prepare(i, carry):
        get, inv_lat = prepare_row(
            i, parts, ratio, pivot, bed_col, top_col, vectors, tile_x, layer_count
        )
        reaction_all[i] = get(F_REACT)
        lateral[i] = inv_lat
        for c in range(2):
            value = jnp.concatenate([sides[c, t, i] for t in range(3)], axis=1)
            source[c, i] = value
            bed[c, i] = get(F_BED + c)
            for k in range(layer_count):
                one[c, k, i + 1] = top_col[k, i] * value
        return carry

    lax.fori_loop(0, count, prepare, 0)
    wrap_rows(one)
    sweep(one, two, ratio, pivot, vectors, top_col=top_col, top_source=source)
    sweep(two, one, ratio, pivot, vectors, top_col=top_col, top_source=source)

    def finish(i, carry):
        total = None
        for c in range(2):
            value = top_col[0, i] * lateral[i] * source[c, i]
            for k in range(layer_count):
                value = value + bed_col[k, i] * lateral_sum(one, c, k, i, vectors)
            value = bed[c, i] * value
            total = value if total is None else total + value
        pulled[i] = total
        return carry

    lax.fori_loop(0, count, finish, 0)
    join_rows(reaction_all, flat)
    reaction = joined(flat)
    join_rows(pulled, flat)
    v0 = joined(flat)
    v1 = shifted_prior(v0, reaction, vectors)
    v2 = shifted_prior(v1, reaction, vectors)
    v3 = shifted_prior(v2, reaction, vectors)
    v0, v1, v2, v3 = [v[HALO : total_rows - HALO, LANES : 2 * LANES] for v in (v0, v1, v2, v3)]
    x = own[0, HALO : total_rows - HALO, :]
    p = previous[...]
    flipped = [v.T for v in (v0, v1, v2, p, x)]
    for i, value in enumerate(flipped):
        for at in range(tile_x):
            stacked[at, i * vectors : (i + 1) * vectors, :] = value[at * vectors : (at + 1) * vectors, :]
    t0, t1, t2, tp, tx = flipped
    pairs = (
        (t0, v0), (t0, v1), (t1, v1), (t1, v2), (t2, v2),
        (tx, v0), (tx, v1), (tx, v2),
        (t0, p), (t1, p), (t2, p),
        (tx, x), (tx, p), (tp, p),
    )
    same = row_ids((LANES, LANES)) // vectors == lane_ids((LANES, LANES)) // vectors
    group = lane_ids((vectors, LANES)) // vectors
    halves = [jnp.zeros((vectors, LANES), jnp.float32)] * 2
    for n, (a, b) in enumerate(pairs):
        product = jnp.dot(a, b, precision=highest, preferred_element_type=jnp.float32)
        product = jnp.where(same, product, 0.0)
        block = product[0:vectors]
        for at in range(1, tile_x):
            block = block + product[at * vectors : (at + 1) * vectors]
        block = fold(block, vectors)
        halves[n // tile_x] = jnp.where(group == n % tile_x, block, halves[n // tile_x])
    last = fold(jnp.sum(v2 * v3, axis=0, keepdims=True), vectors)
    n = len(pairs)
    halves[n // tile_x] = jnp.where(group == n % tile_x, last, halves[n // tile_x])
    both = jnp.concatenate(halves, axis=1)
    for i in range(out.shape[0]):
        out[i] = both


def partial_kernel(received, out):
    total = jnp.sum(received[...], axis=0)
    for i in range(out.shape[0]):
        out[i] = total


def finish_kernel(cells, received, stacked, beta_ref, next_out, alpha_out, beta_out):
    vectors = beta_ref.shape[0]
    total = jnp.sum(received[...], axis=0)

    def block(n):
        return total[:, n * vectors : (n + 1) * vectors]

    def dot(a, b, dims=((1,), (0,))):
        return lax.dot_general(a, b, (dims, ((), ())), precision=highest, preferred_element_type=jnp.float32)

    shape = (vectors, vectors)
    eye = row_ids(shape) == lane_ids(shape)
    s = [block(n) for n in range(5)]
    moments = [jnp.sum(jnp.where(eye, m, 0.0), axis=0, keepdims=True) for m in s]
    moments.append(block(14)[0:1])
    along = galerkin(moments)
    down = [jnp.sum(jnp.where(eye, v, 0.0), axis=1, keepdims=True) for v in along]
    xv = [block(5 + k) for k in range(3)]
    vp = [block(8 + k) for k in range(3)]
    xx, xp, pp = block(11), block(12), block(13)
    beta = beta_ref[...]
    last = ((1,), (1,))
    first = ((0,), (0,))
    xr = xv[0] * along[0] + xv[1] * along[1] + xv[2] * along[2] - dot(xp, beta, last)
    alpha = xr * (1.0 / cells)
    alpha_out[...] = alpha
    rr = None
    for k in range(3):
        for l in range(3):
            term = down[k] * along[l] * s[k + l]
            rr = term if rr is None else rr + term
    cross = dot(down[0] * vp[0] + down[1] * vp[1] + down[2] * vp[2], beta, last)
    rr = rr - cross - cross.T + dot(beta, dot(pp, beta, last))
    gram = rr * (1.0 / cells) - 2.0 * dot(alpha, alpha, first) + dot(
        alpha, dot(xx * (1.0 / cells), alpha), first
    )
    gram = 0.5 * (gram + gram.T)
    work = jnp.concatenate(
        [gram, eye.astype(jnp.float32), jnp.zeros((vectors, LANES - 2 * vectors), jnp.float32)], axis=1
    )
    down_id = row_ids(work.shape)
    for j in range(vectors):
        row = work[j : j + 1, :]
        scale = 1.0 / jnp.sqrt(row[:, j : j + 1])
        row = row * scale
        column = work[:, j : j + 1] * scale
        work = jnp.where(down_id > j, work - column * row, jnp.where(down_id == j, row, work))
    beta_out[...] = jnp.where(row_ids(shape) <= lane_ids(shape), work[:, 0:vectors], 0.0)
    inverse = work[:, vectors : 2 * vectors]
    mix = jnp.concatenate(
        [inverse * v for v in along] + [-dot(inverse, beta), -dot(inverse, alpha, last)], axis=1
    )
    for at in range(stacked.shape[0]):
        next_out[:, at, :] = dot(mix, stacked[at])


def shards(
    lanczos_block,
    previous_block,
    previous_beta,
    prior_reaction,
    vert_coupling,
    horiz_coupling,
    friction,
    base_velocity,
    layers,
    obs_dest,
    obs_cell,
    obs_weight,
):
    vectors, tile_x, tile_y = lanczos_block.shape
    layer_count = horiz_coupling.shape[0]
    obs_rows = obs_cell.shape[0]
    size_x, size_y = lax.axis_size("mx"), lax.axis_size("my")
    devices = size_x * size_y
    cells = tile_x * tile_y * devices
    at_x, at_y = lax.axis_index("mx"), lax.axis_index("my")
    flags = jnp.stack([at_x > 0, at_x + 1 < size_x]).astype(jnp.float32)
    low_flag = (at_y > 0).astype(jnp.float32)
    high_flag = (at_y + 1 < size_y).astype(jnp.float32)
    forward_y = [(i, (i + 1) % size_y) for i in range(size_y)]
    backward_y = [(i, (i - 1) % size_y) for i in range(size_y)]
    forward_x = [(i, (i + 1) % size_x) for i in range(size_x)]
    backward_x = [(i, (i - 1) % size_x) for i in range(size_x)]
    f32 = jnp.float32
    rows = tile_y + 2 * HALO
    wide = 3 * LANES
    tiles = -(-(vectors * tile_x + FIELDS * tile_x) // LANES)
    smem = pl.BlockSpec(memory_space=pltpu.SMEM)
    vmem = pl.BlockSpec(memory_space=pltpu.VMEM)

    def shape(*dims):
        return jax.ShapeDtypeStruct(dims, f32)

    packed, previous, low, high = pl.pallas_call(
        pack_kernel,
        out_shape=(
            shape(tiles, tile_y, LANES), shape(tile_y, LANES), shape(tiles, HALO, LANES), shape(tiles, HALO, LANES)
        ),
        scratch_shapes=[pltpu.VMEM((tiles * LANES, tile_y), f32)],
        compiler_params=params(),
        name="pack",
    )(
        lanczos_block, previous_block, prior_reaction, vert_coupling, horiz_coupling,
        friction, base_velocity, layers,
    )
    table = pl.pallas_call(
        table_kernel, out_shape=shape(devices, LANES), compiler_params=params(), name="table"
    )(obs_dest, obs_cell.reshape(obs_rows, 1), obs_weight)

    from_low = lax.ppermute(high, "my", forward_y)
    from_high = lax.ppermute(low, "my", backward_y)
    own = jnp.concatenate([from_low * low_flag, packed, from_high * high_flag], axis=1)
    left = lax.ppermute(own, "mx", forward_x)
    right = lax.ppermute(own, "mx", backward_x)

    message, basis = pl.pallas_call(
        functools.partial(moment_kernel, vectors),
        out_shape=(shape(devices, LANES), shape(3, 3, rows, LANES)),
        in_specs=[smem, vmem, vmem, vmem, vmem],
        compiler_params=params(),
        name="moments",
    )(flags, own, left, right, table)
    message = lax.all_to_all(message, AXES, split_axis=0, concat_axis=0, tiled=True)

    count = rows // 8
    columns = [
        pltpu.VMEM((layer_count - 1, count, 8, wide), f32),
        pltpu.VMEM((layer_count, count, 8, wide), f32),
        pltpu.VMEM((layer_count, count, 8, wide), f32),
        pltpu.VMEM((layer_count, count, 8, wide), f32),
        pltpu.VMEM((2, layer_count, count + 2, 8, wide), f32),
        pltpu.VMEM((2, layer_count, count + 2, 8, wide), f32),
        pltpu.VMEM((2, count, 8, wide), f32),
        pltpu.VMEM((3, tiles, count, 8, LANES), f32),
        pltpu.VMEM((3, rows, LANES), f32),
    ]
    misfit, low, high = pl.pallas_call(
        functools.partial(velocity_kernel, vectors),
        out_shape=(shape(2, tile_y, LANES), shape(2, HALO, LANES), shape(2, HALO, LANES)),
        in_specs=[smem] + [vmem] * 5,
        scratch_shapes=columns
        + [
            pltpu.VMEM((3, count, 8, LANES), f32),
            pltpu.VMEM((2, count, 8, LANES), f32),
            pltpu.VMEM((1, rows, LANES), f32),
        ],
        compiler_params=params(),
        name="velocity",
    )(flags, message, own, left, right, basis)

    from_low = lax.ppermute(high, "my", forward_y)
    from_high = lax.ppermute(low, "my", backward_y)
    misfit = jnp.concatenate([from_low * low_flag, misfit, from_high * high_flag], axis=1)
    misfit_left = lax.ppermute(misfit, "mx", forward_x)
    misfit_right = lax.ppermute(misfit, "mx", backward_x)

    products, stacked = pl.pallas_call(
        functools.partial(adjoint_kernel, vectors),
        out_shape=(shape(size_x, vectors, 2 * LANES), shape(tile_x, 5 * vectors, tile_y)),
        in_specs=[smem] + [vmem] * 7,
        scratch_shapes=columns
        + [
            pltpu.VMEM((count, 8, wide), f32),
            pltpu.VMEM((2, count, 8, wide), f32),
            pltpu.VMEM((count, 8, wide), f32),
            pltpu.VMEM((count, 8, wide), f32),
            pltpu.VMEM((2, 3, count, 8, LANES), f32),
        ],
        compiler_params=params(),
        name="adjoint",
    )(flags, own, left, right, misfit, misfit_left, misfit_right, previous)

    products = lax.all_to_all(products, "mx", split_axis=0, concat_axis=0, tiled=True)
    products = pl.pallas_call(
        partial_kernel,
        out_shape=shape(size_y, vectors, 2 * LANES),
        compiler_params=params(),
        name="partial",
    )(products)
    products = lax.all_to_all(products, "my", split_axis=0, concat_axis=0, tiled=True)
    return pl.pallas_call(
        functools.partial(finish_kernel, float(cells)),
        out_shape=(shape(vectors, tile_x, tile_y), shape(vectors, vectors), shape(vectors, vectors)),
        compiler_params=params(),
        name="finish",
    )(products, stacked, previous_beta)


def solution(mesh):
    in_specs = (
        P(None, "mx", "my"),
        P(None, "mx", "my"),
        P(),
        P("mx", "my"),
        P(None, "mx", "my"),
        P(None, "mx", "my"),
        P("mx", "my"),
        P(None, "mx", "my"),
        P("mx", "my"),
        P(("mx", "my"), None),
        P(("mx", "my")),
        P(("mx", "my"), None),
    )
    out_specs = (P(None, "mx", "my"), P(), P())
    return jax.shard_map(shards, mesh=mesh, in_specs=in_specs, out_specs=out_specs, check_vma=False)
```

```python
import functools

import jax
import jax.numpy as jnp
from jax import lax
from jax.experimental import pallas as pl
from jax.experimental.pallas import tpu as pltpu
from jax.sharding import PartitionSpec as P

base_damping = 0.02
highest = lax.Precision.HIGHEST
SHIFT = 4.25
SCALE = 4.25
LANES = 128
HALO = 8
AXES = ("mx", "my")
VMEM_LIMIT = 56 * 1024 * 1024

F_RATIO = 0
F_PIVOT = 15
F_INV_LAT = 31
F_TOP = 32
F_LAYER = 33
F_BED = 34
F_REACT = 36
FIELDS = 37


def params():
    return pltpu.CompilerParams(vmem_limit_bytes=VMEM_LIMIT)


def lane_ids(shape):
    return lax.broadcasted_iota(jnp.int32, shape, len(shape) - 1)


def row_ids(shape):
    return lax.broadcasted_iota(jnp.int32, shape, len(shape) - 2)


def pack_kernel(
    block, previous, reaction, vert, horiz, friction, velocity, layers, out, prev_out, low, high, rows
):
    vectors, tile_x, tile_y = block.shape
    layer_count = horiz.shape[0]
    depth = layers[...]
    active = [(depth > k).astype(jnp.float32) for k in range(layer_count)]
    zero = jnp.zeros((tile_x, tile_y), jnp.float32)
    up = [vert[k] * active[k + 1] for k in range(layer_count - 1)] + [zero]
    lateral = [horiz[k] * active[k] for k in range(layer_count)]
    pivots = []
    for k in range(layer_count):
        drag = friction[...] if k == 0 else up[k - 1]
        diagonal = (base_damping + lateral[k] + drag + up[k]) * active[k] + (1.0 - active[k])
        if k > 0:
            diagonal = diagonal - up[k - 1] * up[k - 1] / pivots[k - 1]
        pivots.append(diagonal)
    top = zero
    for b in range(vectors):
        rows[pl.ds(b, tile_x, stride=vectors), :] = block[b]

    def put(field, value):
        rows[pl.ds(vectors * tile_x + field * tile_x, tile_x), :] = value

    for k in range(layer_count):
        put(F_PIVOT + k, lateral[k] * lateral[k] / pivots[k])
        is_top = depth == k + 1
        top = jnp.where(is_top, lateral[k] / pivots[k], top)
        if k + 1 < layer_count:
            below = jnp.where(depth > k + 1, lateral[k + 1], 1.0)
            put(F_RATIO + k, up[k] * lateral[k] / (pivots[k] * below))
    put(F_INV_LAT, 1.0 / lateral[0])
    put(F_TOP, top)
    put(F_LAYER, depth.astype(jnp.float32))
    put(F_BED, friction[...] * velocity[0])
    put(F_BED + 1, friction[...] * velocity[1])
    put(F_REACT, reaction[...])
    used = vectors * tile_x + FIELDS * tile_x
    rows[used:, :] = jnp.zeros((rows.shape[0] - used, tile_y), jnp.float32)
    for t in range(rows.shape[0] // LANES):
        out[t] = rows[t * LANES : (t + 1) * LANES, :].T
    low[...] = out[:, 0:HALO, :]
    high[...] = out[:, tile_y - HALO : tile_y, :]
    for b in range(vectors):
        rows[pl.ds(b, tile_x, stride=vectors), :] = previous[b]
    prev_out[...] = rows[0:LANES, :].T


def table_kernel(dest, cell, weight, out):
    count = dest.shape[0]
    devices = out.shape[0]
    onehot = dest[...] == lane_ids((count, devices))
    lower = row_ids((count, count)) >= lane_ids((count, count))
    running = jnp.dot(
        lower.astype(jnp.bfloat16), onehot.astype(jnp.bfloat16), preferred_element_type=jnp.float32
    )
    chosen = onehot.astype(jnp.float32)
    rank = jnp.sum(running * chosen, axis=1, keepdims=True).astype(jnp.int32) - 1
    lane = lane_ids((count, LANES))
    kind = lane // 4
    value = jnp.where(
        kind == 0,
        weight[:, 0:1],
        jnp.where(kind == 1, weight[:, 1:2], jnp.where(kind == 2, cell[...].astype(jnp.float32), 0.0)),
    )
    value = jnp.where(lane % 4 == rank, value, 0.0)
    out[...] = jnp.dot(chosen.T, value, precision=highest, preferred_element_type=jnp.float32)


def fold(row, stride):
    shift = LANES // 2
    while shift >= stride:
        row = row + pltpu.roll(row, shift, 1)
        shift //= 2
    return row


def gather(tile, index):
    return jnp.take_along_axis(tile, index, axis=1)


def pick(which, values):
    result = values[-1]
    for n in range(len(values) - 2, -1, -1):
        result = jnp.where(which == n, values[n], result)
    return result


def tile_rows(vectors, tiles, offset, tile):
    return offset + (lane_ids((8, LANES)) // vectors) * tiles + tile


def to_blocked(parts, vectors, tiles, offset):
    tile_x = LANES // vectors
    out = []
    for t in range(tiles):
        row = tile_rows(vectors, tiles, offset, t)
        index = (row % tile_x) * vectors + lane_ids((8, LANES)) % vectors
        out.append(pick(row // tile_x, [gather(part, index) for part in parts]))
    return out


def reblock(values, vectors, tiles, offset):
    out = []
    for t in range(tiles):
        row = tile_rows(vectors, tiles, offset, t)
        index = (row // len(values)) * vectors + lane_ids((8, LANES)) % vectors
        out.append(pick(row % len(values), [gather(value, index) for value in values]))
    return out


def to_own(values, vectors, offset):
    tiles = len(values)
    row = lane_ids((8, LANES)) // vectors + LANES // vectors - offset
    index = (row // tiles) * vectors + lane_ids((8, LANES)) % vectors
    return pick(row % tiles, [gather(value, index) for value in values])


def split_rows(source, target, flag=None):
    count = target.shape[-3]
    for i in range(count):
        value = source[pl.ds(i, 8, stride=count), :]
        target[i] = value if flag is None else value * flag


def join_rows(source, target):
    count = source.shape[0]
    for i in range(count):
        target[pl.ds(i, 8, stride=count), :] = source[i]


def put_tile(field, at, t, tiles, stride, value):
    field[(*at, t + 1)] = value
    if t == 0:
        field[(*at, tiles + 1)] = pltpu.roll(value, LANES - stride, 1)
    if t == tiles - 1:
        field[(*at, 0)] = pltpu.roll(value, stride, 1)


def lateral_sum(field, at, i, t):
    return (field[(*at, i, t + 1)] + field[(*at, i + 2, t + 1)]) + (
        field[(*at, i + 1, t)] + field[(*at, i + 1, t + 2)]
    )


def wrap_rows(field, at, count, tiles):
    for t in range(1, tiles + 1):
        field[(*at, 0, t)] = pltpu.roll(field[(*at, count, t)], 1, 0)
        field[(*at, count + 1, t)] = pltpu.roll(field[(*at, 1, t)], 7, 0)


def wrap_layers(field, tiles):
    count = field.shape[2] - 2

    def body(k, carry):
        for c in range(2):
            wrap_rows(field, (c, k), count, tiles)
        return carry

    lax.fori_loop(0, field.shape[1], body, 0)


def own_cells(vectors, tiles, offset, count, tile_y, i, t):
    tile_x = LANES // vectors
    row = tile_rows(vectors, tiles, offset, t)
    column = row_ids((8, LANES)) * count + i
    return (row >= tile_x) & (row < 2 * tile_x) & (column >= HALO) & (column < HALO + tile_y)


def shifted_prior(field, i, t, reaction):
    image = (reaction - (SHIFT - 4.0)) * field[i + 1, t + 1] - lateral_sum(field, (), i, t)
    return jnp.where(reaction > 0.0, image * (1.0 / SCALE), 0.0)


def krylov(first, second, third, reaction, vectors, count, tile_y):
    tiles = reaction.shape[1]

    def step(source, target):
        wrap_rows(source, (), count, tiles)
        for i in range(count):
            for t in range(tiles):
                value = shifted_prior(source, i, t, reaction[i, t])
                put_tile(target, (i + 1,), t, tiles, vectors, value)

    step(first, second)
    step(second, third)
    wrap_rows(third, (), count, tiles)
    total = jnp.zeros((8, LANES), jnp.float32)
    for i in range(count):
        for t in range(tiles):
            value = shifted_prior(third, i, t, reaction[i, t]) * third[i + 1, t + 1]
            total = total + jnp.where(own_cells(vectors, tiles, 0, count, tile_y, i, t), value, 0.0)
    return total


def moment_kernel(
    vectors, flags, own, left, right, table, out, basis, fields, parts, reaction, v0, v1, v2
):
    tile_x = LANES // vectors
    rows = own.shape[1]
    count = rows // 8
    tile_y = rows - 2 * HALO
    for p, (ref, flag) in enumerate(((left, flags[0]), (own, None), (right, flags[1]))):
        for t in range(own.shape[0]):
            split_rows(ref.at[t], parts.at[p, t], flag)
    lane = lane_ids((8, LANES))

    def arrange(i, carry):
        for t, value in enumerate(to_blocked([parts[p, 0, i] for p in range(3)], vectors, 3, 0)):
            put_tile(v0, (i + 1,), t, 3, vectors, value)
        for q in range(fields.shape[0]):
            per_tile = LANES // (4 * tile_x)
            index = (q % per_tile) * 4 * tile_x + (lane // 32) * tile_x + lane % tile_x
            fields[q, i] = pick(
                (lane % 32) // tile_x, [gather(parts[p, 1 + q // per_tile, i], index) for p in range(3)]
            )
        for t in range(3):
            reaction[i, t] = expand(fields, F_REACT, i, t, 3, 0, vectors)
        return carry

    lax.fori_loop(0, count, arrange, 0)
    last = krylov(v0, v1, v2, reaction, vectors, count, tile_y)
    sums = [jnp.zeros((8, LANES), jnp.float32) for _ in range(5)]
    for i in range(count):
        for t in range(3):
            mine = own_cells(vectors, 3, 0, count, tile_y, i, t)
            a, b, c = v0[i + 1, t + 1], v1[i + 1, t + 1], v2[i + 1, t + 1]
            basis[0, i, t] = a
            basis[1, i, t] = b
            basis[2, i, t] = c
            a, b, c = [jnp.where(mine, v, 0.0) for v in (a, b, c)]
            sums = [
                total + one * two
                for total, one, two in zip(sums, (a, a, b, b, c), (a, b, b, c, c))
            ]
    sums.append(last)
    group = lane_ids((1, LANES)) // vectors
    message = jnp.zeros((1, LANES), jnp.float32)
    for j, value in enumerate(sums):
        total = fold(jnp.sum(value, axis=0, keepdims=True), vectors)
        message = jnp.where(group == j + 1, total, message)
    out[...] = table[...] + message


def expand(fields, field, i, t, tiles, offset, vectors):
    index = (field % 4) * 32 + tile_rows(vectors, tiles, offset, t)
    return gather(fields[field // 4, i], index)


def galerkin(moments):
    m = moments
    a = [SHIFT * m[i] + SCALE * m[i + 1] for i in range(5)]

    def over(top, pivot):
        return jnp.where(pivot > 0.0, top / jnp.where(pivot > 0.0, pivot, 1.0), 0.0)

    l10, l20 = over(a[1], a[0]), over(a[2], a[0])
    d1 = a[2] - l10 * a[1]
    e12 = a[3] - l20 * a[1]
    l21 = over(e12, d1)
    d2 = a[4] - l20 * a[2] - l21 * e12
    z1 = m[1] - l10 * m[0]
    z2 = m[2] - l20 * m[0] - l21 * z1
    y2 = over(z2, d2)
    y1 = over(z1, d1) - l21 * y2
    y0 = over(m[0], a[0]) - l10 * y1 - l20 * y2
    return y0, y1, y2


def expand_all(fields, wide, vectors, offset):
    groups, count = fields.shape[:2]
    value = fields[...].reshape(groups * count * 8, LANES)
    high = value.astype(jnp.bfloat16)
    value = value - high.astype(jnp.float32)
    middle = value.astype(jnp.bfloat16)
    low = (value - middle.astype(jnp.float32)).astype(jnp.bfloat16)
    both = jnp.concatenate([high, middle], axis=1)
    lanes = wide.shape[-1]
    shape = (2 * LANES, lanes)
    column = lane_ids(shape)
    row = offset + (column % LANES // vectors) * (lanes // LANES) + column // LANES
    source = row_ids(shape) % LANES
    for j in range(4):
        chosen = (source == j * 32 + row).astype(jnp.float32).astype(jnp.bfloat16)
        out = jnp.dot(both, chosen, preferred_element_type=jnp.float32)
        out = out + jnp.dot(low, chosen[:LANES], preferred_element_type=jnp.float32)
        wide[j] = out.reshape(groups, count, 8, lanes)


def get_field(wide, field, i, t):
    return wide[field % 4, field // 4, i, :, t * LANES : (t + 1) * LANES]


def prepare_row(wide, i, bed_col, top_col, layer_count, tiles):
    across = range(tiles)
    get = functools.partial(get_field, wide, i=i)
    inv_lat = [get(F_INV_LAT, t=t) for t in across]
    top = [get(F_TOP, t=t) for t in across]
    depth = [get(F_LAYER, t=t) for t in across]
    forward = [inv_lat]
    for k in range(1, layer_count):
        forward.append([get(F_RATIO + k - 1, t=t) * forward[k - 1][t] for t in across])
    beds, tops = [None] * layer_count, [None] * layer_count
    for k in range(layer_count - 1, -1, -1):
        beds[k], tops[k] = [], []
        for t in across:
            bed = get(F_PIVOT + k, t=t) * forward[k][t]
            below = 0.0
            if k + 1 < layer_count:
                ratio = get(F_RATIO + k, t=t)
                bed = bed + ratio * beds[k + 1][t]
                below = ratio * tops[k + 1][t]
            surf = jnp.where(depth[t] == float(k + 1), top[t], below)
            if bed_col is not None:
                bed_col[k, i, t] = bed
            top_col[k, i, t] = surf
            beds[k].append(bed)
            tops[k].append(surf)
    return inv_lat, beds, tops


def put_outer(field, i, columns, values, stride):
    tiles = len(values[0])
    right = [pltpu.roll(v[0], LANES - stride, 1) for v in values]
    left = [pltpu.roll(v[tiles - 1], stride, 1) for v in values]
    for k, column in enumerate(columns):
        right_column = pltpu.roll(column[0], LANES - stride, 1)
        left_column = pltpu.roll(column[tiles - 1], stride, 1)
        for c, value in enumerate(values):
            field[c, k, i + 1, 0] = left_column * left[c]
            for t in range(tiles):
                field[c, k, i + 1, t + 1] = column[t] * value[t]
            field[c, k, i + 1, tiles + 1] = right_column * right[c]


def sweep(source, target, wide, stride, bed_source=None, top_col=None, top_source=None):
    layer_count, count, tiles = target.shape[1], target.shape[2] - 2, target.shape[3] - 2
    across = [(t, c) for t in range(tiles) for c in range(2)]

    def body(i, carry):
        carried = []
        for k in range(layer_count):
            now = {}
            for t, c in across:
                value = lateral_sum(source, (c, k), i, t)
                if k > 0:
                    value = value + get_field(wide, F_RATIO + k - 1, i, t) * carried[k - 1][t, c]
                elif bed_source is not None:
                    value = value + bed_source[c, i, t]
                now[t, c] = value
            carried.append(now)
        solved = {}
        for k in range(layer_count - 1, -1, -1):
            for t, c in across:
                value = get_field(wide, F_PIVOT + k, i, t) * carried[k][t, c]
                if k + 1 < layer_count:
                    value = value + get_field(wide, F_RATIO + k, i, t) * solved[t, c]
                solved[t, c] = value
                if top_source is not None:
                    value = value + top_col[k, i, t] * top_source[c, i, t]
                put_tile(target, (c, k, i + 1), t, tiles, stride, value)
        return carry

    lax.fori_loop(0, count, body, 0)
    wrap_layers(target, tiles)


def velocity_kernel(
    vectors, flags, message, basis, fields,
    misfit, low, high,
    wide, top_col, one, two, source, surface, flat,
):
    tile_x = LANES // vectors
    layer_count, count, tiles = top_col.shape[:3]
    tile_y = count * 8 - 2 * HALO
    offset = tile_x // 2
    group = lane_ids((8, LANES)) // vectors
    summed = jnp.broadcast_to(jnp.sum(message[...], axis=0, keepdims=True), (8, LANES))
    moments = [fold(jnp.where(group == j + 1, summed, 0.0), vectors) for j in range(6)]
    y = galerkin(moments)

    def prepare(i, carry):
        smooth = [y[0] * basis[0, i, t] + y[1] * basis[1, i, t] + y[2] * basis[2, i, t] for t in range(3)]
        smooth = reblock(smooth, vectors, tiles, offset)
        inv_lat, beds, _ = prepare_row(wide, i, None, top_col, layer_count, tiles)
        values = [
            [get_field(wide, F_BED + c, i, t) * smooth[t] for t in range(tiles)] for c in range(2)
        ]
        for c in range(2):
            for t in range(tiles):
                source[c, i, t] = values[c][t] * inv_lat[t]
        put_outer(one, i, beds, values, vectors)
        return carry

    expand_all(fields, wide, vectors, offset)

    lax.fori_loop(0, count, prepare, 0)
    wrap_layers(one, tiles)
    sweep(one, two, wide, vectors, bed_source=source)
    sweep(two, one, wide, vectors, bed_source=source)

    def finish(i, carry):
        across = [(c, t) for c in range(2) for t in range(tiles)]
        values = {(c, t): top_col[0, i, t] * source[c, i, t] for c, t in across}
        for k in range(layer_count):
            for c, t in across:
                values[c, t] = values[c, t] + top_col[k, i, t] * lateral_sum(one, (c, k), i, t)
        for c in range(2):
            surface[c, i] = to_own([values[c, t] for t in range(tiles)], vectors, offset)
        return carry

    lax.fori_loop(0, count, finish, 0)

    lane = lane_ids((LANES, LANES))
    for c in range(2):
        total = jnp.zeros((LANES, LANES), jnp.float32)
        for r in range(4):
            cell = message[:, 8 + r : 9 + r].astype(jnp.int32)
            weight = message[:, 4 * c + r : 4 * c + r + 1]
            at_row = (cell % tile_y == lane).astype(jnp.float32)
            at_lane = jnp.where(cell // tile_y == lane // vectors, weight, 0.0)
            total = total + jnp.dot(
                at_row.T, at_lane, precision=highest, preferred_element_type=jnp.float32
            )
        join_rows(surface.at[c], flat)
        misfit[c] = total * flat[HALO : HALO + tile_y, :]
    low[...] = misfit[:, 0:HALO, :]
    high[...] = misfit[:, tile_y - HALO :, :]


def adjoint_kernel(
    vectors, flags, fields, misfit, misfit_left, misfit_right, basis, previous,
    out, stacked,
    wide, top_col, one, two, source, bed_col, sides, bed, reaction, v0, v1, v2, natural, flat,
):
    tile_x = LANES // vectors
    layer_count, count, tiles = top_col.shape[:3]
    tile_y = count * 8 - 2 * HALO
    for c in range(2):
        split_rows(misfit_left.at[c], sides.at[c, 0], flags[0])
        split_rows(misfit.at[c], sides.at[c, 1])
        split_rows(misfit_right.at[c], sides.at[c, 2], flags[1])

    def prepare(i, carry):
        values = [to_blocked([sides[c, p, i] for p in range(3)], vectors, tiles, 0) for c in range(2)]
        inv_lat, _, tops = prepare_row(wide, i, bed_col, top_col, layer_count, tiles)
        for t in range(tiles):
            reaction[i, t] = get_field(wide, F_REACT, i, t)
            total = None
            for c in range(2):
                value = values[c][t]
                source[c, i, t] = value
                drag = get_field(wide, F_BED + c, i, t)
                bed[c, i, t] = drag
                total = drag * value if total is None else total + drag * value
            v1[i + 1, t + 1] = total * (tops[0][t] * inv_lat[t])
        put_outer(one, i, tops, values, vectors)
        return carry

    expand_all(fields, wide, vectors, 0)

    lax.fori_loop(0, count, prepare, 0)
    wrap_layers(one, tiles)
    sweep(one, two, wide, vectors, top_col=top_col, top_source=source)
    sweep(two, one, wide, vectors, top_col=top_col, top_source=source)

    def finish(i, carry):
        totals = {}
        for k in range(layer_count):
            for c in range(2):
                for t in range(tiles):
                    value = bed_col[k, i, t] * lateral_sum(one, (c, k), i, t)
                    totals[c, t] = value if k == 0 else totals[c, t] + value
        for t in range(tiles):
            value = v1[i + 1, t + 1] + (bed[0, i, t] * totals[0, t] + bed[1, i, t] * totals[1, t])
            put_tile(v0, (i + 1,), t, tiles, vectors, value)
        return carry

    lax.fori_loop(0, count, finish, 0)
    last = krylov(v0, v1, v2, reaction, vectors, count, tile_y)
    own = []
    for n, field in enumerate((v0, v1, v2, basis.at[0])):
        at = 0 if n == 3 else 1
        for i in range(count):
            natural[i] = to_own([field[i + at, t + at] for t in range(tiles)], vectors, 0)
        join_rows(natural, flat)
        own.append(flat[HALO : HALO + tile_y, :])
    v0, v1, v2, x = own
    p = previous[...]
    flipped = [v.T for v in (v0, v1, v2, p, x)]
    for i, value in enumerate(flipped):
        for at in range(tile_x):
            stacked[at, i * vectors : (i + 1) * vectors, :] = value[at * vectors : (at + 1) * vectors, :]
    t0, t1, t2, tp, tx = flipped
    pairs = (
        (t0, v0), (t0, v1), (t1, v1), (t1, v2), (t2, v2),
        (tx, v0), (tx, v1), (tx, v2),
        (t0, p), (t1, p), (t2, p),
        (tx, x), (tx, p), (tp, p),
    )
    same = row_ids((LANES, LANES)) // vectors == lane_ids((LANES, LANES)) // vectors
    group = lane_ids((vectors, LANES)) // vectors
    halves = [jnp.zeros((vectors, LANES), jnp.float32)] * 2
    for n, (a, b) in enumerate(pairs):
        product = jnp.dot(a, b, precision=highest, preferred_element_type=jnp.float32)
        product = jnp.where(same, product, 0.0)
        block = product[0:vectors]
        for at in range(1, tile_x):
            block = block + product[at * vectors : (at + 1) * vectors]
        block = fold(block, vectors)
        halves[n // tile_x] = jnp.where(group == n % tile_x, block, halves[n // tile_x])
    last = fold(jnp.sum(last, axis=0, keepdims=True), vectors)
    n = len(pairs)
    halves[n // tile_x] = jnp.where(group == n % tile_x, last, halves[n // tile_x])
    both = jnp.concatenate(halves, axis=1)
    for i in range(out.shape[0]):
        out[i] = both


def partial_kernel(received, out):
    total = jnp.sum(received[...], axis=0)
    for i in range(out.shape[0]):
        out[i] = total


def finish_kernel(cells, received, stacked, beta_ref, next_out, alpha_out, beta_out):
    vectors = beta_ref.shape[0]
    total = jnp.sum(received[...], axis=0)

    def block(n):
        return total[:, n * vectors : (n + 1) * vectors]

    def dot(a, b, dims=((1,), (0,))):
        return lax.dot_general(a, b, (dims, ((), ())), precision=highest, preferred_element_type=jnp.float32)

    shape = (vectors, vectors)
    eye = row_ids(shape) == lane_ids(shape)
    s = [block(n) for n in range(5)]
    moments = [jnp.sum(jnp.where(eye, m, 0.0), axis=0, keepdims=True) for m in s]
    moments.append(block(14)[0:1])
    along = galerkin(moments)
    down = [jnp.sum(jnp.where(eye, v, 0.0), axis=1, keepdims=True) for v in along]
    xv = [block(5 + k) for k in range(3)]
    vp = [block(8 + k) for k in range(3)]
    xx, xp, pp = block(11), block(12), block(13)
    beta = beta_ref[...]
    last = ((1,), (1,))
    first = ((0,), (0,))
    xr = xv[0] * along[0] + xv[1] * along[1] + xv[2] * along[2] - dot(xp, beta, last)
    alpha = xr * (1.0 / cells)
    alpha_out[...] = alpha
    rr = None
    for k in range(3):
        for l in range(3):
            term = down[k] * along[l] * s[k + l]
            rr = term if rr is None else rr + term
    cross = dot(down[0] * vp[0] + down[1] * vp[1] + down[2] * vp[2], beta, last)
    rr = rr - cross - cross.T + dot(beta, dot(pp, beta, last))
    gram = rr * (1.0 / cells) - 2.0 * dot(alpha, alpha, first) + dot(
        alpha, dot(xx * (1.0 / cells), alpha), first
    )
    gram = 0.5 * (gram + gram.T)
    work = jnp.concatenate(
        [gram, eye.astype(jnp.float32), jnp.zeros((vectors, LANES - 2 * vectors), jnp.float32)], axis=1
    )
    down_id = row_ids(work.shape)
    for j in range(vectors):
        row = work[j : j + 1, :]
        scale = 1.0 / jnp.sqrt(row[:, j : j + 1])
        row = row * scale
        column = work[:, j : j + 1] * scale
        work = jnp.where(down_id > j, work - column * row, jnp.where(down_id == j, row, work))
    beta_out[...] = jnp.where(row_ids(shape) <= lane_ids(shape), work[:, 0:vectors], 0.0)
    inverse = work[:, vectors : 2 * vectors]
    mix = jnp.concatenate(
        [inverse * v for v in along] + [-dot(inverse, beta), -dot(inverse, alpha, last)], axis=1
    )
    for at in range(stacked.shape[0]):
        next_out[:, at, :] = dot(mix, stacked[at])


def shards(
    lanczos_block,
    previous_block,
    previous_beta,
    prior_reaction,
    vert_coupling,
    horiz_coupling,
    friction,
    base_velocity,
    layers,
    obs_dest,
    obs_cell,
    obs_weight,
):
    vectors, tile_x, tile_y = lanczos_block.shape
    layer_count = horiz_coupling.shape[0]
    obs_rows = obs_cell.shape[0]
    size_x, size_y = lax.axis_size("mx"), lax.axis_size("my")
    devices = size_x * size_y
    cells = tile_x * tile_y * devices
    at_x, at_y = lax.axis_index("mx"), lax.axis_index("my")
    flags = jnp.stack([at_x > 0, at_x + 1 < size_x]).astype(jnp.float32)
    low_flag = (at_y > 0).astype(jnp.float32)
    high_flag = (at_y + 1 < size_y).astype(jnp.float32)
    forward_y = [(i, (i + 1) % size_y) for i in range(size_y)]
    backward_y = [(i, (i - 1) % size_y) for i in range(size_y)]
    forward_x = [(i, (i + 1) % size_x) for i in range(size_x)]
    backward_x = [(i, (i - 1) % size_x) for i in range(size_x)]
    f32 = jnp.float32
    rows = tile_y + 2 * HALO
    tiles = -(-(vectors * tile_x + FIELDS * tile_x) // LANES)
    smem = pl.BlockSpec(memory_space=pltpu.SMEM)
    vmem = pl.BlockSpec(memory_space=pltpu.VMEM)

    def shape(*dims):
        return jax.ShapeDtypeStruct(dims, f32)

    packed, previous, low, high = pl.pallas_call(
        pack_kernel,
        out_shape=(
            shape(tiles, tile_y, LANES), shape(tile_y, LANES), shape(tiles, HALO, LANES), shape(tiles, HALO, LANES)
        ),
        scratch_shapes=[pltpu.VMEM((tiles * LANES, tile_y), f32)],
        compiler_params=params(),
        name="pack",
    )(
        lanczos_block, previous_block, prior_reaction, vert_coupling, horiz_coupling,
        friction, base_velocity, layers,
    )
    table = pl.pallas_call(
        table_kernel, out_shape=shape(devices, LANES), compiler_params=params(), name="table"
    )(obs_dest, obs_cell.reshape(obs_rows, 1), obs_weight)

    from_low = lax.ppermute(high, "my", forward_y)
    from_high = lax.ppermute(low, "my", backward_y)
    own = jnp.concatenate([from_low * low_flag, packed, from_high * high_flag], axis=1)
    left = lax.ppermute(own, "mx", forward_x)
    right = lax.ppermute(own, "mx", backward_x)

    count = rows // 8
    groups = -(-FIELDS // 4)

    def blocked(*dims):
        return pltpu.VMEM((*dims, 8, LANES), f32)

    message, basis, fields = pl.pallas_call(
        functools.partial(moment_kernel, vectors),
        out_shape=(
            shape(devices, LANES), shape(3, count, 3, 8, LANES), shape(groups, count, 8, LANES)
        ),
        in_specs=[smem, vmem, vmem, vmem, vmem],
        scratch_shapes=[blocked(3, tiles, count), blocked(count, 3)] + [blocked(count + 2, 5)] * 3,
        compiler_params=params(),
        name="moments",
    )(flags, own, left, right, table)
    message = lax.all_to_all(message, AXES, split_axis=0, concat_axis=0, tiled=True)

    def columns(width):
        return [
            pltpu.VMEM((4, groups, count, 8, width * LANES), f32),
            blocked(layer_count, count, width),
            blocked(2, layer_count, count + 2, width + 2),
            blocked(2, layer_count, count + 2, width + 2),
            blocked(2, count, width),
        ]

    misfit, low, high = pl.pallas_call(
        functools.partial(velocity_kernel, vectors),
        out_shape=(shape(2, tile_y, LANES), shape(2, HALO, LANES), shape(2, HALO, LANES)),
        in_specs=[smem] + [vmem] * 3,
        scratch_shapes=columns(2) + [blocked(2, count), pltpu.VMEM((rows, LANES), f32)],
        compiler_params=params(),
        name="velocity",
    )(flags, message, basis, fields)

    from_low = lax.ppermute(high, "my", forward_y)
    from_high = lax.ppermute(low, "my", backward_y)
    misfit = jnp.concatenate([from_low * low_flag, misfit, from_high * high_flag], axis=1)
    misfit_left = lax.ppermute(misfit, "mx", forward_x)
    misfit_right = lax.ppermute(misfit, "mx", backward_x)

    products, stacked = pl.pallas_call(
        functools.partial(adjoint_kernel, vectors),
        out_shape=(shape(size_x, vectors, 2 * LANES), shape(tile_x, 5 * vectors, tile_y)),
        in_specs=[smem] + [vmem] * 6,
        scratch_shapes=columns(3)
        + [blocked(layer_count, count, 3), blocked(2, 3, count), blocked(2, count, 3), blocked(count, 3)]
        + [blocked(count + 2, 5)] * 3
        + [blocked(count), pltpu.VMEM((rows, LANES), f32)],
        compiler_params=params(),
        name="adjoint",
    )(flags, fields, misfit, misfit_left, misfit_right, basis, previous)

    products = lax.all_to_all(products, "mx", split_axis=0, concat_axis=0, tiled=True)
    products = pl.pallas_call(
        partial_kernel,
        out_shape=shape(size_y, vectors, 2 * LANES),
        compiler_params=params(),
        name="partial",
    )(products)
    products = lax.all_to_all(products, "my", split_axis=0, concat_axis=0, tiled=True)
    return pl.pallas_call(
        functools.partial(finish_kernel, float(cells)),
        out_shape=(shape(vectors, tile_x, tile_y), shape(vectors, vectors), shape(vectors, vectors)),
        compiler_params=params(),
        name="finish",
    )(products, stacked, previous_beta)


def solution(mesh):
    in_specs = (
        P(None, "mx", "my"),
        P(None, "mx", "my"),
        P(),
        P("mx", "my"),
        P(None, "mx", "my"),
        P(None, "mx", "my"),
        P("mx", "my"),
        P(None, "mx", "my"),
        P("mx", "my"),
        P(("mx", "my"), None),
        P(("mx", "my")),
        P(("mx", "my"), None),
    )
    out_specs = (P(None, "mx", "my"), P(), P())
    return jax.shard_map(shards, mesh=mesh, in_specs=in_specs, out_specs=out_specs, check_vma=False)
```

```python
import functools

import jax
import jax.numpy as jnp
from jax import lax
from jax.experimental import pallas as pl
from jax.experimental.pallas import tpu as pltpu
from jax.sharding import PartitionSpec as P

base_damping = 0.02
highest = lax.Precision.HIGHEST
SHIFT = 4.25
SCALE = 4.25
LANES = 128
HALO = 8
AXES = ("mx", "my")
VMEM_LIMIT = 56 * 1024 * 1024

F_RATIO = 0
F_PIVOT = 15
F_INV_LAT = 31
F_TOP = 32
F_LAYER = 33
F_BED = 34
F_REACT = 36
FIELDS = 37


def params():
    return pltpu.CompilerParams(vmem_limit_bytes=VMEM_LIMIT)


def lane_ids(shape):
    return lax.broadcasted_iota(jnp.int32, shape, len(shape) - 1)


def row_ids(shape):
    return lax.broadcasted_iota(jnp.int32, shape, len(shape) - 2)


def pack_kernel(
    block, previous, reaction, vert, horiz, friction, velocity, layers, out, prev_out, low, high, rows
):
    vectors, tile_x, tile_y = block.shape
    layer_count = horiz.shape[0]
    depth = layers[...]
    active = [(depth > k).astype(jnp.float32) for k in range(layer_count)]
    zero = jnp.zeros((tile_x, tile_y), jnp.float32)
    up = [vert[k] * active[k + 1] for k in range(layer_count - 1)] + [zero]
    lateral = [horiz[k] * active[k] for k in range(layer_count)]
    pivots = []
    for k in range(layer_count):
        drag = friction[...] if k == 0 else up[k - 1]
        diagonal = (base_damping + lateral[k] + drag + up[k]) * active[k] + (1.0 - active[k])
        if k > 0:
            diagonal = diagonal - up[k - 1] * up[k - 1] / pivots[k - 1]
        pivots.append(diagonal)
    top = zero
    for b in range(vectors):
        rows[pl.ds(b, tile_x, stride=vectors), :] = block[b]

    def put(field, value):
        rows[pl.ds(vectors * tile_x + field * tile_x, tile_x), :] = value

    for k in range(layer_count):
        put(F_PIVOT + k, lateral[k] * lateral[k] / pivots[k])
        is_top = depth == k + 1
        top = jnp.where(is_top, lateral[k] / pivots[k], top)
        if k + 1 < layer_count:
            below = jnp.where(depth > k + 1, lateral[k + 1], 1.0)
            put(F_RATIO + k, up[k] * lateral[k] / (pivots[k] * below))
    put(F_INV_LAT, 1.0 / lateral[0])
    put(F_TOP, top)
    put(F_LAYER, depth.astype(jnp.float32))
    put(F_BED, friction[...] * velocity[0])
    put(F_BED + 1, friction[...] * velocity[1])
    put(F_REACT, reaction[...])
    used = vectors * tile_x + FIELDS * tile_x
    rows[used:, :] = jnp.zeros((rows.shape[0] - used, tile_y), jnp.float32)
    for t in range(rows.shape[0] // LANES):
        out[t] = rows[t * LANES : (t + 1) * LANES, :].T
    low[...] = out[:, 0:HALO, :]
    high[...] = out[:, tile_y - HALO : tile_y, :]
    for b in range(vectors):
        rows[pl.ds(b, tile_x, stride=vectors), :] = previous[b]
    prev_out[...] = rows[0:LANES, :].T


def table_kernel(dest, cell, weight, out):
    count = dest.shape[1]
    devices = out.shape[0]
    rows = jnp.concatenate(
        [
            dest[...].astype(jnp.float32),
            cell[...].astype(jnp.float32),
            weight[...],
            jnp.zeros((4, count), jnp.float32),
        ],
        axis=0,
    )
    columns = rows.T
    target = columns[:, 0:1].astype(jnp.int32)
    onehot = target == lane_ids((count, devices))
    lower = row_ids((count, count)) >= lane_ids((count, count))
    running = jnp.dot(
        lower.astype(jnp.float32).astype(jnp.bfloat16),
        onehot.astype(jnp.float32).astype(jnp.bfloat16),
        preferred_element_type=jnp.float32,
    )
    chosen = onehot.astype(jnp.float32)
    rank = jnp.sum(running * chosen, axis=1, keepdims=True).astype(jnp.int32) - 1
    lane = lane_ids((count, LANES))
    kind = lane // 4
    value = jnp.where(
        kind == 0,
        columns[:, 2:3],
        jnp.where(kind == 1, columns[:, 3:4], jnp.where(kind == 2, columns[:, 1:2], 0.0)),
    )
    value = jnp.where(lane % 4 == rank, value, 0.0)
    chosen = (row_ids((devices, count)) == dest[...]).astype(jnp.float32).astype(jnp.bfloat16)
    out[...] = select_sum(chosen, value)


def select_sum(chosen, value):
    total = None
    for _ in range(3):
        piece = value.astype(jnp.bfloat16)
        value = value - piece.astype(jnp.float32)
        part = jnp.dot(chosen, piece, preferred_element_type=jnp.float32)
        total = part if total is None else total + part
    return total


def fold(row, stride):
    shift = LANES // 2
    while shift >= stride:
        row = row + pltpu.roll(row, shift, 1)
        shift //= 2
    return row


def gather(tile, index):
    return jnp.take_along_axis(tile, index, axis=1)


def pick(which, values):
    result = values[-1]
    for n in range(len(values) - 2, -1, -1):
        result = jnp.where(which == n, values[n], result)
    return result


def tile_rows(vectors, tiles, offset, tile):
    return offset + (lane_ids((8, LANES)) // vectors) * tiles + tile


def to_blocked(parts, vectors, tiles, offset):
    tile_x = LANES // vectors
    out = []
    for t in range(tiles):
        row = tile_rows(vectors, tiles, offset, t)
        index = (row % tile_x) * vectors + lane_ids((8, LANES)) % vectors
        out.append(pick(row // tile_x, [gather(part, index) for part in parts]))
    return out


def reblock(values, vectors, tiles, offset):
    out = []
    for t in range(tiles):
        row = tile_rows(vectors, tiles, offset, t)
        index = (row // len(values)) * vectors + lane_ids((8, LANES)) % vectors
        out.append(pick(row % len(values), [gather(value, index) for value in values]))
    return out


def to_own(values, vectors, offset):
    tiles = len(values)
    row = lane_ids((8, LANES)) // vectors + LANES // vectors - offset
    index = (row // tiles) * vectors + lane_ids((8, LANES)) % vectors
    return pick(row % tiles, [gather(value, index) for value in values])


def split_rows(source, target, flag=None):
    count = target.shape[-3]
    for i in range(count):
        value = source[pl.ds(i, 8, stride=count), :]
        target[i] = value if flag is None else value * flag


def join_rows(source, target):
    count = source.shape[0]
    for i in range(count):
        target[pl.ds(i, 8, stride=count), :] = source[i]


def put_tile(field, at, t, tiles, stride, value):
    field[(*at, t + 1)] = value
    if t == 0:
        field[(*at, tiles + 1)] = pltpu.roll(value, LANES - stride, 1)
    if t == tiles - 1:
        field[(*at, 0)] = pltpu.roll(value, stride, 1)


def lateral_sum(field, at, i, t):
    return (field[(*at, i, t + 1)] + field[(*at, i + 2, t + 1)]) + (
        field[(*at, i + 1, t)] + field[(*at, i + 1, t + 2)]
    )


def wrap_rows(field, at, count, tiles):
    for t in range(1, tiles + 1):
        field[(*at, 0, t)] = pltpu.roll(field[(*at, count, t)], 1, 0)
        field[(*at, count + 1, t)] = pltpu.roll(field[(*at, 1, t)], 7, 0)


def wrap_layers(field, tiles):
    count = field.shape[2] - 2

    def body(k, carry):
        for c in range(2):
            wrap_rows(field, (c, k), count, tiles)
        return carry

    lax.fori_loop(0, field.shape[1], body, 0, unroll=4)


def own_cells(vectors, tiles, offset, count, tile_y, i, t):
    tile_x = LANES // vectors
    row = tile_rows(vectors, tiles, offset, t)
    column = row_ids((8, LANES)) * count + i
    return (row >= tile_x) & (row < 2 * tile_x) & (column >= HALO) & (column < HALO + tile_y)


def shifted_prior(field, i, t, reaction):
    image = (reaction - (SHIFT - 4.0)) * field[i + 1, t + 1] - lateral_sum(field, (), i, t)
    return jnp.where(reaction > 0.0, image * (1.0 / SCALE), 0.0)


def krylov(first, second, third, reaction, vectors, count, tile_y):
    tiles = reaction.shape[1]

    def step(source, target):
        wrap_rows(source, (), count, tiles)
        for i in range(count):
            for t in range(tiles):
                value = shifted_prior(source, i, t, reaction[i, t])
                put_tile(target, (i + 1,), t, tiles, vectors, value)

    step(first, second)
    step(second, third)
    wrap_rows(third, (), count, tiles)
    total = jnp.zeros((8, LANES), jnp.float32)
    for i in range(count):
        for t in range(tiles):
            value = shifted_prior(third, i, t, reaction[i, t]) * third[i + 1, t + 1]
            total = total + jnp.where(own_cells(vectors, tiles, 0, count, tile_y, i, t), value, 0.0)
    return total


def moment_kernel(
    vectors, flags, own, left, right, table, out, basis, fields, parts, reaction, v0, v1, v2
):
    tile_x = LANES // vectors
    rows = own.shape[1]
    count = rows // 8
    tile_y = rows - 2 * HALO
    for p, (ref, flag) in enumerate(((left, flags[0]), (own, None), (right, flags[1]))):
        for t in range(own.shape[0]):
            split_rows(ref.at[t], parts.at[p, t], flag)
    lane = lane_ids((8, LANES))

    def arrange(i, carry):
        for t, value in enumerate(to_blocked([parts[p, 0, i] for p in range(3)], vectors, 3, 0)):
            put_tile(v0, (i + 1,), t, 3, vectors, value)
        for q in range(fields.shape[0]):
            per_tile = LANES // (4 * tile_x)
            index = (q % per_tile) * 4 * tile_x + (lane // 32) * tile_x + lane % tile_x
            fields[q, i] = pick(
                (lane % 32) // tile_x, [gather(parts[p, 1 + q // per_tile, i], index) for p in range(3)]
            )
        for t in range(3):
            reaction[i, t] = expand(fields, F_REACT, i, t, 3, 0, vectors)
        return carry

    lax.fori_loop(0, count, arrange, 0, unroll=3)
    last = krylov(v0, v1, v2, reaction, vectors, count, tile_y)
    sums = [jnp.zeros((8, LANES), jnp.float32) for _ in range(5)]
    for i in range(count):
        for t in range(3):
            mine = own_cells(vectors, 3, 0, count, tile_y, i, t)
            a, b, c = v0[i + 1, t + 1], v1[i + 1, t + 1], v2[i + 1, t + 1]
            basis[0, i, t] = a
            basis[1, i, t] = b
            basis[2, i, t] = c
            a, b, c = [jnp.where(mine, v, 0.0) for v in (a, b, c)]
            sums = [
                total + one * two
                for total, one, two in zip(sums, (a, a, b, b, c), (a, b, b, c, c))
            ]
    sums.append(last)
    group = lane_ids((1, LANES)) // vectors
    message = jnp.zeros((1, LANES), jnp.float32)
    for j, value in enumerate(sums):
        total = fold(jnp.sum(value, axis=0, keepdims=True), vectors)
        message = jnp.where(group == j + 1, total, message)
    out[...] = table[...] + message


def expand(fields, field, i, t, tiles, offset, vectors):
    index = (field % 4) * 32 + tile_rows(vectors, tiles, offset, t)
    return gather(fields[field // 4, i], index)


def galerkin(moments):
    m = moments
    a = [SHIFT * m[i] + SCALE * m[i + 1] for i in range(5)]

    def over(top, pivot):
        return jnp.where(pivot > 0.0, top / jnp.where(pivot > 0.0, pivot, 1.0), 0.0)

    l10, l20 = over(a[1], a[0]), over(a[2], a[0])
    d1 = a[2] - l10 * a[1]
    e12 = a[3] - l20 * a[1]
    l21 = over(e12, d1)
    d2 = a[4] - l20 * a[2] - l21 * e12
    z1 = m[1] - l10 * m[0]
    z2 = m[2] - l20 * m[0] - l21 * z1
    y2 = over(z2, d2)
    y1 = over(z1, d1) - l21 * y2
    y0 = over(m[0], a[0]) - l10 * y1 - l20 * y2
    return y0, y1, y2


def expand_all(fields, wide, vectors, offset):
    groups, count = fields.shape[:2]
    value = fields[...].reshape(groups * count * 8, LANES)
    high = value.astype(jnp.bfloat16)
    value = value - high.astype(jnp.float32)
    middle = value.astype(jnp.bfloat16)
    low = (value - middle.astype(jnp.float32)).astype(jnp.bfloat16)
    both = jnp.concatenate([high, middle], axis=1)
    lanes = wide.shape[-1]
    shape = (2 * LANES, lanes)
    column = lane_ids(shape)
    row = offset + (column % LANES // vectors) * (lanes // LANES) + column // LANES
    source = row_ids(shape) % LANES
    for j in range(4):
        chosen = (source == j * 32 + row).astype(jnp.float32).astype(jnp.bfloat16)
        out = jnp.dot(both, chosen, preferred_element_type=jnp.float32)
        out = out + jnp.dot(low, chosen[:LANES], preferred_element_type=jnp.float32)
        wide[j] = out.reshape(groups, count, 8, lanes)


def get_field(wide, field, i, t):
    return wide[field % 4, field // 4, i, :, t * LANES : (t + 1) * LANES]


def prepare_row(wide, i, bed_col, top_col, layer_count, tiles):
    across = range(tiles)
    get = functools.partial(get_field, wide, i=i)
    inv_lat = [get(F_INV_LAT, t=t) for t in across]
    top = [get(F_TOP, t=t) for t in across]
    depth = [get(F_LAYER, t=t) for t in across]
    forward = [inv_lat]
    for k in range(1, layer_count):
        forward.append([get(F_RATIO + k - 1, t=t) * forward[k - 1][t] for t in across])
    beds, tops = [None] * layer_count, [None] * layer_count
    for k in range(layer_count - 1, -1, -1):
        beds[k], tops[k] = [], []
        for t in across:
            bed = get(F_PIVOT + k, t=t) * forward[k][t]
            below = 0.0
            if k + 1 < layer_count:
                ratio = get(F_RATIO + k, t=t)
                bed = bed + ratio * beds[k + 1][t]
                below = ratio * tops[k + 1][t]
            surf = jnp.where(depth[t] == float(k + 1), top[t], below)
            if bed_col is not None:
                bed_col[k, i, t] = bed
            top_col[k, i, t] = surf
            beds[k].append(bed)
            tops[k].append(surf)
    return inv_lat, beds, tops


def put_outer(field, i, columns, values, stride):
    tiles = len(values[0])
    right = [pltpu.roll(v[0], LANES - stride, 1) for v in values]
    left = [pltpu.roll(v[tiles - 1], stride, 1) for v in values]
    for k, column in enumerate(columns):
        right_column = pltpu.roll(column[0], LANES - stride, 1)
        left_column = pltpu.roll(column[tiles - 1], stride, 1)
        for c, value in enumerate(values):
            field[c, k, i + 1, 0] = left_column * left[c]
            for t in range(tiles):
                field[c, k, i + 1, t + 1] = column[t] * value[t]
            field[c, k, i + 1, tiles + 1] = right_column * right[c]


def sweep(source, target, wide, stride, bed_source=None, top_col=None, top_source=None):
    layer_count, count, tiles = target.shape[1], target.shape[2] - 2, target.shape[3] - 2
    def body(i, carry):
        for t in range(tiles):
            carried = [[], []]
            for k in range(layer_count):
                for c in range(2):
                    value = lateral_sum(source, (c, k), i, t)
                    if k > 0:
                        value = value + get_field(wide, F_RATIO + k - 1, i, t) * carried[c][k - 1]
                    elif bed_source is not None:
                        value = value + bed_source[c, i, t]
                    carried[c].append(value)
            solved = [None, None]
            for k in range(layer_count - 1, -1, -1):
                for c in range(2):
                    value = get_field(wide, F_PIVOT + k, i, t) * carried[c][k]
                    if k + 1 < layer_count:
                        value = value + get_field(wide, F_RATIO + k, i, t) * solved[c]
                    solved[c] = value
                    if top_source is not None:
                        value = value + top_col[k, i, t] * top_source[c, i, t]
                    put_tile(target, (c, k, i + 1), t, tiles, stride, value)
        return carry

    lax.fori_loop(0, count, body, 0, unroll=6)
    wrap_layers(target, tiles)


def velocity_kernel(
    vectors, flags, message, basis, fields,
    misfit, low, high,
    wide, top_col, one, two, source, surface, flat,
):
    tile_x = LANES // vectors
    layer_count, count, tiles = top_col.shape[:3]
    tile_y = count * 8 - 2 * HALO
    offset = tile_x // 2
    group = lane_ids((8, LANES)) // vectors
    summed = jnp.broadcast_to(jnp.sum(message[...], axis=0, keepdims=True), (8, LANES))
    moments = [fold(jnp.where(group == j + 1, summed, 0.0), vectors) for j in range(6)]
    y = galerkin(moments)

    def prepare(i, carry):
        smooth = [y[0] * basis[0, i, t] + y[1] * basis[1, i, t] + y[2] * basis[2, i, t] for t in range(3)]
        smooth = reblock(smooth, vectors, tiles, offset)
        inv_lat, beds, _ = prepare_row(wide, i, None, top_col, layer_count, tiles)
        values = [
            [get_field(wide, F_BED + c, i, t) * smooth[t] for t in range(tiles)] for c in range(2)
        ]
        for c in range(2):
            for t in range(tiles):
                source[c, i, t] = values[c][t] * inv_lat[t]
        put_outer(one, i, beds, values, vectors)
        return carry

    expand_all(fields, wide, vectors, offset)

    lax.fori_loop(0, count, prepare, 0, unroll=6)
    wrap_layers(one, tiles)
    sweep(one, two, wide, vectors, bed_source=source)
    sweep(two, one, wide, vectors, bed_source=source)

    def finish(i, carry):
        across = [(c, t) for c in range(2) for t in range(tiles)]
        values = {(c, t): top_col[0, i, t] * source[c, i, t] for c, t in across}
        for k in range(layer_count):
            for c, t in across:
                values[c, t] = values[c, t] + top_col[k, i, t] * lateral_sum(one, (c, k), i, t)
        for c in range(2):
            surface[c, i] = to_own([values[c, t] for t in range(tiles)], vectors, offset)
        return carry

    lax.fori_loop(0, count, finish, 0, unroll=6)

    table = message[...]
    flipped = table.T
    lane = lane_ids((LANES, 2 * LANES))
    second = lane >= LANES
    at_row, at_lane = [], []
    for r in range(4):
        cell = flipped[8 + r : 9 + r, :].astype(jnp.int32)
        at_row.append((row_ids((tile_y, LANES)) == cell % tile_y).astype(jnp.float32))
        cell = table[:, 8 + r : 9 + r].astype(jnp.int32)
        weight = jnp.where(second, table[:, 4 + r : 5 + r], table[:, r : r + 1])
        at_lane.append(jnp.where(cell // tile_y == lane % LANES // vectors, weight, 0.0))
    weights = select_sum(
        jnp.concatenate(at_row, axis=1).astype(jnp.bfloat16), jnp.concatenate(at_lane, axis=0)
    )
    for c in range(2):
        join_rows(surface.at[c], flat)
        misfit[c] = weights[:, c * LANES : (c + 1) * LANES] * flat[HALO : HALO + tile_y, :]
    low[...] = misfit[:, 0:HALO, :]
    high[...] = misfit[:, tile_y - HALO :, :]


def adjoint_kernel(
    vectors, flags, fields, misfit, misfit_left, misfit_right, basis, previous,
    out, stacked,
    wide, top_col, one, two, source, bed_col, sides, bed, reaction, v0, v1, v2, natural, flat,
):
    tile_x = LANES // vectors
    layer_count, count, tiles = top_col.shape[:3]
    tile_y = count * 8 - 2 * HALO
    for c in range(2):
        split_rows(misfit_left.at[c], sides.at[c, 0], flags[0])
        split_rows(misfit.at[c], sides.at[c, 1])
        split_rows(misfit_right.at[c], sides.at[c, 2], flags[1])

    def prepare(i, carry):
        values = [to_blocked([sides[c, p, i] for p in range(3)], vectors, tiles, 0) for c in range(2)]
        inv_lat, _, tops = prepare_row(wide, i, bed_col, top_col, layer_count, tiles)
        for t in range(tiles):
            reaction[i, t] = get_field(wide, F_REACT, i, t)
            total = None
            for c in range(2):
                value = values[c][t]
                source[c, i, t] = value
                drag = get_field(wide, F_BED + c, i, t)
                bed[c, i, t] = drag
                total = drag * value if total is None else total + drag * value
            v1[i + 1, t + 1] = total * (tops[0][t] * inv_lat[t])
        put_outer(one, i, tops, values, vectors)
        return carry

    expand_all(fields, wide, vectors, 0)

    lax.fori_loop(0, count, prepare, 0, unroll=6)
    wrap_layers(one, tiles)
    sweep(one, two, wide, vectors, top_col=top_col, top_source=source)
    sweep(two, one, wide, vectors, top_col=top_col, top_source=source)

    def finish(i, carry):
        totals = {}
        for k in range(layer_count):
            for c in range(2):
                for t in range(tiles):
                    value = bed_col[k, i, t] * lateral_sum(one, (c, k), i, t)
                    totals[c, t] = value if k == 0 else totals[c, t] + value
        for t in range(tiles):
            value = v1[i + 1, t + 1] + (bed[0, i, t] * totals[0, t] + bed[1, i, t] * totals[1, t])
            put_tile(v0, (i + 1,), t, tiles, vectors, value)
        return carry

    lax.fori_loop(0, count, finish, 0, unroll=6)
    last = krylov(v0, v1, v2, reaction, vectors, count, tile_y)
    own = []
    for n, field in enumerate((v0, v1, v2, basis.at[0])):
        at = 0 if n == 3 else 1
        for i in range(count):
            natural[i] = to_own([field[i + at, t + at] for t in range(tiles)], vectors, 0)
        join_rows(natural, flat)
        own.append(flat[HALO : HALO + tile_y, :])
    v0, v1, v2, x = own
    p = previous[...]
    flipped = [v.T for v in (v0, v1, v2, p, x)]
    for i, value in enumerate(flipped):
        for at in range(tile_x):
            stacked[at, i * vectors : (i + 1) * vectors, :] = value[at * vectors : (at + 1) * vectors, :]
    t0, t1, t2, tp, tx = flipped
    pairs = (
        (t0, v0), (t0, v1), (t1, v1), (t1, v2), (t2, v2),
        (tx, v0), (tx, v1), (tx, v2),
        (t0, p), (t1, p), (t2, p),
        (tx, x), (tx, p), (tp, p),
    )
    same = row_ids((LANES, LANES)) // vectors == lane_ids((LANES, LANES)) // vectors
    group = lane_ids((vectors, LANES)) // vectors
    halves = [jnp.zeros((vectors, LANES), jnp.float32)] * 2
    for n, (a, b) in enumerate(pairs):
        product = jnp.dot(a, b, precision=highest, preferred_element_type=jnp.float32)
        product = jnp.where(same, product, 0.0)
        block = product[0:vectors]
        for at in range(1, tile_x):
            block = block + product[at * vectors : (at + 1) * vectors]
        block = fold(block, vectors)
        halves[n // tile_x] = jnp.where(group == n % tile_x, block, halves[n // tile_x])
    last = fold(jnp.sum(last, axis=0, keepdims=True), vectors)
    n = len(pairs)
    halves[n // tile_x] = jnp.where(group == n % tile_x, last, halves[n // tile_x])
    both = jnp.concatenate(halves, axis=1)
    for i in range(out.shape[0]):
        out[i] = both


def finish_kernel(cells, received, stacked, beta_ref, next_out, alpha_out, beta_out):
    vectors = beta_ref.shape[0]
    total = jnp.sum(received[...], axis=0)

    def block(n):
        return total[:, n * vectors : (n + 1) * vectors]

    def dot(a, b, dims=((1,), (0,))):
        return lax.dot_general(a, b, (dims, ((), ())), precision=highest, preferred_element_type=jnp.float32)

    shape = (vectors, vectors)
    eye = row_ids(shape) == lane_ids(shape)
    s = [block(n) for n in range(5)]
    moments = [jnp.sum(jnp.where(eye, m, 0.0), axis=0, keepdims=True) for m in s]
    moments.append(block(14)[0:1])
    along = galerkin(moments)
    down = [jnp.sum(jnp.where(eye, v, 0.0), axis=1, keepdims=True) for v in along]
    xv = [block(5 + k) for k in range(3)]
    vp = [block(8 + k) for k in range(3)]
    xx, xp, pp = block(11), block(12), block(13)
    beta = beta_ref[...]
    last = ((1,), (1,))
    first = ((0,), (0,))
    xr = xv[0] * along[0] + xv[1] * along[1] + xv[2] * along[2] - dot(xp, beta, last)
    alpha = xr * (1.0 / cells)
    alpha_out[...] = alpha
    rr = None
    for k in range(3):
        for l in range(3):
            term = down[k] * along[l] * s[k + l]
            rr = term if rr is None else rr + term
    cross = dot(down[0] * vp[0] + down[1] * vp[1] + down[2] * vp[2], beta, last)
    rr = rr - cross - cross.T + dot(beta, dot(pp, beta, last))
    gram = rr * (1.0 / cells) - 2.0 * dot(alpha, alpha, first) + dot(
        alpha, dot(xx * (1.0 / cells), alpha), first
    )
    gram = 0.5 * (gram + gram.T)
    work = jnp.concatenate(
        [gram, eye.astype(jnp.float32), jnp.zeros((vectors, LANES - 2 * vectors), jnp.float32)], axis=1
    )
    down_id = row_ids(work.shape)
    for j in range(vectors):
        row = work[j : j + 1, :]
        scale = 1.0 / jnp.sqrt(row[:, j : j + 1])
        row = row * scale
        column = work[:, j : j + 1] * scale
        work = jnp.where(down_id > j, work - column * row, jnp.where(down_id == j, row, work))
    beta_out[...] = jnp.where(row_ids(shape) <= lane_ids(shape), work[:, 0:vectors], 0.0)
    inverse = work[:, vectors : 2 * vectors]
    mix = jnp.concatenate(
        [inverse * v for v in along] + [-dot(inverse, beta), -dot(inverse, alpha, last)], axis=1
    )
    for at in range(stacked.shape[0]):
        next_out[:, at, :] = dot(mix, stacked[at])


def shards(
    lanczos_block,
    previous_block,
    previous_beta,
    prior_reaction,
    vert_coupling,
    horiz_coupling,
    friction,
    base_velocity,
    layers,
    obs_dest,
    obs_cell,
    obs_weight,
):
    vectors, tile_x, tile_y = lanczos_block.shape
    layer_count = horiz_coupling.shape[0]
    obs_rows = obs_cell.shape[0]
    size_x, size_y = lax.axis_size("mx"), lax.axis_size("my")
    devices = size_x * size_y
    cells = tile_x * tile_y * devices
    at_x, at_y = lax.axis_index("mx"), lax.axis_index("my")
    flags = jnp.stack([at_x > 0, at_x + 1 < size_x]).astype(jnp.float32)
    low_flag = (at_y > 0).astype(jnp.float32)
    high_flag = (at_y + 1 < size_y).astype(jnp.float32)
    forward_y = [(i, (i + 1) % size_y) for i in range(size_y)]
    backward_y = [(i, (i - 1) % size_y) for i in range(size_y)]
    forward_x = [(i, (i + 1) % size_x) for i in range(size_x)]
    backward_x = [(i, (i - 1) % size_x) for i in range(size_x)]
    f32 = jnp.float32
    rows = tile_y + 2 * HALO
    tiles = -(-(vectors * tile_x + FIELDS * tile_x) // LANES)
    smem = pl.BlockSpec(memory_space=pltpu.SMEM)
    vmem = pl.BlockSpec(memory_space=pltpu.VMEM)

    def shape(*dims):
        return jax.ShapeDtypeStruct(dims, f32)

    packed, previous, low, high = pl.pallas_call(
        pack_kernel,
        out_shape=(
            shape(tiles, tile_y, LANES), shape(tile_y, LANES), shape(tiles, HALO, LANES), shape(tiles, HALO, LANES)
        ),
        scratch_shapes=[pltpu.VMEM((tiles * LANES, tile_y), f32)],
        compiler_params=params(),
        name="pack",
    )(
        lanczos_block, previous_block, prior_reaction, vert_coupling, horiz_coupling,
        friction, base_velocity, layers,
    )
    table = pl.pallas_call(
        table_kernel, out_shape=shape(devices, LANES), compiler_params=params(), name="table"
    )(obs_dest.reshape(1, obs_rows), obs_cell.reshape(1, obs_rows), obs_weight.T)

    from_low = lax.ppermute(high, "my", forward_y)
    from_high = lax.ppermute(low, "my", backward_y)
    own = jnp.concatenate([from_low * low_flag, packed, from_high * high_flag], axis=1)
    left = lax.ppermute(own, "mx", forward_x)
    right = lax.ppermute(own, "mx", backward_x)

    count = rows // 8
    groups = -(-FIELDS // 4)

    def blocked(*dims):
        return pltpu.VMEM((*dims, 8, LANES), f32)

    message, basis, fields = pl.pallas_call(
        functools.partial(moment_kernel, vectors),
        out_shape=(
            shape(devices, LANES), shape(3, count, 3, 8, LANES), shape(groups, count, 8, LANES)
        ),
        in_specs=[smem, vmem, vmem, vmem, vmem],
        scratch_shapes=[blocked(3, tiles, count), blocked(count, 3)] + [blocked(count + 2, 5)] * 3,
        compiler_params=params(),
        name="moments",
    )(flags, own, left, right, table)
    message = lax.all_to_all(message, AXES, split_axis=0, concat_axis=0, tiled=True)

    def columns(width):
        return [
            pltpu.VMEM((4, groups, count, 8, width * LANES), f32),
            blocked(layer_count, count, width),
            blocked(2, layer_count, count + 2, width + 2),
            blocked(2, layer_count, count + 2, width + 2),
            blocked(2, count, width),
        ]

    misfit, low, high = pl.pallas_call(
        functools.partial(velocity_kernel, vectors),
        out_shape=(shape(2, tile_y, LANES), shape(2, HALO, LANES), shape(2, HALO, LANES)),
        in_specs=[smem] + [vmem] * 3,
        scratch_shapes=columns(2) + [blocked(2, count), pltpu.VMEM((rows, LANES), f32)],
        compiler_params=params(),
        name="velocity",
    )(flags, message, basis, fields)

    from_low = lax.ppermute(high, "my", forward_y)
    from_high = lax.ppermute(low, "my", backward_y)
    misfit = jnp.concatenate([from_low * low_flag, misfit, from_high * high_flag], axis=1)
    misfit_left = lax.ppermute(misfit, "mx", forward_x)
    misfit_right = lax.ppermute(misfit, "mx", backward_x)

    products, stacked = pl.pallas_call(
        functools.partial(adjoint_kernel, vectors),
        out_shape=(shape(size_x, vectors, 2 * LANES), shape(tile_x, 5 * vectors, tile_y)),
        in_specs=[smem] + [vmem] * 6,
        scratch_shapes=columns(3)
        + [blocked(layer_count, count, 3), blocked(2, 3, count), blocked(2, count, 3), blocked(count, 3)]
        + [blocked(count + 2, 5)] * 3
        + [blocked(count), pltpu.VMEM((rows, LANES), f32)],
        compiler_params=params(),
        name="adjoint",
    )(flags, fields, misfit, misfit_left, misfit_right, basis, previous)

    products = lax.all_to_all(products, "mx", split_axis=0, concat_axis=0, tiled=True)
    products = jnp.broadcast_to(jnp.sum(products, axis=0)[None], (size_y, vectors, 2 * LANES))
    products = lax.all_to_all(products, "my", split_axis=0, concat_axis=0, tiled=True)
    return pl.pallas_call(
        functools.partial(finish_kernel, float(cells)),
        out_shape=(shape(vectors, tile_x, tile_y), shape(vectors, vectors), shape(vectors, vectors)),
        compiler_params=params(),
        name="finish",
    )(products, stacked, previous_beta)


def solution(mesh):
    in_specs = (
        P(None, "mx", "my"),
        P(None, "mx", "my"),
        P(),
        P("mx", "my"),
        P(None, "mx", "my"),
        P(None, "mx", "my"),
        P("mx", "my"),
        P(None, "mx", "my"),
        P("mx", "my"),
        P(("mx", "my"), None),
        P(("mx", "my")),
        P(("mx", "my"), None),
    )
    out_specs = (P(None, "mx", "my"), P(), P())
    return jax.shard_map(shards, mesh=mesh, in_specs=in_specs, out_specs=out_specs, check_vma=False)
```

```python
import functools

import jax
import jax.numpy as jnp
from jax import lax
from jax.experimental import pallas as pl
from jax.experimental.pallas import tpu as pltpu
from jax.sharding import PartitionSpec as P

base_damping = 0.02
highest = lax.Precision.HIGHEST
SHIFT = 4.25
SCALE = 4.25
LANES = 128
HALO = 8
AXES = ("mx", "my")
VMEM_LIMIT = 56 * 1024 * 1024

F_RATIO = 0
F_PIVOT = 15
F_INV_LAT = 31
F_TOP = 32
F_LAYER = 33
F_BED = 34
F_REACT = 36
FIELDS = 37


def params():
    return pltpu.CompilerParams(vmem_limit_bytes=VMEM_LIMIT)


def lane_ids(shape):
    return lax.broadcasted_iota(jnp.int32, shape, len(shape) - 1)


def row_ids(shape):
    return lax.broadcasted_iota(jnp.int32, shape, len(shape) - 2)


def pack_kernel(
    block, previous, reaction, vert, horiz, friction, velocity, layers, out, prev_out, low, high, rows
):
    vectors, tile_x, tile_y = block.shape
    layer_count = horiz.shape[0]
    depth = layers[...]
    active = [(depth > k).astype(jnp.float32) for k in range(layer_count)]
    zero = jnp.zeros((tile_x, tile_y), jnp.float32)
    up = [vert[k] * active[k + 1] for k in range(layer_count - 1)] + [zero]
    lateral = [horiz[k] * active[k] for k in range(layer_count)]
    pivots = []
    for k in range(layer_count):
        drag = friction[...] if k == 0 else up[k - 1]
        diagonal = (base_damping + lateral[k] + drag + up[k]) * active[k] + (1.0 - active[k])
        if k > 0:
            diagonal = diagonal - up[k - 1] * up[k - 1] / pivots[k - 1]
        pivots.append(diagonal)
    top = zero
    for b in range(vectors):
        rows[pl.ds(b, tile_x, stride=vectors), :] = block[b]

    def put(field, value):
        rows[pl.ds(vectors * tile_x + field * tile_x, tile_x), :] = value

    for k in range(layer_count):
        put(F_PIVOT + k, lateral[k] * lateral[k] / pivots[k])
        is_top = depth == k + 1
        top = jnp.where(is_top, lateral[k] / pivots[k], top)
        if k + 1 < layer_count:
            below = jnp.where(depth > k + 1, lateral[k + 1], 1.0)
            put(F_RATIO + k, up[k] * lateral[k] / (pivots[k] * below))
    put(F_INV_LAT, 1.0 / lateral[0])
    put(F_TOP, top)
    put(F_LAYER, depth.astype(jnp.float32))
    put(F_BED, friction[...] * velocity[0])
    put(F_BED + 1, friction[...] * velocity[1])
    put(F_REACT, reaction[...])
    used = vectors * tile_x + FIELDS * tile_x
    rows[used:, :] = jnp.zeros((rows.shape[0] - used, tile_y), jnp.float32)
    for t in range(rows.shape[0] // LANES):
        out[t] = rows[t * LANES : (t + 1) * LANES, :].T
    low[...] = out[:, 0:HALO, :]
    high[...] = out[:, tile_y - HALO : tile_y, :]
    for b in range(vectors):
        rows[pl.ds(b, tile_x, stride=vectors), :] = previous[b]
    prev_out[...] = rows[0:LANES, :].T


def table_kernel(dest, cell, weight, out):
    count = dest.shape[1]
    devices = out.shape[0]
    rows = jnp.concatenate(
        [
            dest[...].astype(jnp.float32),
            cell[...].astype(jnp.float32),
            weight[...],
            jnp.zeros((4, count), jnp.float32),
        ],
        axis=0,
    )
    columns = rows.T
    target = columns[:, 0:1].astype(jnp.int32)
    onehot = target == lane_ids((count, devices))
    lower = row_ids((count, count)) >= lane_ids((count, count))
    running = jnp.dot(
        lower.astype(jnp.float32).astype(jnp.bfloat16),
        onehot.astype(jnp.float32).astype(jnp.bfloat16),
        preferred_element_type=jnp.float32,
    )
    chosen = onehot.astype(jnp.float32)
    rank = jnp.sum(running * chosen, axis=1, keepdims=True).astype(jnp.int32) - 1
    lane = lane_ids((count, LANES))
    kind = lane // 4
    value = jnp.where(
        kind == 0,
        columns[:, 2:3],
        jnp.where(kind == 1, columns[:, 3:4], jnp.where(kind == 2, columns[:, 1:2], 0.0)),
    )
    value = jnp.where(lane % 4 == rank, value, 0.0)
    chosen = (row_ids((devices, count)) == dest[...]).astype(jnp.float32).astype(jnp.bfloat16)
    out[...] = select_sum(chosen, value)


def pieces(value, axis):
    parts = []
    for _ in range(3):
        piece = value.astype(jnp.bfloat16)
        value = value - piece.astype(jnp.float32)
        parts.append(piece)
    return jnp.concatenate(parts, axis=axis)


def thrice(chosen):
    chosen = chosen.astype(jnp.float32).astype(jnp.bfloat16)
    return jnp.concatenate([chosen] * 3, axis=0)


def select_sum(chosen, value):
    total = None
    for _ in range(3):
        piece = value.astype(jnp.bfloat16)
        value = value - piece.astype(jnp.float32)
        part = jnp.dot(chosen, piece, preferred_element_type=jnp.float32)
        total = part if total is None else total + part
    return total


def fold(row, stride):
    shift = LANES // 2
    while shift >= stride:
        row = row + pltpu.roll(row, shift, 1)
        shift //= 2
    return row


def gather(tile, index):
    return jnp.take_along_axis(tile, index, axis=1)


def pick(which, values):
    result = values[-1]
    for n in range(len(values) - 2, -1, -1):
        result = jnp.where(which == n, values[n], result)
    return result


def tile_rows(vectors, tiles, offset, tile):
    return offset + (lane_ids((8, LANES)) // vectors) * tiles + tile


def to_blocked(value, vectors, tiles):
    shape = (3 * LANES, tiles * LANES)
    column, source = lane_ids(shape), row_ids(shape)
    row = (column % LANES // vectors) * tiles + column // LANES
    chosen = source == row * vectors + column % vectors
    return jnp.dot(pieces(value, 1), thrice(chosen), preferred_element_type=jnp.float32)


def reblock(values, vectors, tiles, offset):
    out = []
    for t in range(tiles):
        row = tile_rows(vectors, tiles, offset, t)
        index = (row // len(values)) * vectors + lane_ids((8, LANES)) % vectors
        out.append(pick(row % len(values), [gather(value, index) for value in values]))
    return out


def to_own(values, vectors, offset):
    tiles = len(values)
    row = lane_ids((8, LANES)) // vectors + LANES // vectors - offset
    index = (row // tiles) * vectors + lane_ids((8, LANES)) % vectors
    return pick(row % tiles, [gather(value, index) for value in values])


def split_rows(source, target, flag=None):
    count = target.shape[-3]
    for i in range(count):
        value = source[pl.ds(i, 8, stride=count), :]
        target[i] = value if flag is None else value * flag


def join_rows(source, target):
    count = source.shape[0]
    for i in range(count):
        target[pl.ds(i, 8, stride=count), :] = source[i]


def put_tile(field, at, t, tiles, stride, value):
    field[(*at, t + 1)] = value
    if t == 0:
        field[(*at, tiles + 1)] = pltpu.roll(value, LANES - stride, 1)
    if t == tiles - 1:
        field[(*at, 0)] = pltpu.roll(value, stride, 1)


def lateral_sum(field, at, i, t):
    return (field[(*at, i, t + 1)] + field[(*at, i + 2, t + 1)]) + (
        field[(*at, i + 1, t)] + field[(*at, i + 1, t + 2)]
    )


def wrap_rows(field, at, count, tiles):
    for t in range(1, tiles + 1):
        field[(*at, 0, t)] = pltpu.roll(field[(*at, count, t)], 1, 0)
        field[(*at, count + 1, t)] = pltpu.roll(field[(*at, 1, t)], 7, 0)


def wrap_layers(field, tiles):
    count = field.shape[2] - 2

    def body(k, carry):
        for c in range(2):
            wrap_rows(field, (c, k), count, tiles)
        return carry

    lax.fori_loop(0, field.shape[1], body, 0, unroll=4)


def own_cells(vectors, tiles, offset, count, tile_y, i, t):
    tile_x = LANES // vectors
    row = tile_rows(vectors, tiles, offset, t)
    column = row_ids((8, LANES)) * count + i
    return (row >= tile_x) & (row < 2 * tile_x) & (column >= HALO) & (column < HALO + tile_y)


def shifted_prior(field, i, t, reaction):
    image = (reaction - (SHIFT - 4.0)) * field[i + 1, t + 1] - lateral_sum(field, (), i, t)
    return jnp.where(reaction > 0.0, image * (1.0 / SCALE), 0.0)


def krylov(first, second, third, reaction, vectors, count, tile_y):
    tiles = reaction.shape[1]

    def step(source, target):
        wrap_rows(source, (), count, tiles)
        for i in range(count):
            for t in range(tiles):
                value = shifted_prior(source, i, t, reaction[i, t])
                put_tile(target, (i + 1,), t, tiles, vectors, value)

    step(first, second)
    step(second, third)
    wrap_rows(third, (), count, tiles)
    total = jnp.zeros((8, LANES), jnp.float32)
    for i in range(count):
        for t in range(tiles):
            value = shifted_prior(third, i, t, reaction[i, t]) * third[i + 1, t + 1]
            total = total + jnp.where(own_cells(vectors, tiles, 0, count, tile_y, i, t), value, 0.0)
    return total


def moment_kernel(
    vectors, flags, own, left, right, table, out, basis, fields, flat, parts, reaction, v0, v1, v2
):
    tile_x = LANES // vectors
    rows = own.shape[1]
    count = rows // 8
    tile_y = rows - 2 * HALO
    def beside(tiles):
        value = jnp.concatenate([left[tiles] * flags[0], own[tiles], right[tiles] * flags[1]], axis=-1)
        return value.reshape(-1, 3 * LANES)

    blocked = to_blocked(beside(0), vectors, 3)
    for t in range(3):
        flat[t] = blocked[:, t * LANES : (t + 1) * LANES]
    per_tile = LANES // (4 * tile_x)
    shape = (3 * LANES, per_tile * LANES)
    column, at = lane_ids(shape), row_ids(shape)
    lane = column % 32
    field = column // LANES * 4 + column % LANES // 32
    chosen = (at == lane // tile_x * LANES + field * tile_x + lane % tile_x) & (lane < 3 * tile_x)
    value = beside(slice(1, own.shape[0]))
    out_all = jnp.dot(pieces(value, 1), thrice(chosen), preferred_element_type=jnp.float32)
    for q in range(fields.shape[0]):
        first = q // per_tile * rows
        lanes = q % per_tile * LANES
        flat[3 + q] = out_all[first : first + rows, lanes : lanes + LANES]
    for t in range(3):
        split_rows(flat.at[t], parts.at[t])
    for q in range(fields.shape[0]):
        split_rows(flat.at[3 + q], fields.at[q])

    for i in range(count):
        for t in range(3):
            put_tile(v0, (i + 1,), t, 3, vectors, parts[t, i])
            reaction[i, t] = expand(fields, F_REACT, i, t, 3, 0, vectors)
    last = krylov(v0, v1, v2, reaction, vectors, count, tile_y)
    sums = [jnp.zeros((8, LANES), jnp.float32) for _ in range(5)]
    for i in range(count):
        for t in range(3):
            mine = own_cells(vectors, 3, 0, count, tile_y, i, t)
            a, b, c = v0[i + 1, t + 1], v1[i + 1, t + 1], v2[i + 1, t + 1]
            basis[0, i, t] = a
            basis[1, i, t] = b
            basis[2, i, t] = c
            a, b, c = [jnp.where(mine, v, 0.0) for v in (a, b, c)]
            sums = [
                total + one * two
                for total, one, two in zip(sums, (a, a, b, b, c), (a, b, b, c, c))
            ]
    sums.append(last)
    group = lane_ids((1, LANES)) // vectors
    message = jnp.zeros((1, LANES), jnp.float32)
    for j, value in enumerate(sums):
        total = fold(jnp.sum(value, axis=0, keepdims=True), vectors)
        message = jnp.where(group == j + 1, total, message)
    out[...] = table[...] + message


def expand(fields, field, i, t, tiles, offset, vectors):
    index = (field % 4) * 32 + tile_rows(vectors, tiles, offset, t)
    return gather(fields[field // 4, i], index)


def galerkin(moments):
    m = moments
    a = [SHIFT * m[i] + SCALE * m[i + 1] for i in range(5)]

    def over(top, pivot):
        return jnp.where(pivot > 0.0, top / jnp.where(pivot > 0.0, pivot, 1.0), 0.0)

    l10, l20 = over(a[1], a[0]), over(a[2], a[0])
    d1 = a[2] - l10 * a[1]
    e12 = a[3] - l20 * a[1]
    l21 = over(e12, d1)
    d2 = a[4] - l20 * a[2] - l21 * e12
    z1 = m[1] - l10 * m[0]
    z2 = m[2] - l20 * m[0] - l21 * z1
    y2 = over(z2, d2)
    y1 = over(z1, d1) - l21 * y2
    y0 = over(m[0], a[0]) - l10 * y1 - l20 * y2
    return y0, y1, y2


def expand_all(fields, wide, vectors, offset):
    groups, count = fields.shape[:2]
    value = pieces(fields[...].reshape(groups * count * 8, LANES), 1)
    half = wide.shape[-1] // 2
    tiles = half // (2 * LANES)
    shape = (LANES, half)
    column = lane_ids(shape)
    tile = column // LANES
    row = offset + (column % LANES // vectors) * tiles + tile % tiles
    for j in range(2):
        chosen = row_ids(shape) == (2 * j + tile // tiles) * 32 + row
        out = jnp.dot(value, thrice(chosen), preferred_element_type=jnp.float32)
        wide[:, :, :, j * half : (j + 1) * half] = out.reshape(groups, count, 8, half)


def get_field(wide, field, i, t):
    at = (field % 4) * (wide.shape[-1] // (4 * LANES)) + t
    return wide[field // 4, i, :, at * LANES : (at + 1) * LANES]


def prepare_row(wide, i, bed_col, top_col, layer_count, tiles):
    across = range(tiles)
    get = functools.partial(get_field, wide, i=i)
    inv_lat = [get(F_INV_LAT, t=t) for t in across]
    top = [get(F_TOP, t=t) for t in across]
    depth = [get(F_LAYER, t=t) for t in across]
    forward = [inv_lat]
    for k in range(1, layer_count):
        forward.append([get(F_RATIO + k - 1, t=t) * forward[k - 1][t] for t in across])
    beds, tops = [None] * layer_count, [None] * layer_count
    for k in range(layer_count - 1, -1, -1):
        beds[k], tops[k] = [], []
        for t in across:
            bed = get(F_PIVOT + k, t=t) * forward[k][t]
            below = 0.0
            if k + 1 < layer_count:
                ratio = get(F_RATIO + k, t=t)
                bed = bed + ratio * beds[k + 1][t]
                below = ratio * tops[k + 1][t]
            surf = jnp.where(depth[t] == float(k + 1), top[t], below)
            if bed_col is not None:
                bed_col[k, i, t] = bed
            top_col[k, i, t] = surf
            beds[k].append(bed)
            tops[k].append(surf)
    return inv_lat, beds, tops


def put_outer(field, i, columns, values, stride):
    tiles = len(values[0])
    right = [pltpu.roll(v[0], LANES - stride, 1) for v in values]
    left = [pltpu.roll(v[tiles - 1], stride, 1) for v in values]
    for k, column in enumerate(columns):
        right_column = pltpu.roll(column[0], LANES - stride, 1)
        left_column = pltpu.roll(column[tiles - 1], stride, 1)
        for c, value in enumerate(values):
            field[c, k, i + 1, 0] = left_column * left[c]
            for t in range(tiles):
                field[c, k, i + 1, t + 1] = column[t] * value[t]
            field[c, k, i + 1, tiles + 1] = right_column * right[c]


def sweep(source, target, wide, stride, bed_source=None, top_col=None, top_source=None):
    layer_count, count, tiles = target.shape[1], target.shape[2] - 2, target.shape[3] - 2
    def body(i, carry):
        for t in range(tiles):
            carried = [[], []]
            for k in range(layer_count):
                for c in range(2):
                    value = lateral_sum(source, (c, k), i, t)
                    if k > 0:
                        value = value + get_field(wide, F_RATIO + k - 1, i, t) * carried[c][k - 1]
                    elif bed_source is not None:
                        value = value + bed_source[c, i, t]
                    carried[c].append(value)
            solved = [None, None]
            for k in range(layer_count - 1, -1, -1):
                for c in range(2):
                    value = get_field(wide, F_PIVOT + k, i, t) * carried[c][k]
                    if k + 1 < layer_count:
                        value = value + get_field(wide, F_RATIO + k, i, t) * solved[c]
                    solved[c] = value
                    if top_source is not None:
                        value = value + top_col[k, i, t] * top_source[c, i, t]
                    put_tile(target, (c, k, i + 1), t, tiles, stride, value)
        return carry

    lax.fori_loop(0, count, body, 0, unroll=6)
    wrap_layers(target, tiles)


def velocity_kernel(
    vectors, flags, message, basis, fields,
    misfit, low, high,
    wide, top_col, one, two, source, surface, flat,
):
    tile_x = LANES // vectors
    layer_count, count, tiles = top_col.shape[:3]
    tile_y = count * 8 - 2 * HALO
    offset = tile_x // 2
    group = lane_ids((8, LANES)) // vectors
    summed = jnp.broadcast_to(jnp.sum(message[...], axis=0, keepdims=True), (8, LANES))
    moments = [fold(jnp.where(group == j + 1, summed, 0.0), vectors) for j in range(6)]
    y = galerkin(moments)

    def prepare(i, carry):
        smooth = [y[0] * basis[0, i, t] + y[1] * basis[1, i, t] + y[2] * basis[2, i, t] for t in range(3)]
        smooth = reblock(smooth, vectors, tiles, offset)
        inv_lat, beds, _ = prepare_row(wide, i, None, top_col, layer_count, tiles)
        values = [
            [get_field(wide, F_BED + c, i, t) * smooth[t] for t in range(tiles)] for c in range(2)
        ]
        for c in range(2):
            for t in range(tiles):
                source[c, i, t] = values[c][t] * inv_lat[t]
        put_outer(one, i, beds, values, vectors)
        return carry

    expand_all(fields, wide, vectors, offset)

    lax.fori_loop(0, count, prepare, 0, unroll=6)
    wrap_layers(one, tiles)
    sweep(one, two, wide, vectors, bed_source=source)
    sweep(two, one, wide, vectors, bed_source=source)

    def finish(i, carry):
        across = [(c, t) for c in range(2) for t in range(tiles)]
        values = {(c, t): top_col[0, i, t] * source[c, i, t] for c, t in across}
        for k in range(layer_count):
            for c, t in across:
                values[c, t] = values[c, t] + top_col[k, i, t] * lateral_sum(one, (c, k), i, t)
        for c in range(2):
            surface[c, i] = to_own([values[c, t] for t in range(tiles)], vectors, offset)
        return carry

    lax.fori_loop(0, count, finish, 0, unroll=6)

    table = message[...]
    flipped = table.T
    lane = lane_ids((LANES, 2 * LANES))
    second = lane >= LANES
    at_row, at_lane = [], []
    for r in range(4):
        cell = flipped[8 + r : 9 + r, :].astype(jnp.int32)
        at_row.append((row_ids((tile_y, LANES)) == cell % tile_y).astype(jnp.float32))
        cell = table[:, 8 + r : 9 + r].astype(jnp.int32)
        weight = jnp.where(second, table[:, 4 + r : 5 + r], table[:, r : r + 1])
        at_lane.append(jnp.where(cell // tile_y == lane % LANES // vectors, weight, 0.0))
    weights = select_sum(
        jnp.concatenate(at_row, axis=1).astype(jnp.bfloat16), jnp.concatenate(at_lane, axis=0)
    )
    for c in range(2):
        join_rows(surface.at[c], flat)
        misfit[c] = weights[:, c * LANES : (c + 1) * LANES] * flat[HALO : HALO + tile_y, :]
    low[...] = misfit[:, 0:HALO, :]
    high[...] = misfit[:, tile_y - HALO :, :]


def adjoint_kernel(
    vectors, flags, fields, misfit, misfit_left, misfit_right, basis, previous,
    out, stacked,
    wide, top_col, one, two, source, bed_col, sides, spread, bed, reaction, v0, v1, v2, natural, flat,
):
    tile_x = LANES // vectors
    layer_count, count, tiles = top_col.shape[:3]
    tile_y = count * 8 - 2 * HALO
    value = jnp.concatenate(
        [misfit_left[...] * flags[0], misfit[...], misfit_right[...] * flags[1]], axis=-1
    )
    value = to_blocked(value.reshape(-1, 3 * LANES), vectors, tiles)
    for c in range(2):
        for t in range(tiles):
            sides[c, t] = value[c * count * 8 : (c + 1) * count * 8, t * LANES : (t + 1) * LANES]
            split_rows(sides.at[c, t], spread.at[c, t])

    def prepare(i, carry):
        values = [[spread[c, t, i] for t in range(tiles)] for c in range(2)]
        inv_lat, _, tops = prepare_row(wide, i, bed_col, top_col, layer_count, tiles)
        for t in range(tiles):
            reaction[i, t] = get_field(wide, F_REACT, i, t)
            total = None
            for c in range(2):
                value = values[c][t]
                source[c, i, t] = value
                drag = get_field(wide, F_BED + c, i, t)
                bed[c, i, t] = drag
                total = drag * value if total is None else total + drag * value
            v1[i + 1, t + 1] = total * (tops[0][t] * inv_lat[t])
        put_outer(one, i, tops, values, vectors)
        return carry

    expand_all(fields, wide, vectors, 0)

    lax.fori_loop(0, count, prepare, 0, unroll=6)
    wrap_layers(one, tiles)
    sweep(one, two, wide, vectors, top_col=top_col, top_source=source)
    sweep(two, one, wide, vectors, top_col=top_col, top_source=source)

    def finish(i, carry):
        totals = {}
        for k in range(layer_count):
            for c in range(2):
                for t in range(tiles):
                    value = bed_col[k, i, t] * lateral_sum(one, (c, k), i, t)
                    totals[c, t] = value if k == 0 else totals[c, t] + value
        for t in range(tiles):
            value = v1[i + 1, t + 1] + (bed[0, i, t] * totals[0, t] + bed[1, i, t] * totals[1, t])
            put_tile(v0, (i + 1,), t, tiles, vectors, value)
        return carry

    lax.fori_loop(0, count, finish, 0, unroll=6)
    last = krylov(v0, v1, v2, reaction, vectors, count, tile_y)
    own = []
    for n, field in enumerate((v0, v1, v2, basis.at[0])):
        at = 0 if n == 3 else 1
        for i in range(count):
            natural[i] = to_own([field[i + at, t + at] for t in range(tiles)], vectors, 0)
        join_rows(natural, flat)
        own.append(flat[HALO : HALO + tile_y, :])
    v0, v1, v2, x = own
    p = previous[...]
    flipped = [v.T for v in (v0, v1, v2, p, x)]
    for i, value in enumerate(flipped):
        for at in range(tile_x):
            stacked[at, i * vectors : (i + 1) * vectors, :] = value[at * vectors : (at + 1) * vectors, :]
    t0, t1, t2, tp, tx = flipped
    pairs = (
        (t0, v0), (t0, v1), (t1, v1), (t1, v2), (t2, v2),
        (tx, v0), (tx, v1), (tx, v2),
        (t0, p), (t1, p), (t2, p),
        (tx, x), (tx, p), (tp, p),
    )
    same = row_ids((LANES, LANES)) // vectors == lane_ids((LANES, LANES)) // vectors
    group = lane_ids((vectors, LANES)) // vectors
    halves = [jnp.zeros((vectors, LANES), jnp.float32)] * 2
    for n, (a, b) in enumerate(pairs):
        product = jnp.dot(a, b, precision=highest, preferred_element_type=jnp.float32)
        product = jnp.where(same, product, 0.0)
        block = product[0:vectors]
        for at in range(1, tile_x):
            block = block + product[at * vectors : (at + 1) * vectors]
        block = fold(block, vectors)
        halves[n // tile_x] = jnp.where(group == n % tile_x, block, halves[n // tile_x])
    last = fold(jnp.sum(last, axis=0, keepdims=True), vectors)
    n = len(pairs)
    halves[n // tile_x] = jnp.where(group == n % tile_x, last, halves[n // tile_x])
    both = jnp.concatenate(halves, axis=1)
    for i in range(out.shape[0]):
        out[i] = both


def finish_kernel(cells, received, stacked, beta_ref, next_out, alpha_out, beta_out):
    vectors = beta_ref.shape[0]
    total = jnp.sum(received[...], axis=0)

    def block(n):
        return total[:, n * vectors : (n + 1) * vectors]

    def dot(a, b, dims=((1,), (0,))):
        return lax.dot_general(a, b, (dims, ((), ())), precision=highest, preferred_element_type=jnp.float32)

    shape = (vectors, vectors)
    eye = row_ids(shape) == lane_ids(shape)
    s = [block(n) for n in range(5)]
    moments = [jnp.sum(jnp.where(eye, m, 0.0), axis=0, keepdims=True) for m in s]
    moments.append(block(14)[0:1])
    along = galerkin(moments)
    down = [jnp.sum(jnp.where(eye, v, 0.0), axis=1, keepdims=True) for v in along]
    xv = [block(5 + k) for k in range(3)]
    vp = [block(8 + k) for k in range(3)]
    xx, xp, pp = block(11), block(12), block(13)
    beta = beta_ref[...]
    last = ((1,), (1,))
    first = ((0,), (0,))
    xr = xv[0] * along[0] + xv[1] * along[1] + xv[2] * along[2] - dot(xp, beta, last)
    alpha = xr * (1.0 / cells)
    alpha_out[...] = alpha
    rr = None
    for k in range(3):
        for l in range(3):
            term = down[k] * along[l] * s[k + l]
            rr = term if rr is None else rr + term
    cross = dot(down[0] * vp[0] + down[1] * vp[1] + down[2] * vp[2], beta, last)
    rr = rr - cross - cross.T + dot(beta, dot(pp, beta, last))
    gram = rr * (1.0 / cells) - 2.0 * dot(alpha, alpha, first) + dot(
        alpha, dot(xx * (1.0 / cells), alpha), first
    )
    gram = 0.5 * (gram + gram.T)
    work = jnp.concatenate(
        [gram, eye.astype(jnp.float32), jnp.zeros((vectors, LANES - 2 * vectors), jnp.float32)], axis=1
    )
    down_id = row_ids(work.shape)
    for j in range(vectors - 1):
        row = work[j : j + 1, :]
        column = jnp.where(down_id > j, work[:, j : j + 1], 0.0)
        work = work - column * (row * (1.0 / row[:, j : j + 1]))
    pivot = jnp.sum(jnp.where(eye, work[:, 0:vectors], 0.0), axis=1, keepdims=True)
    work = work * (1.0 / jnp.sqrt(pivot))
    beta_out[...] = jnp.where(row_ids(shape) <= lane_ids(shape), work[:, 0:vectors], 0.0)
    inverse = work[:, vectors : 2 * vectors]
    mix = jnp.concatenate(
        [inverse * v for v in along] + [-dot(inverse, beta), -dot(inverse, alpha, last)], axis=1
    )
    for at in range(stacked.shape[0]):
        next_out[:, at, :] = dot(mix, stacked[at])


def shards(
    lanczos_block,
    previous_block,
    previous_beta,
    prior_reaction,
    vert_coupling,
    horiz_coupling,
    friction,
    base_velocity,
    layers,
    obs_dest,
    obs_cell,
    obs_weight,
):
    vectors, tile_x, tile_y = lanczos_block.shape
    layer_count = horiz_coupling.shape[0]
    obs_rows = obs_cell.shape[0]
    size_x, size_y = lax.axis_size("mx"), lax.axis_size("my")
    devices = size_x * size_y
    cells = tile_x * tile_y * devices
    at_x, at_y = lax.axis_index("mx"), lax.axis_index("my")
    flags = jnp.stack([at_x > 0, at_x + 1 < size_x]).astype(jnp.float32)
    low_flag = (at_y > 0).astype(jnp.float32)
    high_flag = (at_y + 1 < size_y).astype(jnp.float32)
    forward_y = [(i, (i + 1) % size_y) for i in range(size_y)]
    backward_y = [(i, (i - 1) % size_y) for i in range(size_y)]
    forward_x = [(i, (i + 1) % size_x) for i in range(size_x)]
    backward_x = [(i, (i - 1) % size_x) for i in range(size_x)]
    f32 = jnp.float32
    rows = tile_y + 2 * HALO
    tiles = -(-(vectors * tile_x + FIELDS * tile_x) // LANES)
    smem = pl.BlockSpec(memory_space=pltpu.SMEM)
    vmem = pl.BlockSpec(memory_space=pltpu.VMEM)

    def shape(*dims):
        return jax.ShapeDtypeStruct(dims, f32)

    packed, previous, low, high = pl.pallas_call(
        pack_kernel,
        out_shape=(
            shape(tiles, tile_y, LANES), shape(tile_y, LANES), shape(tiles, HALO, LANES), shape(tiles, HALO, LANES)
        ),
        scratch_shapes=[pltpu.VMEM((tiles * LANES, tile_y), f32)],
        compiler_params=params(),
        name="pack",
    )(
        lanczos_block, previous_block, prior_reaction, vert_coupling, horiz_coupling,
        friction, base_velocity, layers,
    )
    table = pl.pallas_call(
        table_kernel, out_shape=shape(devices, LANES), compiler_params=params(), name="table"
    )(obs_dest.reshape(1, obs_rows), obs_cell.reshape(1, obs_rows), obs_weight.T)

    from_low = lax.ppermute(high, "my", forward_y)
    from_high = lax.ppermute(low, "my", backward_y)
    own = jnp.concatenate([from_low * low_flag, packed, from_high * high_flag], axis=1)
    left = lax.ppermute(own, "mx", forward_x)
    right = lax.ppermute(own, "mx", backward_x)

    count = rows // 8
    groups = -(-FIELDS // 4)

    def blocked(*dims):
        return pltpu.VMEM((*dims, 8, LANES), f32)

    message, basis, fields = pl.pallas_call(
        functools.partial(moment_kernel, vectors),
        out_shape=(
            shape(devices, LANES), shape(3, count, 3, 8, LANES), shape(groups, count, 8, LANES)
        ),
        in_specs=[smem, vmem, vmem, vmem, vmem],
        scratch_shapes=[pltpu.VMEM((3 + groups, rows, LANES), f32), blocked(3, count), blocked(count, 3)]
        + [blocked(count + 2, 5)] * 3,
        compiler_params=params(),
        name="moments",
    )(flags, own, left, right, table)
    message = lax.all_to_all(message, AXES, split_axis=0, concat_axis=0, tiled=True)

    def columns(width):
        return [
            pltpu.VMEM((groups, count, 8, 4 * width * LANES), f32),
            blocked(layer_count, count, width),
            blocked(2, layer_count, count + 2, width + 2),
            blocked(2, layer_count, count + 2, width + 2),
            blocked(2, count, width),
        ]

    misfit, low, high = pl.pallas_call(
        functools.partial(velocity_kernel, vectors),
        out_shape=(shape(2, tile_y, LANES), shape(2, HALO, LANES), shape(2, HALO, LANES)),
        in_specs=[smem] + [vmem] * 3,
        scratch_shapes=columns(2) + [blocked(2, count), pltpu.VMEM((rows, LANES), f32)],
        compiler_params=params(),
        name="velocity",
    )(flags, message, basis, fields)

    from_low = lax.ppermute(high, "my", forward_y)
    from_high = lax.ppermute(low, "my", backward_y)
    misfit = jnp.concatenate([from_low * low_flag, misfit, from_high * high_flag], axis=1)
    misfit_left = lax.ppermute(misfit, "mx", forward_x)
    misfit_right = lax.ppermute(misfit, "mx", backward_x)

    products, stacked = pl.pallas_call(
        functools.partial(adjoint_kernel, vectors),
        out_shape=(shape(size_x, vectors, 2 * LANES), shape(tile_x, 5 * vectors, tile_y)),
        in_specs=[smem] + [vmem] * 6,
        scratch_shapes=columns(3)
        + [blocked(layer_count, count, 3), pltpu.VMEM((2, 3, rows, LANES), f32), blocked(2, 3, count), blocked(2, count, 3), blocked(count, 3)]
        + [blocked(count + 2, 5)] * 3
        + [blocked(count), pltpu.VMEM((rows, LANES), f32)],
        compiler_params=params(),
        name="adjoint",
    )(flags, fields, misfit, misfit_left, misfit_right, basis, previous)

    products = lax.all_to_all(products, "mx", split_axis=0, concat_axis=0, tiled=True)
    products = jnp.broadcast_to(jnp.sum(products, axis=0)[None], (size_y, vectors, 2 * LANES))
    products = lax.all_to_all(products, "my", split_axis=0, concat_axis=0, tiled=True)
    return pl.pallas_call(
        functools.partial(finish_kernel, float(cells)),
        out_shape=(shape(vectors, tile_x, tile_y), shape(vectors, vectors), shape(vectors, vectors)),
        compiler_params=params(),
        name="finish",
    )(products, stacked, previous_beta)


def solution(mesh):
    in_specs = (
        P(None, "mx", "my"),
        P(None, "mx", "my"),
        P(),
        P("mx", "my"),
        P(None, "mx", "my"),
        P(None, "mx", "my"),
        P("mx", "my"),
        P(None, "mx", "my"),
        P("mx", "my"),
        P(("mx", "my"), None),
        P(("mx", "my")),
        P(("mx", "my"), None),
    )
    out_specs = (P(None, "mx", "my"), P(), P())
    return jax.shard_map(shards, mesh=mesh, in_specs=in_specs, out_specs=out_specs, check_vma=False)
```

```python
import functools

import jax
import jax.numpy as jnp
from jax import lax
from jax.experimental import pallas as pl
from jax.experimental.pallas import tpu as pltpu
from jax.sharding import PartitionSpec as P

base_damping = 0.02
highest = lax.Precision.HIGHEST
SHIFT = 4.25
SCALE = 4.25
LANES = 128
HALO = 8
AXES = ("mx", "my")
VMEM_LIMIT = 50 * 1024 * 1024

F_RATIO = 0
F_PIVOT = 15
F_INV_LAT = 31
F_TOP = 32
F_LAYER = 33
F_BED = 34
F_REACT = 36
FIELDS = 37


def params():
    return pltpu.CompilerParams(vmem_limit_bytes=VMEM_LIMIT)


def lane_ids(shape):
    return lax.broadcasted_iota(jnp.int32, shape, len(shape) - 1)


def row_ids(shape):
    return lax.broadcasted_iota(jnp.int32, shape, len(shape) - 2)


def pack_kernel(
    block, previous, reaction, vert, horiz, friction, velocity, layers, out, prev_out, low, high, rows
):
    vectors, tile_x, tile_y = block.shape
    layer_count = horiz.shape[0]
    depth = layers[...]
    active = [(depth > k).astype(jnp.float32) for k in range(layer_count)]
    zero = jnp.zeros((tile_x, tile_y), jnp.float32)
    up = [vert[k] * active[k + 1] for k in range(layer_count - 1)] + [zero]
    lateral = [horiz[k] * active[k] for k in range(layer_count)]
    pivots = []
    for k in range(layer_count):
        drag = friction[...] if k == 0 else up[k - 1]
        diagonal = (base_damping + lateral[k] + drag + up[k]) * active[k] + (1.0 - active[k])
        if k > 0:
            diagonal = diagonal - up[k - 1] * up[k - 1] / pivots[k - 1]
        pivots.append(diagonal)
    top = zero
    for b in range(vectors):
        rows[pl.ds(b, tile_x, stride=vectors), :] = block[b]

    def put(field, value):
        rows[pl.ds(vectors * tile_x + field * tile_x, tile_x), :] = value

    for k in range(layer_count):
        put(F_PIVOT + k, lateral[k] * lateral[k] / pivots[k])
        is_top = depth == k + 1
        top = jnp.where(is_top, lateral[k] / pivots[k], top)
        if k + 1 < layer_count:
            below = jnp.where(depth > k + 1, lateral[k + 1], 1.0)
            put(F_RATIO + k, up[k] * lateral[k] / (pivots[k] * below))
    put(F_INV_LAT, 1.0 / lateral[0])
    put(F_TOP, top)
    put(F_LAYER, depth.astype(jnp.float32))
    put(F_BED, friction[...] * velocity[0])
    put(F_BED + 1, friction[...] * velocity[1])
    put(F_REACT, reaction[...])
    used = vectors * tile_x + FIELDS * tile_x
    rows[used:, :] = jnp.zeros((rows.shape[0] - used, tile_y), jnp.float32)
    for t in range(rows.shape[0] // LANES):
        out[t] = rows[t * LANES : (t + 1) * LANES, :].T
    low[...] = out[:, 0:HALO, :]
    high[...] = out[:, tile_y - HALO : tile_y, :]
    for b in range(vectors):
        rows[pl.ds(b, tile_x, stride=vectors), :] = previous[b]
    prev_out[...] = rows[0:LANES, :].T


def table_kernel(dest, cell, weight, out):
    count = dest.shape[1]
    devices = out.shape[0]
    rows = jnp.concatenate(
        [
            dest[...].astype(jnp.float32),
            cell[...].astype(jnp.float32),
            weight[...],
            jnp.zeros((4, count), jnp.float32),
        ],
        axis=0,
    )
    columns = rows.T
    target = columns[:, 0:1].astype(jnp.int32)
    onehot = target == lane_ids((count, devices))
    lower = row_ids((count, count)) >= lane_ids((count, count))
    running = jnp.dot(
        lower.astype(jnp.float32).astype(jnp.bfloat16),
        onehot.astype(jnp.float32).astype(jnp.bfloat16),
        preferred_element_type=jnp.float32,
    )
    chosen = onehot.astype(jnp.float32)
    rank = jnp.sum(running * chosen, axis=1, keepdims=True).astype(jnp.int32) - 1
    lane = lane_ids((count, LANES))
    kind = lane // 4
    value = jnp.where(
        kind == 0,
        columns[:, 2:3],
        jnp.where(kind == 1, columns[:, 3:4], jnp.where(kind == 2, columns[:, 1:2], 0.0)),
    )
    value = jnp.where(lane % 4 == rank, value, 0.0)
    chosen = (row_ids((devices, count)) == dest[...]).astype(jnp.float32).astype(jnp.bfloat16)
    out[...] = select_sum(chosen, value)


def pieces(value, axis):
    parts = []
    for _ in range(3):
        piece = value.astype(jnp.bfloat16)
        value = value - piece.astype(jnp.float32)
        parts.append(piece)
    return jnp.concatenate(parts, axis=axis)


def thrice(chosen):
    chosen = chosen.astype(jnp.float32).astype(jnp.bfloat16)
    return jnp.concatenate([chosen] * 3, axis=0)


def select_sum(chosen, value):
    total = None
    for _ in range(3):
        piece = value.astype(jnp.bfloat16)
        value = value - piece.astype(jnp.float32)
        part = jnp.dot(chosen, piece, preferred_element_type=jnp.float32)
        total = part if total is None else total + part
    return total


def fold(row, stride):
    shift = LANES // 2
    while shift >= stride:
        row = row + pltpu.roll(row, shift, 1)
        shift //= 2
    return row


def gather(tile, index):
    return jnp.take_along_axis(tile, index, axis=1)


def pick(which, values):
    result = values[-1]
    for n in range(len(values) - 2, -1, -1):
        result = jnp.where(which == n, values[n], result)
    return result


def tile_rows(vectors, tiles, offset, tile):
    return offset + (lane_ids((8, LANES)) // vectors) * tiles + tile


def to_blocked(value, vectors, tiles):
    shape = (3 * LANES, tiles * LANES)
    column, source = lane_ids(shape), row_ids(shape)
    row = (column % LANES // vectors) * tiles + column // LANES
    chosen = source == row * vectors + column % vectors
    return jnp.dot(pieces(value, 1), thrice(chosen), preferred_element_type=jnp.float32)


def reblock(values, vectors, tiles, offset):
    out = []
    for t in range(tiles):
        row = tile_rows(vectors, tiles, offset, t)
        index = (row // len(values)) * vectors + lane_ids((8, LANES)) % vectors
        out.append(pick(row % len(values), [gather(value, index) for value in values]))
    return out


def to_own(values, vectors, offset):
    tiles = len(values)
    row = lane_ids((8, LANES)) // vectors + LANES // vectors - offset
    index = (row // tiles) * vectors + lane_ids((8, LANES)) % vectors
    return pick(row % tiles, [gather(value, index) for value in values])


def split_rows(source, target, flag=None):
    count = target.shape[-3]
    for i in range(count):
        value = source[pl.ds(i, 8, stride=count), :]
        target[i] = value if flag is None else value * flag


def join_rows(source, target):
    count = source.shape[0]
    for i in range(count):
        target[pl.ds(i, 8, stride=count), :] = source[i]


def put_tile(field, at, t, tiles, stride, value):
    field[(*at, t + 1)] = value
    if t == 0:
        field[(*at, tiles + 1)] = pltpu.roll(value, LANES - stride, 1)
    if t == tiles - 1:
        field[(*at, 0)] = pltpu.roll(value, stride, 1)


def lateral_sum(field, at, i, t):
    return (field[(*at, i, t + 1)] + field[(*at, i + 2, t + 1)]) + (
        field[(*at, i + 1, t)] + field[(*at, i + 1, t + 2)]
    )


def wrap_rows(field, at, count, tiles):
    for t in range(1, tiles + 1):
        field[(*at, 0, t)] = pltpu.roll(field[(*at, count, t)], 1, 0)
        field[(*at, count + 1, t)] = pltpu.roll(field[(*at, 1, t)], 7, 0)


def wrap_layers(field, tiles):
    count = field.shape[2] - 2

    def body(k, carry):
        for c in range(2):
            wrap_rows(field, (c, k), count, tiles)
        return carry

    lax.fori_loop(0, field.shape[1], body, 0, unroll=4)


def own_cells(vectors, tiles, offset, count, tile_y, i, t):
    tile_x = LANES // vectors
    row = tile_rows(vectors, tiles, offset, t)
    column = row_ids((8, LANES)) * count + i
    return (row >= tile_x) & (row < 2 * tile_x) & (column >= HALO) & (column < HALO + tile_y)


def shifted_prior(field, i, t, reaction):
    image = (reaction - (SHIFT - 4.0)) * field[i + 1, t + 1] - lateral_sum(field, (), i, t)
    return jnp.where(reaction > 0.0, image * (1.0 / SCALE), 0.0)


def krylov(first, second, third, reaction, vectors, count, tile_y):
    tiles = reaction.shape[1]

    def step(source, target):
        wrap_rows(source, (), count, tiles)
        for i in range(count):
            for t in range(tiles):
                value = shifted_prior(source, i, t, reaction[i, t])
                put_tile(target, (i + 1,), t, tiles, vectors, value)

    step(first, second)
    step(second, third)
    wrap_rows(third, (), count, tiles)
    total = jnp.zeros((8, LANES), jnp.float32)
    for i in range(count):
        for t in range(tiles):
            value = shifted_prior(third, i, t, reaction[i, t]) * third[i + 1, t + 1]
            total = total + jnp.where(own_cells(vectors, tiles, 0, count, tile_y, i, t), value, 0.0)
    return total


def moment_kernel(
    vectors, flags, own, left, right, table, out, basis, fields, flat, parts, reaction, v0, v1, v2
):
    tile_x = LANES // vectors
    rows = own.shape[1]
    count = rows // 8
    tile_y = rows - 2 * HALO
    def beside(tiles):
        value = jnp.concatenate([left[tiles] * flags[0], own[tiles], right[tiles] * flags[1]], axis=-1)
        return value.reshape(-1, 3 * LANES)

    blocked = to_blocked(beside(0), vectors, 3)
    for t in range(3):
        flat[t] = blocked[:, t * LANES : (t + 1) * LANES]
    per_tile = LANES // (4 * tile_x)
    shape = (3 * LANES, per_tile * LANES)
    column, at = lane_ids(shape), row_ids(shape)
    lane = column % 32
    field = column // LANES * 4 + column % LANES // 32
    chosen = (at == lane // tile_x * LANES + field * tile_x + lane % tile_x) & (lane < 3 * tile_x)
    value = beside(slice(1, own.shape[0]))
    out_all = jnp.dot(pieces(value, 1), thrice(chosen), preferred_element_type=jnp.float32)
    for q in range(fields.shape[0]):
        first = q // per_tile * rows
        lanes = q % per_tile * LANES
        flat[3 + q] = out_all[first : first + rows, lanes : lanes + LANES]
    for t in range(3):
        split_rows(flat.at[t], parts.at[t])
    for q in range(fields.shape[0]):
        split_rows(flat.at[3 + q], fields.at[q])

    for i in range(count):
        for t in range(3):
            put_tile(v0, (i + 1,), t, 3, vectors, parts[t, i])
            reaction[i, t] = expand(fields, F_REACT, i, t, 3, 0, vectors)
    last = krylov(v0, v1, v2, reaction, vectors, count, tile_y)
    sums = [jnp.zeros((8, LANES), jnp.float32) for _ in range(5)]
    for i in range(count):
        for t in range(3):
            mine = own_cells(vectors, 3, 0, count, tile_y, i, t)
            a, b, c = v0[i + 1, t + 1], v1[i + 1, t + 1], v2[i + 1, t + 1]
            basis[0, i, t] = a
            basis[1, i, t] = b
            basis[2, i, t] = c
            a, b, c = [jnp.where(mine, v, 0.0) for v in (a, b, c)]
            sums = [
                total + one * two
                for total, one, two in zip(sums, (a, a, b, b, c), (a, b, b, c, c))
            ]
    sums.append(last)
    group = lane_ids((1, LANES)) // vectors
    message = jnp.zeros((1, LANES), jnp.float32)
    for j, value in enumerate(sums):
        total = fold(jnp.sum(value, axis=0, keepdims=True), vectors)
        message = jnp.where(group == j + 1, total, message)
    out[...] = table[...] + message


def expand(fields, field, i, t, tiles, offset, vectors):
    index = (field % 4) * 32 + tile_rows(vectors, tiles, offset, t)
    return gather(fields[field // 4, i], index)


def galerkin(moments):
    m = moments
    a = [SHIFT * m[i] + SCALE * m[i + 1] for i in range(5)]

    def over(top, pivot):
        return jnp.where(pivot > 0.0, top / jnp.where(pivot > 0.0, pivot, 1.0), 0.0)

    l10, l20 = over(a[1], a[0]), over(a[2], a[0])
    d1 = a[2] - l10 * a[1]
    e12 = a[3] - l20 * a[1]
    l21 = over(e12, d1)
    d2 = a[4] - l20 * a[2] - l21 * e12
    z1 = m[1] - l10 * m[0]
    z2 = m[2] - l20 * m[0] - l21 * z1
    y2 = over(z2, d2)
    y1 = over(z1, d1) - l21 * y2
    y0 = over(m[0], a[0]) - l10 * y1 - l20 * y2
    return y0, y1, y2


def expand_all(fields, wide, vectors, offset):
    groups, count = fields.shape[:2]
    value = pieces(fields[...].reshape(groups * count * 8, LANES), 1)
    half = wide.shape[-1] // 2
    tiles = half // (2 * LANES)
    shape = (LANES, half)
    column = lane_ids(shape)
    tile = column // LANES
    row = offset + (column % LANES // vectors) * tiles + tile % tiles
    for j in range(2):
        chosen = row_ids(shape) == (2 * j + tile // tiles) * 32 + row
        out = jnp.dot(value, thrice(chosen), preferred_element_type=jnp.float32)
        wide[:, :, :, j * half : (j + 1) * half] = out.reshape(groups, count, 8, half)


def get_field(wide, field, i, t):
    at = (field % 4) * (wide.shape[-1] // (4 * LANES)) + t
    return wide[field // 4, i, :, at * LANES : (at + 1) * LANES]


def prepare_row(wide, i, bed_col, top_col, layer_count, tiles):
    across = range(tiles)
    get = functools.partial(get_field, wide, i=i)
    inv_lat = [get(F_INV_LAT, t=t) for t in across]
    top = [get(F_TOP, t=t) for t in across]
    depth = [get(F_LAYER, t=t) for t in across]
    forward = [inv_lat]
    for k in range(1, layer_count):
        forward.append([get(F_RATIO + k - 1, t=t) * forward[k - 1][t] for t in across])
    beds, tops = [None] * layer_count, [None] * layer_count
    for k in range(layer_count - 1, -1, -1):
        beds[k], tops[k] = [], []
        for t in across:
            bed = get(F_PIVOT + k, t=t) * forward[k][t]
            below = 0.0
            if k + 1 < layer_count:
                ratio = get(F_RATIO + k, t=t)
                bed = bed + ratio * beds[k + 1][t]
                if top_col is not None:
                    below = ratio * tops[k + 1][t]
            beds[k].append(bed)
            if top_col is not None:
                surf = jnp.where(depth[t] == float(k + 1), top[t], below)
                bed_col[k, i, t] = bed
                top_col[k, i, t] = surf
                tops[k].append(surf)
    return inv_lat, beds, tops


def put_outer(field, i, columns, values, stride):
    tiles = len(values[0])
    right = [pltpu.roll(v[0], LANES - stride, 1) for v in values]
    left = [pltpu.roll(v[tiles - 1], stride, 1) for v in values]
    for k, column in enumerate(columns):
        right_column = pltpu.roll(column[0], LANES - stride, 1)
        left_column = pltpu.roll(column[tiles - 1], stride, 1)
        for c, value in enumerate(values):
            field[c, k, i + 1, 0] = left_column * left[c]
            for t in range(tiles):
                field[c, k, i + 1, t + 1] = column[t] * value[t]
            field[c, k, i + 1, tiles + 1] = right_column * right[c]


def sweep(source, target, wide, stride, unroll, bed_source=None, top_col=None, top_source=None):
    layer_count, count, tiles = target.shape[1], target.shape[2] - 2, target.shape[3] - 2
    def body(i, carry):
        for t in range(tiles):
            carried = [[], []]
            for k in range(layer_count):
                for c in range(2):
                    value = lateral_sum(source, (c, k), i, t)
                    if k > 0:
                        value = value + get_field(wide, F_RATIO + k - 1, i, t) * carried[c][k - 1]
                    elif bed_source is not None:
                        value = value + bed_source[c, i, t]
                    carried[c].append(value)
            solved = [None, None]
            for k in range(layer_count - 1, -1, -1):
                for c in range(2):
                    value = get_field(wide, F_PIVOT + k, i, t) * carried[c][k]
                    if k + 1 < layer_count:
                        value = value + get_field(wide, F_RATIO + k, i, t) * solved[c]
                    solved[c] = value
                    if top_source is not None:
                        value = value + top_col[k, i, t] * top_source[c, i, t]
                    put_tile(target, (c, k, i + 1), t, tiles, stride, value)
        return carry

    lax.fori_loop(0, count, body, 0, unroll=unroll)
    wrap_layers(target, tiles)


def velocity_kernel(
    vectors, flags, message, basis, fields,
    misfit, low, high,
    wide, one, two, source, surface, flat,
):
    tile_x = LANES // vectors
    layer_count, count, tiles = one.shape[1], one.shape[2] - 2, one.shape[3] - 2
    tile_y = count * 8 - 2 * HALO
    offset = tile_x // 2
    group = lane_ids((8, LANES)) // vectors
    summed = jnp.broadcast_to(jnp.sum(message[...], axis=0, keepdims=True), (8, LANES))
    moments = [fold(jnp.where(group == j + 1, summed, 0.0), vectors) for j in range(6)]
    y = galerkin(moments)

    def prepare(i, carry):
        smooth = [y[0] * basis[0, i, t] + y[1] * basis[1, i, t] + y[2] * basis[2, i, t] for t in range(3)]
        smooth = reblock(smooth, vectors, tiles, offset)
        inv_lat, beds, _ = prepare_row(wide, i, None, None, layer_count, tiles)
        values = [
            [get_field(wide, F_BED + c, i, t) * smooth[t] for t in range(tiles)] for c in range(2)
        ]
        for c in range(2):
            for t in range(tiles):
                source[c, i, t] = values[c][t] * inv_lat[t]
        put_outer(one, i, beds, values, vectors)
        return carry

    expand_all(fields, wide, vectors, offset)

    lax.fori_loop(0, count, prepare, 0, unroll=6)
    wrap_layers(one, tiles)
    sweep(one, two, wide, vectors, count, bed_source=source)
    sweep(two, one, wide, vectors, count, bed_source=source)

    def finish(i, carry):
        across = [(c, t) for c in range(2) for t in range(tiles)]
        values, carried = {}, {}
        for k in range(layer_count):
            for c, t in across:
                value = lateral_sum(one, (c, k), i, t)
                if k == 0:
                    value = value + source[c, i, t]
                    values[c, t] = value
                else:
                    value = value + get_field(wide, F_RATIO + k - 1, i, t) * carried[c, t]
                    deep = get_field(wide, F_LAYER, i, t) > float(k)
                    values[c, t] = jnp.where(deep, value, values[c, t])
                carried[c, t] = value
        for c, t in across:
            values[c, t] = values[c, t] * get_field(wide, F_TOP, i, t)
        for c in range(2):
            surface[c, i] = to_own([values[c, t] for t in range(tiles)], vectors, offset)
        return carry

    lax.fori_loop(0, count, finish, 0, unroll=6)

    table = message[...]
    flipped = table.T
    lane = lane_ids((LANES, 2 * LANES))
    second = lane >= LANES
    at_row, at_lane = [], []
    for r in range(4):
        cell = flipped[8 + r : 9 + r, :].astype(jnp.int32)
        at_row.append((row_ids((tile_y, LANES)) == cell % tile_y).astype(jnp.float32))
        cell = table[:, 8 + r : 9 + r].astype(jnp.int32)
        weight = jnp.where(second, table[:, 4 + r : 5 + r], table[:, r : r + 1])
        at_lane.append(jnp.where(cell // tile_y == lane % LANES // vectors, weight, 0.0))
    weights = select_sum(
        jnp.concatenate(at_row, axis=1).astype(jnp.bfloat16), jnp.concatenate(at_lane, axis=0)
    )
    for c in range(2):
        join_rows(surface.at[c], flat)
        misfit[c] = weights[:, c * LANES : (c + 1) * LANES] * flat[HALO : HALO + tile_y, :]
    low[...] = misfit[:, 0:HALO, :]
    high[...] = misfit[:, tile_y - HALO :, :]


def adjoint_kernel(
    vectors, flags, fields, misfit, misfit_left, misfit_right, basis, previous,
    out, stacked,
    wide, one, two, source, top_col, bed_col, sides, spread, bed, reaction, v0, v1, v2, natural, flat,
):
    tile_x = LANES // vectors
    layer_count, count, tiles = top_col.shape[:3]
    tile_y = count * 8 - 2 * HALO
    value = jnp.concatenate(
        [misfit_left[...] * flags[0], misfit[...], misfit_right[...] * flags[1]], axis=-1
    )
    value = to_blocked(value.reshape(-1, 3 * LANES), vectors, tiles)
    for c in range(2):
        for t in range(tiles):
            sides[c, t] = value[c * count * 8 : (c + 1) * count * 8, t * LANES : (t + 1) * LANES]
            split_rows(sides.at[c, t], spread.at[c, t])

    def prepare(i, carry):
        values = [[spread[c, t, i] for t in range(tiles)] for c in range(2)]
        inv_lat, _, tops = prepare_row(wide, i, bed_col, top_col, layer_count, tiles)
        for t in range(tiles):
            reaction[i, t] = get_field(wide, F_REACT, i, t)
            total = None
            for c in range(2):
                value = values[c][t]
                source[c, i, t] = value
                drag = get_field(wide, F_BED + c, i, t)
                bed[c, i, t] = drag
                total = drag * value if total is None else total + drag * value
            v1[i + 1, t + 1] = total * (tops[0][t] * inv_lat[t])
        put_outer(one, i, tops, values, vectors)
        return carry

    expand_all(fields, wide, vectors, 0)

    lax.fori_loop(0, count, prepare, 0, unroll=6)
    wrap_layers(one, tiles)
    sweep(one, two, wide, vectors, 6, top_col=top_col, top_source=source)
    sweep(two, one, wide, vectors, 6, top_col=top_col, top_source=source)

    def finish(i, carry):
        totals = {}
        for k in range(layer_count):
            for c in range(2):
                for t in range(tiles):
                    value = bed_col[k, i, t] * lateral_sum(one, (c, k), i, t)
                    totals[c, t] = value if k == 0 else totals[c, t] + value
        for t in range(tiles):
            value = v1[i + 1, t + 1] + (bed[0, i, t] * totals[0, t] + bed[1, i, t] * totals[1, t])
            put_tile(v0, (i + 1,), t, tiles, vectors, value)
        return carry

    lax.fori_loop(0, count, finish, 0, unroll=6)
    last = krylov(v0, v1, v2, reaction, vectors, count, tile_y)
    own = []
    for n, field in enumerate((v0, v1, v2, basis.at[0])):
        at = 0 if n == 3 else 1
        for i in range(count):
            natural[i] = to_own([field[i + at, t + at] for t in range(tiles)], vectors, 0)
        join_rows(natural, flat)
        own.append(flat[HALO : HALO + tile_y, :])
    v0, v1, v2, x = own
    p = previous[...]
    flipped = [v.T for v in (v0, v1, v2, p, x)]
    for i, value in enumerate(flipped):
        for at in range(tile_x):
            stacked[at, i * vectors : (i + 1) * vectors, :] = value[at * vectors : (at + 1) * vectors, :]
    t0, t1, t2, tp, tx = flipped
    pairs = (
        (t0, v0), (t0, v1), (t1, v1), (t1, v2), (t2, v2),
        (tx, v0), (tx, v1), (tx, v2),
        (t0, p), (t1, p), (t2, p),
        (tx, x), (tx, p), (tp, p),
    )
    same = row_ids((LANES, LANES)) // vectors == lane_ids((LANES, LANES)) // vectors
    group = lane_ids((vectors, LANES)) // vectors
    halves = [jnp.zeros((vectors, LANES), jnp.float32)] * 2
    for n, (a, b) in enumerate(pairs):
        product = jnp.dot(a, b, precision=highest, preferred_element_type=jnp.float32)
        product = jnp.where(same, product, 0.0)
        block = product[0:vectors]
        for at in range(1, tile_x):
            block = block + product[at * vectors : (at + 1) * vectors]
        block = fold(block, vectors)
        halves[n // tile_x] = jnp.where(group == n % tile_x, block, halves[n // tile_x])
    last = fold(jnp.sum(last, axis=0, keepdims=True), vectors)
    n = len(pairs)
    halves[n // tile_x] = jnp.where(group == n % tile_x, last, halves[n // tile_x])
    both = jnp.concatenate(halves, axis=1)
    for i in range(out.shape[0]):
        out[i] = both


def finish_kernel(cells, received, stacked, beta_ref, next_out, alpha_out, beta_out):
    vectors = beta_ref.shape[0]
    total = jnp.sum(received[...], axis=0)

    def block(n):
        return total[:, n * vectors : (n + 1) * vectors]

    def dot(a, b, dims=((1,), (0,))):
        return lax.dot_general(a, b, (dims, ((), ())), precision=highest, preferred_element_type=jnp.float32)

    shape = (vectors, vectors)
    eye = row_ids(shape) == lane_ids(shape)
    s = [block(n) for n in range(5)]
    moments = [jnp.sum(jnp.where(eye, m, 0.0), axis=0, keepdims=True) for m in s]
    moments.append(block(14)[0:1])
    along = galerkin(moments)
    down = [jnp.sum(jnp.where(eye, v, 0.0), axis=1, keepdims=True) for v in along]
    xv = [block(5 + k) for k in range(3)]
    vp = [block(8 + k) for k in range(3)]
    xx, xp, pp = block(11), block(12), block(13)
    beta = beta_ref[...]
    last = ((1,), (1,))
    first = ((0,), (0,))
    xr = xv[0] * along[0] + xv[1] * along[1] + xv[2] * along[2] - dot(xp, beta, last)
    alpha = xr * (1.0 / cells)
    alpha_out[...] = alpha
    rr = None
    for k in range(3):
        for l in range(3):
            term = down[k] * along[l] * s[k + l]
            rr = term if rr is None else rr + term
    cross = dot(down[0] * vp[0] + down[1] * vp[1] + down[2] * vp[2], beta, last)
    rr = rr - cross - cross.T + dot(beta, dot(pp, beta, last))
    gram = rr * (1.0 / cells) - 2.0 * dot(alpha, alpha, first) + dot(
        alpha, dot(xx * (1.0 / cells), alpha), first
    )
    gram = 0.5 * (gram + gram.T)
    work = jnp.concatenate(
        [gram, eye.astype(jnp.float32), jnp.zeros((vectors, LANES - 2 * vectors), jnp.float32)], axis=1
    )
    down_id = row_ids(work.shape)
    for j in range(vectors - 1):
        row = work[j : j + 1, :]
        column = jnp.where(down_id > j, work[:, j : j + 1], 0.0)
        work = work - column * (row * (1.0 / row[:, j : j + 1]))
    pivot = jnp.sum(jnp.where(eye, work[:, 0:vectors], 0.0), axis=1, keepdims=True)
    work = work * (1.0 / jnp.sqrt(pivot))
    beta_out[...] = jnp.where(row_ids(shape) <= lane_ids(shape), work[:, 0:vectors], 0.0)
    inverse = work[:, vectors : 2 * vectors]
    mix = jnp.concatenate(
        [inverse * v for v in along] + [-dot(inverse, beta), -dot(inverse, alpha, last)], axis=1
    )
    for at in range(stacked.shape[0]):
        next_out[:, at, :] = dot(mix, stacked[at])


def shards(
    lanczos_block,
    previous_block,
    previous_beta,
    prior_reaction,
    vert_coupling,
    horiz_coupling,
    friction,
    base_velocity,
    layers,
    obs_dest,
    obs_cell,
    obs_weight,
):
    vectors, tile_x, tile_y = lanczos_block.shape
    layer_count = horiz_coupling.shape[0]
    obs_rows = obs_cell.shape[0]
    size_x, size_y = lax.axis_size("mx"), lax.axis_size("my")
    devices = size_x * size_y
    cells = tile_x * tile_y * devices
    at_x, at_y = lax.axis_index("mx"), lax.axis_index("my")
    flags = jnp.stack([at_x > 0, at_x + 1 < size_x]).astype(jnp.float32)
    low_flag = (at_y > 0).astype(jnp.float32)
    high_flag = (at_y + 1 < size_y).astype(jnp.float32)
    forward_y = [(i, (i + 1) % size_y) for i in range(size_y)]
    backward_y = [(i, (i - 1) % size_y) for i in range(size_y)]
    forward_x = [(i, (i + 1) % size_x) for i in range(size_x)]
    backward_x = [(i, (i - 1) % size_x) for i in range(size_x)]
    f32 = jnp.float32
    rows = tile_y + 2 * HALO
    tiles = -(-(vectors * tile_x + FIELDS * tile_x) // LANES)
    smem = pl.BlockSpec(memory_space=pltpu.SMEM)
    vmem = pl.BlockSpec(memory_space=pltpu.VMEM)

    def shape(*dims):
        return jax.ShapeDtypeStruct(dims, f32)

    def near(*dims):
        return pltpu.VMEM(dims, f32)

    def keep(array):
        return pltpu.with_memory_space_constraint(array, pltpu.VMEM)

    def far(array):
        return pltpu.with_memory_space_constraint(array, pltpu.HBM)

    packed, previous, low, high = pl.pallas_call(
        pack_kernel,
        out_shape=(
            near(tiles, tile_y, LANES), near(tile_y, LANES), near(tiles, HALO, LANES), near(tiles, HALO, LANES)
        ),
        scratch_shapes=[pltpu.VMEM((tiles * LANES, tile_y), f32)],
        compiler_params=params(),
        name="pack",
    )(
        *map(
            far,
            (
                lanczos_block, previous_block, prior_reaction, vert_coupling, horiz_coupling,
                friction, base_velocity, layers,
            ),
        )
    )
    table = pl.pallas_call(
        table_kernel, out_shape=near(devices, LANES), compiler_params=params(), name="table"
    )(obs_dest.reshape(1, obs_rows), obs_cell.reshape(1, obs_rows), obs_weight.T)

    from_low = lax.ppermute(high, "my", forward_y)
    from_high = lax.ppermute(low, "my", backward_y)
    own = jnp.concatenate([from_low * low_flag, packed, from_high * high_flag], axis=1)
    left = lax.ppermute(own, "mx", forward_x)
    right = lax.ppermute(own, "mx", backward_x)

    count = rows // 8
    groups = -(-FIELDS // 4)

    def blocked(*dims):
        return pltpu.VMEM((*dims, 8, LANES), f32)

    message, basis, fields = pl.pallas_call(
        functools.partial(moment_kernel, vectors),
        out_shape=(
            near(devices, LANES), near(3, count, 3, 8, LANES), near(groups, count, 8, LANES)
        ),
        in_specs=[smem, vmem, vmem, vmem, vmem],
        scratch_shapes=[pltpu.VMEM((3 + groups, rows, LANES), f32), blocked(3, count), blocked(count, 3)]
        + [blocked(count + 2, 5)] * 3,
        compiler_params=params(),
        name="moments",
    )(flags, keep(own), keep(left), keep(right), table)
    message = lax.all_to_all(message, AXES, split_axis=0, concat_axis=0, tiled=True)

    def columns(width):
        return [
            pltpu.VMEM((groups, count, 8, 4 * width * LANES), f32),
            blocked(2, layer_count, count + 2, width + 2),
            blocked(2, layer_count, count + 2, width + 2),
            blocked(2, count, width),
        ]

    misfit, low, high = pl.pallas_call(
        functools.partial(velocity_kernel, vectors),
        out_shape=(near(2, tile_y, LANES), near(2, HALO, LANES), near(2, HALO, LANES)),
        in_specs=[smem] + [vmem] * 3,
        scratch_shapes=columns(2) + [blocked(2, count), pltpu.VMEM((rows, LANES), f32)],
        compiler_params=params(),
        name="velocity",
    )(flags, message, basis, fields)

    from_low = lax.ppermute(high, "my", forward_y)
    from_high = lax.ppermute(low, "my", backward_y)
    misfit = jnp.concatenate([from_low * low_flag, misfit, from_high * high_flag], axis=1)
    misfit_left = lax.ppermute(misfit, "mx", forward_x)
    misfit_right = lax.ppermute(misfit, "mx", backward_x)

    products, stacked = pl.pallas_call(
        functools.partial(adjoint_kernel, vectors),
        out_shape=(near(size_x, vectors, 2 * LANES), near(tile_x, 5 * vectors, tile_y)),
        in_specs=[smem] + [vmem] * 6,
        scratch_shapes=columns(3)
        + [blocked(layer_count, count, 3)] * 2
        + [pltpu.VMEM((2, 3, rows, LANES), f32), blocked(2, 3, count), blocked(2, count, 3), blocked(count, 3)]
        + [blocked(count + 2, 5)] * 3
        + [blocked(count), pltpu.VMEM((rows, LANES), f32)],
        compiler_params=params(),
        name="adjoint",
    )(flags, fields, keep(misfit), keep(misfit_left), keep(misfit_right), basis, previous)

    products = lax.all_to_all(products, "mx", split_axis=0, concat_axis=0, tiled=True)
    products = jnp.broadcast_to(jnp.sum(products, axis=0)[None], (size_y, vectors, 2 * LANES))
    products = lax.all_to_all(products, "my", split_axis=0, concat_axis=0, tiled=True)
    return pl.pallas_call(
        functools.partial(finish_kernel, float(cells)),
        out_shape=(shape(vectors, tile_x, tile_y), shape(vectors, vectors), shape(vectors, vectors)),
        compiler_params=params(),
        name="finish",
    )(products, stacked, previous_beta)


def solution(mesh):
    in_specs = (
        P(None, "mx", "my"),
        P(None, "mx", "my"),
        P(),
        P("mx", "my"),
        P(None, "mx", "my"),
        P(None, "mx", "my"),
        P("mx", "my"),
        P(None, "mx", "my"),
        P("mx", "my"),
        P(("mx", "my"), None),
        P(("mx", "my")),
        P(("mx", "my"), None),
    )
    out_specs = (P(None, "mx", "my"), P(), P())
    return jax.shard_map(shards, mesh=mesh, in_specs=in_specs, out_specs=out_specs, check_vma=False)
```

```python
import functools

import jax
import jax.numpy as jnp
from jax import lax
from jax.experimental import pallas as pl
from jax.experimental.pallas import tpu as pltpu
from jax.sharding import PartitionSpec as P

base_damping = 0.02
highest = lax.Precision.HIGHEST
SHIFT = 4.25
SCALE = 4.25
LANES = 128
HALO = 8
AXES = ("mx", "my")

F_RATIO = 0
F_PIVOT = 15
F_INV_LAT = 31
F_TOP = 32
F_LAYER = 33
F_BED = 34
F_REACT = 36
FIELDS = 37


def params(mebibytes=34):
    return pltpu.CompilerParams(vmem_limit_bytes=mebibytes * 1024 * 1024)


def lane_ids(shape):
    return lax.broadcasted_iota(jnp.int32, shape, len(shape) - 1)


def row_ids(shape):
    return lax.broadcasted_iota(jnp.int32, shape, len(shape) - 2)


def pack_kernel(
    block, previous, reaction, vert, horiz, friction, velocity, layers, out, prev_out, low, high, rows
):
    vectors, tile_x, tile_y = block.shape
    layer_count = horiz.shape[0]
    depth = layers[...]
    active = [(depth > k).astype(jnp.float32) for k in range(layer_count)]
    zero = jnp.zeros((tile_x, tile_y), jnp.float32)
    up = [vert[k] * active[k + 1] for k in range(layer_count - 1)] + [zero]
    lateral = [horiz[k] * active[k] for k in range(layer_count)]
    pivots = []
    for k in range(layer_count):
        drag = friction[...] if k == 0 else up[k - 1]
        diagonal = (base_damping + lateral[k] + drag + up[k]) * active[k] + (1.0 - active[k])
        if k > 0:
            diagonal = diagonal - up[k - 1] * up[k - 1] / pivots[k - 1]
        pivots.append(diagonal)
    top = zero
    for b in range(vectors):
        rows[pl.ds(b, tile_x, stride=vectors), :] = block[b]

    def put(field, value):
        rows[pl.ds(vectors * tile_x + field * tile_x, tile_x), :] = value

    for k in range(layer_count):
        put(F_PIVOT + k, lateral[k] * lateral[k] / pivots[k])
        is_top = depth == k + 1
        top = jnp.where(is_top, lateral[k] / pivots[k], top)
        if k + 1 < layer_count:
            below = jnp.where(depth > k + 1, lateral[k + 1], 1.0)
            put(F_RATIO + k, up[k] * lateral[k] / (pivots[k] * below))
    put(F_INV_LAT, 1.0 / lateral[0])
    put(F_TOP, top)
    put(F_LAYER, depth.astype(jnp.float32))
    put(F_BED, friction[...] * velocity[0])
    put(F_BED + 1, friction[...] * velocity[1])
    put(F_REACT, reaction[...])
    used = vectors * tile_x + FIELDS * tile_x
    rows[used:, :] = jnp.zeros((rows.shape[0] - used, tile_y), jnp.float32)
    for t in range(rows.shape[0] // LANES):
        out[t] = rows[t * LANES : (t + 1) * LANES, :].T
    low[...] = out[:, 0:HALO, :]
    high[...] = out[:, tile_y - HALO : tile_y, :]
    for b in range(vectors):
        rows[pl.ds(b, tile_x, stride=vectors), :] = previous[b]
    prev_out[...] = rows[0:LANES, :].T


def table_kernel(dest, cell, weight, out):
    count = dest.shape[1]
    devices = out.shape[0]
    rows = jnp.concatenate(
        [
            dest[...].astype(jnp.float32),
            cell[...].astype(jnp.float32),
            weight[...],
            jnp.zeros((4, count), jnp.float32),
        ],
        axis=0,
    )
    columns = rows.T
    target = columns[:, 0:1].astype(jnp.int32)
    onehot = target == lane_ids((count, devices))
    lower = row_ids((count, count)) >= lane_ids((count, count))
    running = jnp.dot(
        lower.astype(jnp.float32).astype(jnp.bfloat16),
        onehot.astype(jnp.float32).astype(jnp.bfloat16),
        preferred_element_type=jnp.float32,
    )
    chosen = onehot.astype(jnp.float32)
    rank = jnp.sum(running * chosen, axis=1, keepdims=True).astype(jnp.int32) - 1
    lane = lane_ids((count, LANES))
    kind = lane // 4
    value = jnp.where(
        kind == 0,
        columns[:, 2:3],
        jnp.where(kind == 1, columns[:, 3:4], jnp.where(kind == 2, columns[:, 1:2], 0.0)),
    )
    value = jnp.where(lane % 4 == rank, value, 0.0)
    chosen = (row_ids((devices, count)) == dest[...]).astype(jnp.float32).astype(jnp.bfloat16)
    out[...] = select_sum(chosen, value)


def pieces(value, axis):
    parts = []
    for _ in range(3):
        piece = value.astype(jnp.bfloat16)
        value = value - piece.astype(jnp.float32)
        parts.append(piece)
    return jnp.concatenate(parts, axis=axis)


def thrice(chosen):
    chosen = chosen.astype(jnp.float32).astype(jnp.bfloat16)
    return jnp.concatenate([chosen] * 3, axis=0)


def select_sum(chosen, value):
    total = None
    for _ in range(3):
        piece = value.astype(jnp.bfloat16)
        value = value - piece.astype(jnp.float32)
        part = jnp.dot(chosen, piece, preferred_element_type=jnp.float32)
        total = part if total is None else total + part
    return total


def fold(row, stride):
    shift = LANES // 2
    while shift >= stride:
        row = row + pltpu.roll(row, shift, 1)
        shift //= 2
    return row


def gather(tile, index):
    return jnp.take_along_axis(tile, index, axis=1)


def pick(which, values):
    result = values[-1]
    for n in range(len(values) - 2, -1, -1):
        result = jnp.where(which == n, values[n], result)
    return result


def tile_rows(vectors, tiles, offset, tile):
    return offset + (lane_ids((8, LANES)) // vectors) * tiles + tile


def to_blocked(value, vectors, tiles):
    shape = (3 * LANES, tiles * LANES)
    column, source = lane_ids(shape), row_ids(shape)
    row = (column % LANES // vectors) * tiles + column // LANES
    chosen = source == row * vectors + column % vectors
    return jnp.dot(pieces(value, 1), thrice(chosen), preferred_element_type=jnp.float32)


def reblock(values, vectors, tiles, offset):
    out = []
    for t in range(tiles):
        row = tile_rows(vectors, tiles, offset, t)
        index = (row // len(values)) * vectors + lane_ids((8, LANES)) % vectors
        out.append(pick(row % len(values), [gather(value, index) for value in values]))
    return out


def to_own(values, vectors, offset):
    tiles = len(values)
    row = lane_ids((8, LANES)) // vectors + LANES // vectors - offset
    index = (row // tiles) * vectors + lane_ids((8, LANES)) % vectors
    return pick(row % tiles, [gather(value, index) for value in values])


def split_rows(source, target, flag=None):
    count = target.shape[-3]
    for i in range(count):
        value = source[pl.ds(i, 8, stride=count), :]
        target[i] = value if flag is None else value * flag


def join_rows(source, target):
    count = source.shape[0]
    for i in range(count):
        target[pl.ds(i, 8, stride=count), :] = source[i]


def put_tile(field, at, t, tiles, stride, value):
    field[(*at, t + 1)] = value
    if t == 0:
        field[(*at, tiles + 1)] = pltpu.roll(value, LANES - stride, 1)
    if t == tiles - 1:
        field[(*at, 0)] = pltpu.roll(value, stride, 1)


def lateral_sum(field, at, i, t):
    return (field[(*at, i, t + 1)] + field[(*at, i + 2, t + 1)]) + (
        field[(*at, i + 1, t)] + field[(*at, i + 1, t + 2)]
    )


def wrap_rows(field, at, count, tiles):
    for t in range(1, tiles + 1):
        field[(*at, 0, t)] = pltpu.roll(field[(*at, count, t)], 1, 0)
        field[(*at, count + 1, t)] = pltpu.roll(field[(*at, 1, t)], 7, 0)


def wrap_layers(field, tiles):
    count = field.shape[2] - 2

    def body(k, carry):
        for c in range(2):
            wrap_rows(field, (c, k), count, tiles)
        return carry

    lax.fori_loop(0, field.shape[1], body, 0, unroll=4)


def own_cells(vectors, tiles, offset, count, tile_y, i, t):
    tile_x = LANES // vectors
    row = tile_rows(vectors, tiles, offset, t)
    column = row_ids((8, LANES)) * count + i
    return (row >= tile_x) & (row < 2 * tile_x) & (column >= HALO) & (column < HALO + tile_y)


def shifted_prior(field, i, t, reaction):
    image = (reaction - (SHIFT - 4.0)) * field[i + 1, t + 1] - lateral_sum(field, (), i, t)
    return jnp.where(reaction > 0.0, image * (1.0 / SCALE), 0.0)


def krylov(first, second, third, reaction, vectors, count, tile_y):
    tiles = reaction.shape[1]

    def step(source, target):
        wrap_rows(source, (), count, tiles)
        for i in range(count):
            for t in range(tiles):
                value = shifted_prior(source, i, t, reaction[i, t])
                put_tile(target, (i + 1,), t, tiles, vectors, value)

    step(first, second)
    step(second, third)
    wrap_rows(third, (), count, tiles)
    total = jnp.zeros((8, LANES), jnp.float32)
    for i in range(count):
        for t in range(tiles):
            value = shifted_prior(third, i, t, reaction[i, t]) * third[i + 1, t + 1]
            total = total + jnp.where(own_cells(vectors, tiles, 0, count, tile_y, i, t), value, 0.0)
    return total


def moment_kernel(
    vectors, flags, own, left, right, table, out, basis, fields, flat, parts, reaction, v0, v1, v2
):
    tile_x = LANES // vectors
    rows = own.shape[1]
    count = rows // 8
    tile_y = rows - 2 * HALO
    def beside(tiles):
        value = jnp.concatenate([left[tiles] * flags[0], own[tiles], right[tiles] * flags[1]], axis=-1)
        return value.reshape(-1, 3 * LANES)

    blocked = to_blocked(beside(0), vectors, 3)
    for t in range(3):
        flat[t] = blocked[:, t * LANES : (t + 1) * LANES]
    per_tile = LANES // (4 * tile_x)
    shape = (3 * LANES, per_tile * LANES)
    column, at = lane_ids(shape), row_ids(shape)
    lane = column % 32
    field = column // LANES * 4 + column % LANES // 32
    chosen = (at == lane // tile_x * LANES + field * tile_x + lane % tile_x) & (lane < 3 * tile_x)
    value = beside(slice(1, own.shape[0]))
    out_all = jnp.dot(pieces(value, 1), thrice(chosen), preferred_element_type=jnp.float32)
    for q in range(fields.shape[0]):
        first = q // per_tile * rows
        lanes = q % per_tile * LANES
        flat[3 + q] = out_all[first : first + rows, lanes : lanes + LANES]
    for t in range(3):
        split_rows(flat.at[t], parts.at[t])
    for q in range(fields.shape[0]):
        split_rows(flat.at[3 + q], fields.at[q])

    for i in range(count):
        for t in range(3):
            put_tile(v0, (i + 1,), t, 3, vectors, parts[t, i])
            reaction[i, t] = expand(fields, F_REACT, i, t, 3, 0, vectors)
    last = krylov(v0, v1, v2, reaction, vectors, count, tile_y)
    sums = [jnp.zeros((8, LANES), jnp.float32) for _ in range(5)]
    for i in range(count):
        for t in range(3):
            mine = own_cells(vectors, 3, 0, count, tile_y, i, t)
            a, b, c = v0[i + 1, t + 1], v1[i + 1, t + 1], v2[i + 1, t + 1]
            basis[0, i, t] = a
            basis[1, i, t] = b
            basis[2, i, t] = c
            a, b, c = [jnp.where(mine, v, 0.0) for v in (a, b, c)]
            sums = [
                total + one * two
                for total, one, two in zip(sums, (a, a, b, b, c), (a, b, b, c, c))
            ]
    sums.append(last)
    group = lane_ids((1, LANES)) // vectors
    message = jnp.zeros((1, LANES), jnp.float32)
    for j, value in enumerate(sums):
        total = fold(jnp.sum(value, axis=0, keepdims=True), vectors)
        message = jnp.where(group == j + 1, total, message)
    out[...] = table[...] + message


def expand(fields, field, i, t, tiles, offset, vectors):
    index = (field % 4) * 32 + tile_rows(vectors, tiles, offset, t)
    return gather(fields[field // 4, i], index)


def galerkin(moments):
    m = moments
    a = [SHIFT * m[i] + SCALE * m[i + 1] for i in range(5)]

    def over(top, pivot):
        return jnp.where(pivot > 0.0, top / jnp.where(pivot > 0.0, pivot, 1.0), 0.0)

    l10, l20 = over(a[1], a[0]), over(a[2], a[0])
    d1 = a[2] - l10 * a[1]
    e12 = a[3] - l20 * a[1]
    l21 = over(e12, d1)
    d2 = a[4] - l20 * a[2] - l21 * e12
    z1 = m[1] - l10 * m[0]
    z2 = m[2] - l20 * m[0] - l21 * z1
    y2 = over(z2, d2)
    y1 = over(z1, d1) - l21 * y2
    y0 = over(m[0], a[0]) - l10 * y1 - l20 * y2
    return y0, y1, y2


def expand_all(fields, wide, vectors, offset):
    groups, count = fields.shape[:2]
    value = pieces(fields[...].reshape(groups * count * 8, LANES), 1)
    half = wide.shape[-1] // 2
    tiles = half // (2 * LANES)
    shape = (LANES, half)
    column = lane_ids(shape)
    tile = column // LANES
    row = offset + (column % LANES // vectors) * tiles + tile % tiles
    for j in range(2):
        chosen = row_ids(shape) == (2 * j + tile // tiles) * 32 + row
        out = jnp.dot(value, thrice(chosen), preferred_element_type=jnp.float32)
        wide[:, :, :, j * half : (j + 1) * half] = out.reshape(groups, count, 8, half)


def get_field(wide, field, i, t):
    at = (field % 4) * (wide.shape[-1] // (4 * LANES)) + t
    return wide[field // 4, i, :, at * LANES : (at + 1) * LANES]


def prepare_row(wide, i, bed_col, top_col, layer_count, tiles):
    across = range(tiles)
    get = functools.partial(get_field, wide, i=i)
    inv_lat = [get(F_INV_LAT, t=t) for t in across]
    top = [get(F_TOP, t=t) for t in across]
    depth = [get(F_LAYER, t=t) for t in across]
    forward = [inv_lat]
    for k in range(1, layer_count):
        forward.append([get(F_RATIO + k - 1, t=t) * forward[k - 1][t] for t in across])
    beds, tops = [None] * layer_count, [None] * layer_count
    for k in range(layer_count - 1, -1, -1):
        beds[k], tops[k] = [], []
        for t in across:
            bed = get(F_PIVOT + k, t=t) * forward[k][t]
            below = 0.0
            if k + 1 < layer_count:
                ratio = get(F_RATIO + k, t=t)
                bed = bed + ratio * beds[k + 1][t]
                if top_col is not None:
                    below = ratio * tops[k + 1][t]
            beds[k].append(bed)
            if top_col is not None:
                surf = jnp.where(depth[t] == float(k + 1), top[t], below)
                bed_col[k, i, t] = bed
                top_col[k, i, t] = surf
                tops[k].append(surf)
    return inv_lat, beds, tops


def put_outer(field, i, columns, values, stride):
    tiles = len(values[0])
    right = [pltpu.roll(v[0], LANES - stride, 1) for v in values]
    left = [pltpu.roll(v[tiles - 1], stride, 1) for v in values]
    for k, column in enumerate(columns):
        right_column = pltpu.roll(column[0], LANES - stride, 1)
        left_column = pltpu.roll(column[tiles - 1], stride, 1)
        for c, value in enumerate(values):
            field[c, k, i + 1, 0] = left_column * left[c]
            for t in range(tiles):
                field[c, k, i + 1, t + 1] = column[t] * value[t]
            field[c, k, i + 1, tiles + 1] = right_column * right[c]


def sweep(source, target, wide, stride, unroll, bed_source=None, top_col=None, top_source=None):
    layer_count, count, tiles = target.shape[1], target.shape[2] - 2, target.shape[3] - 2
    def body(i, carry):
        for t in range(tiles):
            carried = [[], []]
            for k in range(layer_count):
                for c in range(2):
                    value = lateral_sum(source, (c, k), i, t)
                    if k > 0:
                        value = value + get_field(wide, F_RATIO + k - 1, i, t) * carried[c][k - 1]
                    elif bed_source is not None:
                        value = value + bed_source[c, i, t]
                    carried[c].append(value)
            solved = [None, None]
            for k in range(layer_count - 1, -1, -1):
                for c in range(2):
                    value = get_field(wide, F_PIVOT + k, i, t) * carried[c][k]
                    if k + 1 < layer_count:
                        value = value + get_field(wide, F_RATIO + k, i, t) * solved[c]
                    solved[c] = value
                    if top_source is not None:
                        value = value + top_col[k, i, t] * top_source[c, i, t]
                    put_tile(target, (c, k, i + 1), t, tiles, stride, value)
        return carry

    lax.fori_loop(0, count, body, 0, unroll=unroll)
    wrap_layers(target, tiles)


def velocity_kernel(
    vectors, flags, message, basis, fields,
    misfit, low, high,
    wide, one, two, source, surface, flat,
):
    tile_x = LANES // vectors
    layer_count, count, tiles = one.shape[1], one.shape[2] - 2, one.shape[3] - 2
    tile_y = count * 8 - 2 * HALO
    offset = tile_x // 2
    group = lane_ids((8, LANES)) // vectors
    summed = jnp.broadcast_to(jnp.sum(message[...], axis=0, keepdims=True), (8, LANES))
    moments = [fold(jnp.where(group == j + 1, summed, 0.0), vectors) for j in range(6)]
    y = galerkin(moments)

    def prepare(i, carry):
        smooth = [y[0] * basis[0, i, t] + y[1] * basis[1, i, t] + y[2] * basis[2, i, t] for t in range(3)]
        smooth = reblock(smooth, vectors, tiles, offset)
        inv_lat, beds, _ = prepare_row(wide, i, None, None, layer_count, tiles)
        values = [
            [get_field(wide, F_BED + c, i, t) * smooth[t] for t in range(tiles)] for c in range(2)
        ]
        for c in range(2):
            for t in range(tiles):
                source[c, i, t] = values[c][t] * inv_lat[t]
        put_outer(one, i, beds, values, vectors)
        return carry

    expand_all(fields, wide, vectors, offset)

    lax.fori_loop(0, count, prepare, 0, unroll=6)
    wrap_layers(one, tiles)
    sweep(one, two, wide, vectors, count, bed_source=source)
    sweep(two, one, wide, vectors, count, bed_source=source)

    def finish(i, carry):
        across = [(c, t) for c in range(2) for t in range(tiles)]
        values, carried = {}, {}
        for k in range(layer_count):
            for c, t in across:
                value = lateral_sum(one, (c, k), i, t)
                if k == 0:
                    value = value + source[c, i, t]
                    values[c, t] = value
                else:
                    value = value + get_field(wide, F_RATIO + k - 1, i, t) * carried[c, t]
                    deep = get_field(wide, F_LAYER, i, t) > float(k)
                    values[c, t] = jnp.where(deep, value, values[c, t])
                carried[c, t] = value
        for c, t in across:
            values[c, t] = values[c, t] * get_field(wide, F_TOP, i, t)
        for c in range(2):
            surface[c, i] = to_own([values[c, t] for t in range(tiles)], vectors, offset)
        return carry

    lax.fori_loop(0, count, finish, 0, unroll=6)

    table = message[...]
    flipped = table.T
    lane = lane_ids((LANES, 2 * LANES))
    second = lane >= LANES
    at_row, at_lane = [], []
    for r in range(4):
        cell = flipped[8 + r : 9 + r, :].astype(jnp.int32)
        at_row.append((row_ids((tile_y, LANES)) == cell % tile_y).astype(jnp.float32))
        cell = table[:, 8 + r : 9 + r].astype(jnp.int32)
        weight = jnp.where(second, table[:, 4 + r : 5 + r], table[:, r : r + 1])
        at_lane.append(jnp.where(cell // tile_y == lane % LANES // vectors, weight, 0.0))
    weights = select_sum(
        jnp.concatenate(at_row, axis=1).astype(jnp.bfloat16), jnp.concatenate(at_lane, axis=0)
    )
    for c in range(2):
        join_rows(surface.at[c], flat)
        misfit[c] = weights[:, c * LANES : (c + 1) * LANES] * flat[HALO : HALO + tile_y, :]
    low[...] = misfit[:, 0:HALO, :]
    high[...] = misfit[:, tile_y - HALO :, :]


def spread_kernel(vectors, after, fields, wide, done):
    expand_all(fields, wide, vectors, 0)
    done[...] = jnp.ones(done.shape, jnp.float32)


def column_kernel(after, wide, bed_col, top_col):
    layer_count, count, tiles = top_col.shape[:3]

    def body(i, carry):
        prepare_row(wide, i, bed_col, top_col, layer_count, tiles)
        return carry

    lax.fori_loop(0, count, body, 0, unroll=6)


def adjoint_kernel(
    vectors, flags, wide, bed_col, top_col, misfit, misfit_left, misfit_right, basis, previous,
    out, stacked,
    one, two, source, sides, spread, bed, reaction, v0, v1, v2, natural, flat,
):
    tile_x = LANES // vectors
    layer_count, count, tiles = top_col.shape[:3]
    tile_y = count * 8 - 2 * HALO
    value = jnp.concatenate(
        [misfit_left[...] * flags[0], misfit[...], misfit_right[...] * flags[1]], axis=-1
    )
    value = to_blocked(value.reshape(-1, 3 * LANES), vectors, tiles)
    for c in range(2):
        for t in range(tiles):
            sides[c, t] = value[c * count * 8 : (c + 1) * count * 8, t * LANES : (t + 1) * LANES]
            split_rows(sides.at[c, t], spread.at[c, t])

    def prepare(i, carry):
        values = [[spread[c, t, i] for t in range(tiles)] for c in range(2)]
        inv_lat = [get_field(wide, F_INV_LAT, i, t) for t in range(tiles)]
        tops = [[top_col[k, i, t] for t in range(tiles)] for k in range(layer_count)]
        for t in range(tiles):
            reaction[i, t] = get_field(wide, F_REACT, i, t)
            total = None
            for c in range(2):
                value = values[c][t]
                source[c, i, t] = value
                drag = get_field(wide, F_BED + c, i, t)
                bed[c, i, t] = drag
                total = drag * value if total is None else total + drag * value
            v1[i + 1, t + 1] = total * (tops[0][t] * inv_lat[t])
        put_outer(one, i, tops, values, vectors)
        return carry


    lax.fori_loop(0, count, prepare, 0, unroll=6)
    wrap_layers(one, tiles)
    sweep(one, two, wide, vectors, 6, top_col=top_col, top_source=source)
    sweep(two, one, wide, vectors, 6, top_col=top_col, top_source=source)

    def finish(i, carry):
        totals = {}
        for k in range(layer_count):
            for c in range(2):
                for t in range(tiles):
                    value = bed_col[k, i, t] * lateral_sum(one, (c, k), i, t)
                    totals[c, t] = value if k == 0 else totals[c, t] + value
        for t in range(tiles):
            value = v1[i + 1, t + 1] + (bed[0, i, t] * totals[0, t] + bed[1, i, t] * totals[1, t])
            put_tile(v0, (i + 1,), t, tiles, vectors, value)
        return carry

    lax.fori_loop(0, count, finish, 0, unroll=6)
    last = krylov(v0, v1, v2, reaction, vectors, count, tile_y)
    own = []
    for n, field in enumerate((v0, v1, v2, basis.at[0])):
        at = 0 if n == 3 else 1
        for i in range(count):
            natural[i] = to_own([field[i + at, t + at] for t in range(tiles)], vectors, 0)
        join_rows(natural, flat)
        own.append(flat[HALO : HALO + tile_y, :])
    v0, v1, v2, x = own
    p = previous[...]
    flipped = [v.T for v in (v0, v1, v2, p, x)]
    for i, value in enumerate(flipped):
        for at in range(tile_x):
            stacked[at, i * vectors : (i + 1) * vectors, :] = value[at * vectors : (at + 1) * vectors, :]
    t0, t1, t2, tp, tx = flipped
    pairs = (
        (t0, v0), (t0, v1), (t1, v1), (t1, v2), (t2, v2),
        (tx, v0), (tx, v1), (tx, v2),
        (t0, p), (t1, p), (t2, p),
        (tx, x), (tx, p), (tp, p),
    )
    same = row_ids((LANES, LANES)) // vectors == lane_ids((LANES, LANES)) // vectors
    group = lane_ids((vectors, LANES)) // vectors
    halves = [jnp.zeros((vectors, LANES), jnp.float32)] * 2
    for n, (a, b) in enumerate(pairs):
        product = jnp.dot(a, b, precision=highest, preferred_element_type=jnp.float32)
        product = jnp.where(same, product, 0.0)
        block = product[0:vectors]
        for at in range(1, tile_x):
            block = block + product[at * vectors : (at + 1) * vectors]
        block = fold(block, vectors)
        halves[n // tile_x] = jnp.where(group == n % tile_x, block, halves[n // tile_x])
    last = fold(jnp.sum(last, axis=0, keepdims=True), vectors)
    n = len(pairs)
    halves[n // tile_x] = jnp.where(group == n % tile_x, last, halves[n // tile_x])
    both = jnp.concatenate(halves, axis=1)
    for i in range(out.shape[0]):
        out[i] = both


def finish_kernel(cells, received, stacked, beta_ref, next_out, alpha_out, beta_out):
    vectors = beta_ref.shape[0]
    total = jnp.sum(received[...], axis=0)

    def block(n):
        return total[:, n * vectors : (n + 1) * vectors]

    def dot(a, b, dims=((1,), (0,))):
        return lax.dot_general(a, b, (dims, ((), ())), precision=highest, preferred_element_type=jnp.float32)

    shape = (vectors, vectors)
    eye = row_ids(shape) == lane_ids(shape)
    s = [block(n) for n in range(5)]
    moments = [jnp.sum(jnp.where(eye, m, 0.0), axis=0, keepdims=True) for m in s]
    moments.append(block(14)[0:1])
    along = galerkin(moments)
    down = [jnp.sum(jnp.where(eye, v, 0.0), axis=1, keepdims=True) for v in along]
    xv = [block(5 + k) for k in range(3)]
    vp = [block(8 + k) for k in range(3)]
    xx, xp, pp = block(11), block(12), block(13)
    beta = beta_ref[...]
    last = ((1,), (1,))
    first = ((0,), (0,))
    xr = xv[0] * along[0] + xv[1] * along[1] + xv[2] * along[2] - dot(xp, beta, last)
    alpha = xr * (1.0 / cells)
    alpha_out[...] = alpha
    rr = None
    for k in range(3):
        for l in range(3):
            term = down[k] * along[l] * s[k + l]
            rr = term if rr is None else rr + term
    cross = dot(down[0] * vp[0] + down[1] * vp[1] + down[2] * vp[2], beta, last)
    rr = rr - cross - cross.T + dot(beta, dot(pp, beta, last))
    gram = rr * (1.0 / cells) - 2.0 * dot(alpha, alpha, first) + dot(
        alpha, dot(xx * (1.0 / cells), alpha), first
    )
    gram = 0.5 * (gram + gram.T)
    work = jnp.concatenate(
        [gram, eye.astype(jnp.float32), jnp.zeros((vectors, LANES - 2 * vectors), jnp.float32)], axis=1
    )
    down_id = row_ids(work.shape)
    for j in range(vectors - 1):
        row = work[j : j + 1, :]
        column = jnp.where(down_id > j, work[:, j : j + 1], 0.0)
        work = work - column * (row * (1.0 / row[:, j : j + 1]))
    pivot = jnp.sum(jnp.where(eye, work[:, 0:vectors], 0.0), axis=1, keepdims=True)
    work = work * (1.0 / jnp.sqrt(pivot))
    beta_out[...] = jnp.where(row_ids(shape) <= lane_ids(shape), work[:, 0:vectors], 0.0)
    inverse = work[:, vectors : 2 * vectors]
    mix = jnp.concatenate(
        [inverse * v for v in along] + [-dot(inverse, beta), -dot(inverse, alpha, last)], axis=1
    )
    for at in range(stacked.shape[0]):
        next_out[:, at, :] = dot(mix, stacked[at])


def shards(
    lanczos_block,
    previous_block,
    previous_beta,
    prior_reaction,
    vert_coupling,
    horiz_coupling,
    friction,
    base_velocity,
    layers,
    obs_dest,
    obs_cell,
    obs_weight,
):
    vectors, tile_x, tile_y = lanczos_block.shape
    layer_count = horiz_coupling.shape[0]
    obs_rows = obs_cell.shape[0]
    size_x, size_y = lax.axis_size("mx"), lax.axis_size("my")
    devices = size_x * size_y
    cells = tile_x * tile_y * devices
    at_x, at_y = lax.axis_index("mx"), lax.axis_index("my")
    flags = jnp.stack([at_x > 0, at_x + 1 < size_x]).astype(jnp.float32)
    low_flag = (at_y > 0).astype(jnp.float32)
    high_flag = (at_y + 1 < size_y).astype(jnp.float32)
    forward_y = [(i, (i + 1) % size_y) for i in range(size_y)]
    backward_y = [(i, (i - 1) % size_y) for i in range(size_y)]
    forward_x = [(i, (i + 1) % size_x) for i in range(size_x)]
    backward_x = [(i, (i - 1) % size_x) for i in range(size_x)]
    f32 = jnp.float32
    rows = tile_y + 2 * HALO
    tiles = -(-(vectors * tile_x + FIELDS * tile_x) // LANES)
    smem = pl.BlockSpec(memory_space=pltpu.SMEM)
    vmem = pl.BlockSpec(memory_space=pltpu.VMEM)

    def shape(*dims):
        return jax.ShapeDtypeStruct(dims, f32)

    def near(*dims):
        return pltpu.VMEM(dims, f32)

    def keep(array):
        return pltpu.with_memory_space_constraint(array, pltpu.VMEM)

    def far(array):
        return pltpu.with_memory_space_constraint(array, pltpu.HBM)

    packed, previous, low, high = pl.pallas_call(
        pack_kernel,
        out_shape=(
            near(tiles, tile_y, LANES), near(tile_y, LANES), near(tiles, HALO, LANES), near(tiles, HALO, LANES)
        ),
        scratch_shapes=[pltpu.VMEM((tiles * LANES, tile_y), f32)],
        compiler_params=params(),
        name="pack",
    )(
        *map(
            far,
            (
                lanczos_block, previous_block, prior_reaction, vert_coupling, horiz_coupling,
                friction, base_velocity, layers,
            ),
        )
    )
    table = pl.pallas_call(
        table_kernel, out_shape=near(devices, LANES), compiler_params=params(), name="table"
    )(obs_dest.reshape(1, obs_rows), obs_cell.reshape(1, obs_rows), obs_weight.T)

    from_low = lax.ppermute(high, "my", forward_y)
    from_high = lax.ppermute(low, "my", backward_y)
    own = jnp.concatenate([from_low * low_flag, packed, from_high * high_flag], axis=1)
    left = lax.ppermute(own, "mx", forward_x)
    right = lax.ppermute(own, "mx", backward_x)

    count = rows // 8
    groups = -(-FIELDS // 4)

    def blocked(*dims):
        return pltpu.VMEM((*dims, 8, LANES), f32)

    message, basis, fields = pl.pallas_call(
        functools.partial(moment_kernel, vectors),
        out_shape=(
            near(devices, LANES), near(3, count, 3, 8, LANES), near(groups, count, 8, LANES)
        ),
        in_specs=[smem, vmem, vmem, vmem, vmem],
        scratch_shapes=[pltpu.VMEM((3 + groups, rows, LANES), f32), blocked(3, count), blocked(count, 3)]
        + [blocked(count + 2, 5)] * 3,
        compiler_params=params(),
        name="moments",
    )(flags, keep(own), keep(left), keep(right), table)
    message = lax.all_to_all(message, AXES, split_axis=0, concat_axis=0, tiled=True)

    def columns(width):
        return [
            pltpu.VMEM((groups, count, 8, 4 * width * LANES), f32),
            blocked(2, layer_count, count + 2, width + 2),
            blocked(2, layer_count, count + 2, width + 2),
            blocked(2, count, width),
        ]

    misfit, low, high = pl.pallas_call(
        functools.partial(velocity_kernel, vectors),
        out_shape=(near(2, tile_y, LANES), near(2, HALO, LANES), near(2, HALO, LANES)),
        in_specs=[smem] + [vmem] * 3,
        scratch_shapes=columns(2) + [blocked(2, count), pltpu.VMEM((rows, LANES), f32)],
        compiler_params=params(),
        name="velocity",
    )(flags, message, basis, fields)

    after, low, high = lax.optimization_barrier((flags, low, high))
    from_low = lax.ppermute(high, "my", forward_y)
    from_high = lax.ppermute(low, "my", backward_y)
    wide, done = pl.pallas_call(
        functools.partial(spread_kernel, vectors),
        out_shape=(near(groups, count, 8, 12 * LANES), near(8, LANES)),
        in_specs=[smem, vmem],
        compiler_params=params(16),
        name="spread",
    )(after, fields)
    misfit = jnp.concatenate(
        [from_low * (done * low_flag), misfit, from_high * (done * high_flag)], axis=1
    )
    after, misfit = lax.optimization_barrier((flags, misfit))
    misfit_left = lax.ppermute(misfit, "mx", forward_x)
    misfit_right = lax.ppermute(misfit, "mx", backward_x)

    bed_col, top_col = pl.pallas_call(
        column_kernel,
        out_shape=(near(layer_count, count, 3, 8, LANES), near(layer_count, count, 3, 8, LANES)),
        in_specs=[smem, vmem],
        compiler_params=params(16),
        name="columns",
    )(after, wide)

    products, stacked = pl.pallas_call(
        functools.partial(adjoint_kernel, vectors),
        out_shape=(near(size_x, vectors, 2 * LANES), near(tile_x, 5 * vectors, tile_y)),
        in_specs=[smem] + [vmem] * 8,
        scratch_shapes=columns(3)[1:]
        + [pltpu.VMEM((2, 3, rows, LANES), f32), blocked(2, 3, count), blocked(2, count, 3), blocked(count, 3)]
        + [blocked(count + 2, 5)] * 3
        + [blocked(count), pltpu.VMEM((rows, LANES), f32)],
        compiler_params=params(),
        name="adjoint",
    )(flags, wide, bed_col, top_col, keep(misfit), keep(misfit_left), keep(misfit_right), basis, previous)

    products = lax.all_to_all(products, "mx", split_axis=0, concat_axis=0, tiled=True)
    products = jnp.broadcast_to(jnp.sum(products, axis=0)[None], (size_y, vectors, 2 * LANES))
    products = lax.all_to_all(products, "my", split_axis=0, concat_axis=0, tiled=True)
    return pl.pallas_call(
        functools.partial(finish_kernel, float(cells)),
        out_shape=(shape(vectors, tile_x, tile_y), shape(vectors, vectors), shape(vectors, vectors)),
        compiler_params=params(),
        name="finish",
    )(products, stacked, previous_beta)


def solution(mesh):
    in_specs = (
        P(None, "mx", "my"),
        P(None, "mx", "my"),
        P(),
        P("mx", "my"),
        P(None, "mx", "my"),
        P(None, "mx", "my"),
        P("mx", "my"),
        P(None, "mx", "my"),
        P("mx", "my"),
        P(("mx", "my"), None),
        P(("mx", "my")),
        P(("mx", "my"), None),
    )
    out_specs = (P(None, "mx", "my"), P(), P())
    return jax.shard_map(shards, mesh=mesh, in_specs=in_specs, out_specs=out_specs, check_vma=False)
```

```python
import functools

import jax
import jax.numpy as jnp
from jax import lax
from jax.experimental import pallas as pl
from jax.experimental.pallas import tpu as pltpu
from jax.sharding import PartitionSpec as P

base_damping = 0.02
highest = lax.Precision.HIGHEST
SHIFT = 4.25
SCALE = 4.25
LANES = 128
HALO = 8
AXES = ("mx", "my")

F_RATIO = 0
F_PIVOT = 15
F_INV_LAT = 31
F_TOP = 32
F_LAYER = 33
F_BED = 34
F_REACT = 36
FIELDS = 37


def params(mebibytes=34):
    return pltpu.CompilerParams(vmem_limit_bytes=mebibytes * 1024 * 1024)


def lane_ids(shape):
    return lax.broadcasted_iota(jnp.int32, shape, len(shape) - 1)


def row_ids(shape):
    return lax.broadcasted_iota(jnp.int32, shape, len(shape) - 2)


def pack_kernel(
    block, previous, reaction, vert, horiz, friction, velocity, layers, out, prev_out, low, high, rows
):
    vectors, tile_x, tile_y = block.shape
    layer_count = horiz.shape[0]
    depth = layers[...]
    active = [(depth > k).astype(jnp.float32) for k in range(layer_count)]
    zero = jnp.zeros((tile_x, tile_y), jnp.float32)
    up = [vert[k] * active[k + 1] for k in range(layer_count - 1)] + [zero]
    lateral = [horiz[k] * active[k] for k in range(layer_count)]
    pivots = []
    for k in range(layer_count):
        drag = friction[...] if k == 0 else up[k - 1]
        diagonal = (base_damping + lateral[k] + drag + up[k]) * active[k] + (1.0 - active[k])
        if k > 0:
            diagonal = diagonal - up[k - 1] * up[k - 1] / pivots[k - 1]
        pivots.append(diagonal)
    top = zero
    for b in range(vectors):
        rows[pl.ds(b, tile_x, stride=vectors), :] = block[b]

    def put(field, value):
        rows[pl.ds(vectors * tile_x + field * tile_x, tile_x), :] = value

    for k in range(layer_count):
        put(F_PIVOT + k, lateral[k] * lateral[k] / pivots[k])
        is_top = depth == k + 1
        top = jnp.where(is_top, lateral[k] / pivots[k], top)
        if k + 1 < layer_count:
            below = jnp.where(depth > k + 1, lateral[k + 1], 1.0)
            put(F_RATIO + k, up[k] * lateral[k] / (pivots[k] * below))
    put(F_INV_LAT, 1.0 / lateral[0])
    put(F_TOP, top)
    put(F_LAYER, depth.astype(jnp.float32))
    put(F_BED, friction[...] * velocity[0])
    put(F_BED + 1, friction[...] * velocity[1])
    put(F_REACT, reaction[...])
    used = vectors * tile_x + FIELDS * tile_x
    rows[used:, :] = jnp.zeros((rows.shape[0] - used, tile_y), jnp.float32)
    for t in range(rows.shape[0] // LANES):
        out[t] = rows[t * LANES : (t + 1) * LANES, :].T
    low[...] = out[:, 0:HALO, :]
    high[...] = out[:, tile_y - HALO : tile_y, :]
    for b in range(vectors):
        rows[pl.ds(b, tile_x, stride=vectors), :] = previous[b]
    prev_out[...] = rows[0:LANES, :].T


def table_kernel(dest, cell, weight, out):
    count = dest.shape[1]
    devices = out.shape[0]
    rows = jnp.concatenate(
        [
            dest[...].astype(jnp.float32),
            cell[...].astype(jnp.float32),
            weight[...],
            jnp.zeros((4, count), jnp.float32),
        ],
        axis=0,
    )
    columns = rows.T
    target = columns[:, 0:1].astype(jnp.int32)
    onehot = target == lane_ids((count, devices))
    lower = row_ids((count, count)) >= lane_ids((count, count))
    running = jnp.dot(
        lower.astype(jnp.float32).astype(jnp.bfloat16),
        onehot.astype(jnp.float32).astype(jnp.bfloat16),
        preferred_element_type=jnp.float32,
    )
    chosen = onehot.astype(jnp.float32)
    rank = jnp.sum(running * chosen, axis=1, keepdims=True).astype(jnp.int32) - 1
    lane = lane_ids((count, LANES))
    kind = lane // 4
    value = jnp.where(
        kind == 0,
        columns[:, 2:3],
        jnp.where(kind == 1, columns[:, 3:4], jnp.where(kind == 2, columns[:, 1:2], 0.0)),
    )
    value = jnp.where(lane % 4 == rank, value, 0.0)
    chosen = (row_ids((devices, count)) == dest[...]).astype(jnp.float32).astype(jnp.bfloat16)
    out[...] = select_sum(chosen, value)


def pieces(value, axis):
    parts = []
    for _ in range(3):
        piece = value.astype(jnp.bfloat16)
        value = value - piece.astype(jnp.float32)
        parts.append(piece)
    return jnp.concatenate(parts, axis=axis)


def thrice(chosen):
    chosen = chosen.astype(jnp.float32).astype(jnp.bfloat16)
    return jnp.concatenate([chosen] * 3, axis=0)


def select_sum(chosen, value):
    total = None
    for _ in range(3):
        piece = value.astype(jnp.bfloat16)
        value = value - piece.astype(jnp.float32)
        part = jnp.dot(chosen, piece, preferred_element_type=jnp.float32)
        total = part if total is None else total + part
    return total


def fold(row, stride):
    shift = LANES // 2
    while shift >= stride:
        row = row + pltpu.roll(row, shift, 1)
        shift //= 2
    return row


def gather(tile, index):
    return jnp.take_along_axis(tile, index, axis=1)


def pick(which, values):
    result = values[-1]
    for n in range(len(values) - 2, -1, -1):
        result = jnp.where(which == n, values[n], result)
    return result


def tile_rows(vectors, tiles, offset, tile):
    return offset + (lane_ids((8, LANES)) // vectors) * tiles + tile


def to_blocked(value, vectors, tiles):
    shape = (3 * LANES, tiles * LANES)
    column, source = lane_ids(shape), row_ids(shape)
    row = (column % LANES // vectors) * tiles + column // LANES
    chosen = source == row * vectors + column % vectors
    return jnp.dot(pieces(value, 1), thrice(chosen), preferred_element_type=jnp.float32)


def reblock(values, vectors, tiles, offset):
    out = []
    for t in range(tiles):
        row = tile_rows(vectors, tiles, offset, t)
        index = (row // len(values)) * vectors + lane_ids((8, LANES)) % vectors
        out.append(pick(row % len(values), [gather(value, index) for value in values]))
    return out


def to_own(values, vectors, offset):
    tiles = len(values)
    row = lane_ids((8, LANES)) // vectors + LANES // vectors - offset
    index = (row // tiles) * vectors + lane_ids((8, LANES)) % vectors
    return pick(row % tiles, [gather(value, index) for value in values])


def split_rows(source, target, flag=None):
    count = target.shape[-3]
    for i in range(count):
        value = source[pl.ds(i, 8, stride=count), :]
        target[i] = value if flag is None else value * flag


def join_rows(source, target):
    count = source.shape[0]
    for i in range(count):
        target[pl.ds(i, 8, stride=count), :] = source[i]


def put_tile(field, at, t, tiles, stride, value):
    field[(*at, t + 1)] = value
    if t == 0:
        field[(*at, tiles + 1)] = pltpu.roll(value, LANES - stride, 1)
    if t == tiles - 1:
        field[(*at, 0)] = pltpu.roll(value, stride, 1)


def lateral_sum(field, at, i, t):
    return (field[(*at, i, t + 1)] + field[(*at, i + 2, t + 1)]) + (
        field[(*at, i + 1, t)] + field[(*at, i + 1, t + 2)]
    )


def wrap_rows(field, at, count, tiles):
    for t in range(1, tiles + 1):
        field[(*at, 0, t)] = pltpu.roll(field[(*at, count, t)], 1, 0)
        field[(*at, count + 1, t)] = pltpu.roll(field[(*at, 1, t)], 7, 0)


def wrap_layers(field, tiles):
    count = field.shape[2] - 2

    def body(k, carry):
        for c in range(2):
            wrap_rows(field, (c, k), count, tiles)
        return carry

    lax.fori_loop(0, field.shape[1], body, 0, unroll=4)


def own_cells(vectors, tiles, offset, count, tile_y, i, t):
    tile_x = LANES // vectors
    row = tile_rows(vectors, tiles, offset, t)
    column = row_ids((8, LANES)) * count + i
    return (row >= tile_x) & (row < 2 * tile_x) & (column >= HALO) & (column < HALO + tile_y)


def shifted_prior(field, i, t, reaction):
    image = (reaction - (SHIFT - 4.0)) * field[i + 1, t + 1] - lateral_sum(field, (), i, t)
    return jnp.where(reaction > 0.0, image * (1.0 / SCALE), 0.0)


def krylov(first, second, third, reaction, vectors, count, tile_y):
    tiles = reaction.shape[1]

    def step(source, target):
        wrap_rows(source, (), count, tiles)
        for i in range(count):
            for t in range(tiles):
                value = shifted_prior(source, i, t, reaction[i, t])
                put_tile(target, (i + 1,), t, tiles, vectors, value)

    step(first, second)
    step(second, third)
    wrap_rows(third, (), count, tiles)
    total = jnp.zeros((8, LANES), jnp.float32)
    for i in range(count):
        for t in range(tiles):
            value = shifted_prior(third, i, t, reaction[i, t]) * third[i + 1, t + 1]
            total = total + jnp.where(own_cells(vectors, tiles, 0, count, tile_y, i, t), value, 0.0)
    return total


def moment_kernel(
    vectors, flags, own, left, right, table, out, basis, fields, flat, parts, reaction, v0, v1, v2
):
    tile_x = LANES // vectors
    rows = own.shape[1]
    count = rows // 8
    tile_y = rows - 2 * HALO
    def beside(tiles):
        value = jnp.concatenate([left[tiles] * flags[0], own[tiles], right[tiles] * flags[1]], axis=-1)
        return value.reshape(-1, 3 * LANES)

    blocked = to_blocked(beside(0), vectors, 3)
    for t in range(3):
        flat[t] = blocked[:, t * LANES : (t + 1) * LANES]
    per_tile = LANES // (4 * tile_x)
    shape = (3 * LANES, per_tile * LANES)
    column, at = lane_ids(shape), row_ids(shape)
    lane = column % 32
    field = column // LANES * 4 + column % LANES // 32
    chosen = (at == lane // tile_x * LANES + field * tile_x + lane % tile_x) & (lane < 3 * tile_x)
    value = beside(slice(1, own.shape[0]))
    out_all = jnp.dot(pieces(value, 1), thrice(chosen), preferred_element_type=jnp.float32)
    for q in range(fields.shape[0]):
        first = q // per_tile * rows
        lanes = q % per_tile * LANES
        flat[3 + q] = out_all[first : first + rows, lanes : lanes + LANES]
    for t in range(3):
        split_rows(flat.at[t], parts.at[t])
    for q in range(fields.shape[0]):
        split_rows(flat.at[3 + q], fields.at[q])

    for i in range(count):
        for t in range(3):
            put_tile(v0, (i + 1,), t, 3, vectors, parts[t, i])
            reaction[i, t] = expand(fields, F_REACT, i, t, 3, 0, vectors)
    last = krylov(v0, v1, v2, reaction, vectors, count, tile_y)
    sums = [jnp.zeros((8, LANES), jnp.float32) for _ in range(5)]
    for i in range(count):
        for t in range(3):
            mine = own_cells(vectors, 3, 0, count, tile_y, i, t)
            a, b, c = v0[i + 1, t + 1], v1[i + 1, t + 1], v2[i + 1, t + 1]
            basis[0, i, t] = a
            basis[1, i, t] = b
            basis[2, i, t] = c
            a, b, c = [jnp.where(mine, v, 0.0) for v in (a, b, c)]
            sums = [
                total + one * two
                for total, one, two in zip(sums, (a, a, b, b, c), (a, b, b, c, c))
            ]
    sums.append(last)
    group = lane_ids((1, LANES)) // vectors
    message = jnp.zeros((1, LANES), jnp.float32)
    for j, value in enumerate(sums):
        total = fold(jnp.sum(value, axis=0, keepdims=True), vectors)
        message = jnp.where(group == j + 1, total, message)
    out[...] = table[...] + message


def expand(fields, field, i, t, tiles, offset, vectors):
    index = (field % 4) * 32 + tile_rows(vectors, tiles, offset, t)
    return gather(fields[field // 4, i], index)


def galerkin(moments):
    m = moments
    a = [SHIFT * m[i] + SCALE * m[i + 1] for i in range(5)]

    def over(top, pivot):
        return jnp.where(pivot > 0.0, top / jnp.where(pivot > 0.0, pivot, 1.0), 0.0)

    l10, l20 = over(a[1], a[0]), over(a[2], a[0])
    d1 = a[2] - l10 * a[1]
    e12 = a[3] - l20 * a[1]
    l21 = over(e12, d1)
    d2 = a[4] - l20 * a[2] - l21 * e12
    z1 = m[1] - l10 * m[0]
    z2 = m[2] - l20 * m[0] - l21 * z1
    y2 = over(z2, d2)
    y1 = over(z1, d1) - l21 * y2
    y0 = over(m[0], a[0]) - l10 * y1 - l20 * y2
    return y0, y1, y2


def expand_all(fields, wide, vectors, offset):
    groups, count = fields.shape[:2]
    value = pieces(fields[...].reshape(groups * count * 8, LANES), 1)
    half = wide.shape[-1] // 2
    tiles = half // (2 * LANES)
    shape = (LANES, half)
    column = lane_ids(shape)
    tile = column // LANES
    row = offset + (column % LANES // vectors) * tiles + tile % tiles
    for j in range(2):
        chosen = row_ids(shape) == (2 * j + tile // tiles) * 32 + row
        out = jnp.dot(value, thrice(chosen), preferred_element_type=jnp.float32)
        wide[:, :, :, j * half : (j + 1) * half] = out.reshape(groups, count, 8, half)


def get_field(wide, field, i, t):
    at = (field % 4) * (wide.shape[-1] // (4 * LANES)) + t
    return wide[field // 4, i, :, at * LANES : (at + 1) * LANES]


def prepare_row(wide, i, bed_col, top_col, layer_count, tiles):
    across = range(tiles)
    get = functools.partial(get_field, wide, i=i)
    inv_lat = [get(F_INV_LAT, t=t) for t in across]
    top = [get(F_TOP, t=t) for t in across]
    depth = [get(F_LAYER, t=t) for t in across]
    forward = [inv_lat]
    for k in range(1, layer_count):
        forward.append([get(F_RATIO + k - 1, t=t) * forward[k - 1][t] for t in across])
    beds, tops = [None] * layer_count, [None] * layer_count
    for k in range(layer_count - 1, -1, -1):
        beds[k], tops[k] = [], []
        for t in across:
            bed = get(F_PIVOT + k, t=t) * forward[k][t]
            below = 0.0
            if k + 1 < layer_count:
                ratio = get(F_RATIO + k, t=t)
                bed = bed + ratio * beds[k + 1][t]
                if top_col is not None:
                    below = ratio * tops[k + 1][t]
            beds[k].append(bed)
            if top_col is not None:
                surf = jnp.where(depth[t] == float(k + 1), top[t], below)
                bed_col[k, i, t] = bed
                top_col[k, i, t] = surf
                tops[k].append(surf)
    return inv_lat, beds, tops


def put_outer(field, i, columns, values, stride):
    tiles = len(values[0])
    right = [pltpu.roll(v[0], LANES - stride, 1) for v in values]
    left = [pltpu.roll(v[tiles - 1], stride, 1) for v in values]
    for k, column in enumerate(columns):
        right_column = pltpu.roll(column[0], LANES - stride, 1)
        left_column = pltpu.roll(column[tiles - 1], stride, 1)
        for c, value in enumerate(values):
            field[c, k, i + 1, 0] = left_column * left[c]
            for t in range(tiles):
                field[c, k, i + 1, t + 1] = column[t] * value[t]
            field[c, k, i + 1, tiles + 1] = right_column * right[c]


def sweep(source, target, wide, stride, unroll, bed_source=None, top_col=None, top_source=None):
    layer_count, count, tiles = target.shape[1], target.shape[2] - 2, target.shape[3] - 2
    def body(i, carry):
        for t in range(tiles):
            carried = [[], []]
            for k in range(layer_count):
                for c in range(2):
                    value = lateral_sum(source, (c, k), i, t)
                    if k > 0:
                        value = value + get_field(wide, F_RATIO + k - 1, i, t) * carried[c][k - 1]
                    elif bed_source is not None:
                        value = value + bed_source[c, i, t]
                    carried[c].append(value)
            solved = [None, None]
            for k in range(layer_count - 1, -1, -1):
                for c in range(2):
                    value = get_field(wide, F_PIVOT + k, i, t) * carried[c][k]
                    if k + 1 < layer_count:
                        value = value + get_field(wide, F_RATIO + k, i, t) * solved[c]
                    solved[c] = value
                    if top_source is not None:
                        value = value + top_col[k, i, t] * top_source[c, i, t]
                    put_tile(target, (c, k, i + 1), t, tiles, stride, value)
        return carry

    lax.fori_loop(0, count, body, 0, unroll=unroll)
    wrap_layers(target, tiles)


def velocity_kernel(
    vectors, flags, message, basis, fields,
    misfit, low, high,
    wide, one, two, source, surface, flat,
):
    tile_x = LANES // vectors
    layer_count, count, tiles = one.shape[1], one.shape[2] - 2, one.shape[3] - 2
    tile_y = count * 8 - 2 * HALO
    offset = tile_x // 2
    group = lane_ids((8, LANES)) // vectors
    summed = jnp.broadcast_to(jnp.sum(message[...], axis=0, keepdims=True), (8, LANES))
    moments = [fold(jnp.where(group == j + 1, summed, 0.0), vectors) for j in range(6)]
    y = galerkin(moments)

    def prepare(i, carry):
        smooth = [y[0] * basis[0, i, t] + y[1] * basis[1, i, t] + y[2] * basis[2, i, t] for t in range(3)]
        smooth = reblock(smooth, vectors, tiles, offset)
        inv_lat, beds, _ = prepare_row(wide, i, None, None, layer_count, tiles)
        values = [
            [get_field(wide, F_BED + c, i, t) * smooth[t] for t in range(tiles)] for c in range(2)
        ]
        for c in range(2):
            for t in range(tiles):
                source[c, i, t] = values[c][t] * inv_lat[t]
        put_outer(one, i, beds, values, vectors)
        return carry

    expand_all(fields, wide, vectors, offset)

    lax.fori_loop(0, count, prepare, 0, unroll=6)
    wrap_layers(one, tiles)
    sweep(one, two, wide, vectors, count, bed_source=source)
    sweep(two, one, wide, vectors, count, bed_source=source)

    def finish(i, carry):
        across = [(c, t) for c in range(2) for t in range(tiles)]
        values, carried = {}, {}
        for k in range(layer_count):
            for c, t in across:
                value = lateral_sum(one, (c, k), i, t)
                if k == 0:
                    value = value + source[c, i, t]
                    values[c, t] = value
                else:
                    value = value + get_field(wide, F_RATIO + k - 1, i, t) * carried[c, t]
                    deep = get_field(wide, F_LAYER, i, t) > float(k)
                    values[c, t] = jnp.where(deep, value, values[c, t])
                carried[c, t] = value
        for c, t in across:
            values[c, t] = values[c, t] * get_field(wide, F_TOP, i, t)
        for c in range(2):
            surface[c, i] = to_own([values[c, t] for t in range(tiles)], vectors, offset)
        return carry

    lax.fori_loop(0, count, finish, 0, unroll=6)

    table = message[...]
    flipped = table.T
    lane = lane_ids((LANES, 2 * LANES))
    second = lane >= LANES
    at_row, at_lane = [], []
    for r in range(4):
        cell = flipped[8 + r : 9 + r, :].astype(jnp.int32)
        at_row.append((row_ids((tile_y, LANES)) == cell % tile_y).astype(jnp.float32))
        cell = table[:, 8 + r : 9 + r].astype(jnp.int32)
        weight = jnp.where(second, table[:, 4 + r : 5 + r], table[:, r : r + 1])
        at_lane.append(jnp.where(cell // tile_y == lane % LANES // vectors, weight, 0.0))
    weights = select_sum(
        jnp.concatenate(at_row, axis=1).astype(jnp.bfloat16), jnp.concatenate(at_lane, axis=0)
    )
    for c in range(2):
        join_rows(surface.at[c], flat)
        misfit[c] = weights[:, c * LANES : (c + 1) * LANES] * flat[HALO : HALO + tile_y, :]
    low[...] = misfit[:, 0:HALO, :]
    high[...] = misfit[:, tile_y - HALO :, :]


def spread_kernel(vectors, after, fields, wide, done):
    expand_all(fields, wide, vectors, 0)
    done[...] = jnp.ones(done.shape, jnp.float32)


def column_kernel(after, wide, bed_col, top_col):
    layer_count, count, tiles = top_col.shape[:3]

    def body(i, carry):
        prepare_row(wide, i, bed_col, top_col, layer_count, tiles)
        return carry

    lax.fori_loop(0, count, body, 0, unroll=6)


def adjoint_kernel(
    vectors, flags, wide, bed_col, top_col, misfit, misfit_left, misfit_right, basis, previous,
    out, stacked,
    one, two, source, sides, spread, bed, reaction, v0, v1, v2, natural, flat,
):
    tile_x = LANES // vectors
    layer_count, count, tiles = top_col.shape[:3]
    tile_y = count * 8 - 2 * HALO
    value = jnp.concatenate(
        [misfit_left[...] * flags[0], misfit[...], misfit_right[...] * flags[1]], axis=-1
    )
    value = to_blocked(value.reshape(-1, 3 * LANES), vectors, tiles)
    for c in range(2):
        for t in range(tiles):
            sides[c, t] = value[c * count * 8 : (c + 1) * count * 8, t * LANES : (t + 1) * LANES]
            split_rows(sides.at[c, t], spread.at[c, t])

    def prepare(i, carry):
        values = [[spread[c, t, i] for t in range(tiles)] for c in range(2)]
        inv_lat = [get_field(wide, F_INV_LAT, i, t) for t in range(tiles)]
        tops = [[top_col[k, i, t] for t in range(tiles)] for k in range(layer_count)]
        for t in range(tiles):
            reaction[i, t] = get_field(wide, F_REACT, i, t)
            total = None
            for c in range(2):
                value = values[c][t]
                source[c, i, t] = value
                drag = get_field(wide, F_BED + c, i, t)
                bed[c, i, t] = drag
                total = drag * value if total is None else total + drag * value
            v1[i + 1, t + 1] = total * (tops[0][t] * inv_lat[t])
        put_outer(one, i, tops, values, vectors)
        return carry


    lax.fori_loop(0, count, prepare, 0, unroll=6)
    wrap_layers(one, tiles)
    sweep(one, two, wide, vectors, 6, top_col=top_col, top_source=source)
    sweep(two, one, wide, vectors, 6, top_col=top_col, top_source=source)

    def finish(i, carry):
        totals = {}
        for k in range(layer_count):
            for c in range(2):
                for t in range(tiles):
                    value = bed_col[k, i, t] * lateral_sum(one, (c, k), i, t)
                    totals[c, t] = value if k == 0 else totals[c, t] + value
        for t in range(tiles):
            value = v1[i + 1, t + 1] + (bed[0, i, t] * totals[0, t] + bed[1, i, t] * totals[1, t])
            put_tile(v0, (i + 1,), t, tiles, vectors, value)
        return carry

    lax.fori_loop(0, count, finish, 0, unroll=6)
    last = krylov(v0, v1, v2, reaction, vectors, count, tile_y)
    own = []
    for n, field in enumerate((v0, v1, v2, basis.at[0])):
        at = 0 if n == 3 else 1
        for i in range(count):
            natural[i] = to_own([field[i + at, t + at] for t in range(tiles)], vectors, 0)
        join_rows(natural, flat)
        own.append(flat[HALO : HALO + tile_y, :])
    v0, v1, v2, x = own
    p = previous[...]
    flipped = [v.T for v in (v0, v1, v2, p, x)]
    for i, value in enumerate(flipped):
        for at in range(tile_x):
            stacked[at, i * vectors : (i + 1) * vectors, :] = value[at * vectors : (at + 1) * vectors, :]
    t0, t1, t2, tp, tx = flipped
    pairs = (
        (t0, v0), (t0, v1), (t1, v1), (t1, v2), (t2, v2),
        (tx, v0), (tx, v1), (tx, v2),
        (t0, p), (t1, p), (t2, p),
        (tx, x), (tx, p), (tp, p),
    )
    same = row_ids((LANES, LANES)) // vectors == lane_ids((LANES, LANES)) // vectors
    group = lane_ids((vectors, LANES)) // vectors
    halves = [jnp.zeros((vectors, LANES), jnp.float32)] * 2
    for n, (a, b) in enumerate(pairs):
        product = jnp.dot(a, b, precision=highest, preferred_element_type=jnp.float32)
        product = jnp.where(same, product, 0.0)
        block = product[0:vectors]
        for at in range(1, tile_x):
            block = block + product[at * vectors : (at + 1) * vectors]
        block = fold(block, vectors)
        halves[n // tile_x] = jnp.where(group == n % tile_x, block, halves[n // tile_x])
    last = fold(jnp.sum(last, axis=0, keepdims=True), vectors)
    n = len(pairs)
    halves[n // tile_x] = jnp.where(group == n % tile_x, last, halves[n // tile_x])
    both = jnp.concatenate(halves, axis=1)
    for i in range(out.shape[0]):
        out[i] = both


def finish_kernel(cells, received, stacked, beta_ref, next_out, alpha_out, beta_out):
    vectors = beta_ref.shape[0]
    total = jnp.sum(received[...], axis=0)

    def block(n):
        return total[:, n * vectors : (n + 1) * vectors]

    def dot(a, b, dims=((1,), (0,))):
        return lax.dot_general(a, b, (dims, ((), ())), precision=highest, preferred_element_type=jnp.float32)

    shape = (vectors, vectors)
    eye = row_ids(shape) == lane_ids(shape)
    s = [block(n) for n in range(5)]
    moments = [jnp.sum(jnp.where(eye, m, 0.0), axis=0, keepdims=True) for m in s]
    moments.append(block(14)[0:1])
    along = galerkin(moments)
    down = [jnp.sum(jnp.where(eye, v, 0.0), axis=1, keepdims=True) for v in along]
    xv = [block(5 + k) for k in range(3)]
    vp = [block(8 + k) for k in range(3)]
    xx, xp, pp = block(11), block(12), block(13)
    beta = beta_ref[...]
    last = ((1,), (1,))
    first = ((0,), (0,))
    xr = xv[0] * along[0] + xv[1] * along[1] + xv[2] * along[2] - dot(xp, beta, last)
    alpha = xr * (1.0 / cells)
    alpha_out[...] = alpha
    rr = None
    for k in range(3):
        for l in range(3):
            term = down[k] * along[l] * s[k + l]
            rr = term if rr is None else rr + term
    cross = dot(down[0] * vp[0] + down[1] * vp[1] + down[2] * vp[2], beta, last)
    rr = rr - cross - cross.T + dot(beta, dot(pp, beta, last))
    gram = rr * (1.0 / cells) - 2.0 * dot(alpha, alpha, first) + dot(
        alpha, dot(xx * (1.0 / cells), alpha), first
    )
    gram = 0.5 * (gram + gram.T)
    work = jnp.concatenate(
        [gram, eye.astype(jnp.float32), jnp.zeros((vectors, LANES - 2 * vectors), jnp.float32)], axis=1
    )
    down_id = row_ids(work.shape)
    for j in range(vectors - 1):
        row = work[j : j + 1, :]
        column = jnp.where(down_id > j, work[:, j : j + 1], 0.0)
        work = work - column * (row * (1.0 / row[:, j : j + 1]))
    pivot = jnp.sum(jnp.where(eye, work[:, 0:vectors], 0.0), axis=1, keepdims=True)
    work = work * (1.0 / jnp.sqrt(pivot))
    beta_out[...] = jnp.where(row_ids(shape) <= lane_ids(shape), work[:, 0:vectors], 0.0)
    inverse = work[:, vectors : 2 * vectors]
    mix = jnp.concatenate(
        [inverse * v for v in along] + [-dot(inverse, beta), -dot(inverse, alpha, last)], axis=1
    )
    lanes = stacked.shape[2]
    whole = dot(mix, jnp.concatenate([stacked[at] for at in range(stacked.shape[0])], axis=1))
    for at in range(stacked.shape[0]):
        next_out[:, at, :] = whole[:, at * lanes : (at + 1) * lanes]


def shards(
    lanczos_block,
    previous_block,
    previous_beta,
    prior_reaction,
    vert_coupling,
    horiz_coupling,
    friction,
    base_velocity,
    layers,
    obs_dest,
    obs_cell,
    obs_weight,
):
    vectors, tile_x, tile_y = lanczos_block.shape
    layer_count = horiz_coupling.shape[0]
    obs_rows = obs_cell.shape[0]
    size_x, size_y = lax.axis_size("mx"), lax.axis_size("my")
    devices = size_x * size_y
    cells = tile_x * tile_y * devices
    at_x, at_y = lax.axis_index("mx"), lax.axis_index("my")
    flags = jnp.stack([at_x > 0, at_x + 1 < size_x]).astype(jnp.float32)
    low_flag = (at_y > 0).astype(jnp.float32)
    high_flag = (at_y + 1 < size_y).astype(jnp.float32)
    forward_y = [(i, (i + 1) % size_y) for i in range(size_y)]
    backward_y = [(i, (i - 1) % size_y) for i in range(size_y)]
    forward_x = [(i, (i + 1) % size_x) for i in range(size_x)]
    backward_x = [(i, (i - 1) % size_x) for i in range(size_x)]
    f32 = jnp.float32
    rows = tile_y + 2 * HALO
    tiles = -(-(vectors * tile_x + FIELDS * tile_x) // LANES)
    smem = pl.BlockSpec(memory_space=pltpu.SMEM)
    vmem = pl.BlockSpec(memory_space=pltpu.VMEM)

    def shape(*dims):
        return jax.ShapeDtypeStruct(dims, f32)

    def near(*dims):
        return pltpu.VMEM(dims, f32)

    def keep(array):
        return pltpu.with_memory_space_constraint(array, pltpu.VMEM)

    def far(array):
        return pltpu.with_memory_space_constraint(array, pltpu.HBM)

    packed, previous, low, high = pl.pallas_call(
        pack_kernel,
        out_shape=(
            near(tiles, tile_y, LANES), near(tile_y, LANES), near(tiles, HALO, LANES), near(tiles, HALO, LANES)
        ),
        scratch_shapes=[pltpu.VMEM((tiles * LANES, tile_y), f32)],
        compiler_params=params(),
        name="pack",
    )(
        *map(
            far,
            (
                lanczos_block, previous_block, prior_reaction, vert_coupling, horiz_coupling,
                friction, base_velocity, layers,
            ),
        )
    )
    table = pl.pallas_call(
        table_kernel, out_shape=near(devices, LANES), compiler_params=params(), name="table"
    )(obs_dest.reshape(1, obs_rows), obs_cell.reshape(1, obs_rows), obs_weight.T)

    from_low = lax.ppermute(high, "my", forward_y)
    from_high = lax.ppermute(low, "my", backward_y)
    own = jnp.concatenate([from_low * low_flag, packed, from_high * high_flag], axis=1)
    left = lax.ppermute(own, "mx", forward_x)
    right = lax.ppermute(own, "mx", backward_x)

    count = rows // 8
    groups = -(-FIELDS // 4)

    def blocked(*dims):
        return pltpu.VMEM((*dims, 8, LANES), f32)

    message, basis, fields = pl.pallas_call(
        functools.partial(moment_kernel, vectors),
        out_shape=(
            near(devices, LANES), near(3, count, 3, 8, LANES), near(groups, count, 8, LANES)
        ),
        in_specs=[smem, vmem, vmem, vmem, vmem],
        scratch_shapes=[pltpu.VMEM((3 + groups, rows, LANES), f32), blocked(3, count), blocked(count, 3)]
        + [blocked(count + 2, 5)] * 3,
        compiler_params=params(),
        name="moments",
    )(flags, keep(own), keep(left), keep(right), table)
    message = lax.all_to_all(message, AXES, split_axis=0, concat_axis=0, tiled=True)

    def columns(width):
        return [
            pltpu.VMEM((groups, count, 8, 4 * width * LANES), f32),
            blocked(2, layer_count, count + 2, width + 2),
            blocked(2, layer_count, count + 2, width + 2),
            blocked(2, count, width),
        ]

    misfit, low, high = pl.pallas_call(
        functools.partial(velocity_kernel, vectors),
        out_shape=(near(2, tile_y, LANES), near(2, HALO, LANES), near(2, HALO, LANES)),
        in_specs=[smem] + [vmem] * 3,
        scratch_shapes=columns(2) + [blocked(2, count), pltpu.VMEM((rows, LANES), f32)],
        compiler_params=params(),
        name="velocity",
    )(flags, message, basis, fields)

    after, low, high = lax.optimization_barrier((flags, low, high))
    from_low = lax.ppermute(high, "my", forward_y)
    from_high = lax.ppermute(low, "my", backward_y)
    wide, done = pl.pallas_call(
        functools.partial(spread_kernel, vectors),
        out_shape=(near(groups, count, 8, 12 * LANES), near(8, LANES)),
        in_specs=[smem, vmem],
        compiler_params=params(16),
        name="spread",
    )(after, fields)
    misfit = jnp.concatenate(
        [from_low * (done * low_flag), misfit, from_high * (done * high_flag)], axis=1
    )
    after, misfit = lax.optimization_barrier((flags, misfit))
    misfit_left = lax.ppermute(misfit, "mx", forward_x)
    misfit_right = lax.ppermute(misfit, "mx", backward_x)

    bed_col, top_col = pl.pallas_call(
        column_kernel,
        out_shape=(near(layer_count, count, 3, 8, LANES), near(layer_count, count, 3, 8, LANES)),
        in_specs=[smem, vmem],
        compiler_params=params(16),
        name="columns",
    )(after, wide)

    products, stacked = pl.pallas_call(
        functools.partial(adjoint_kernel, vectors),
        out_shape=(near(size_x, vectors, 2 * LANES), near(tile_x, 5 * vectors, tile_y)),
        in_specs=[smem] + [vmem] * 8,
        scratch_shapes=columns(3)[1:]
        + [pltpu.VMEM((2, 3, rows, LANES), f32), blocked(2, 3, count), blocked(2, count, 3), blocked(count, 3)]
        + [blocked(count + 2, 5)] * 3
        + [blocked(count), pltpu.VMEM((rows, LANES), f32)],
        compiler_params=params(),
        name="adjoint",
    )(flags, wide, bed_col, top_col, keep(misfit), keep(misfit_left), keep(misfit_right), basis, previous)

    products = lax.all_to_all(products, "mx", split_axis=0, concat_axis=0, tiled=True)
    products = jnp.broadcast_to(jnp.sum(products, axis=0)[None], (size_y, vectors, 2 * LANES))
    products = lax.all_to_all(products, "my", split_axis=0, concat_axis=0, tiled=True)
    return pl.pallas_call(
        functools.partial(finish_kernel, float(cells)),
        out_shape=(shape(vectors, tile_x, tile_y), shape(vectors, vectors), shape(vectors, vectors)),
        compiler_params=params(),
        name="finish",
    )(products, stacked, previous_beta)


def solution(mesh):
    in_specs = (
        P(None, "mx", "my"),
        P(None, "mx", "my"),
        P(),
        P("mx", "my"),
        P(None, "mx", "my"),
        P(None, "mx", "my"),
        P("mx", "my"),
        P(None, "mx", "my"),
        P("mx", "my"),
        P(("mx", "my"), None),
        P(("mx", "my")),
        P(("mx", "my"), None),
    )
    out_specs = (P(None, "mx", "my"), P(), P())
    return jax.shard_map(shards, mesh=mesh, in_specs=in_specs, out_specs=out_specs, check_vma=False)
```
